32 devices in a mesh: cuts: 1, mode: 32 (over z, y, x, core).
Axes of the slice: x: 2, y: 2, z: 4, core: 2. Of those that a mesh axis runs over, the one named last changes fastest.
Arguments:
- branch_in: bfloat16 [4, 2, 2048, 1024], P(None, None, ('cuts', 'mode')), may hold values from -6 to 6
- column_order: int32 [4, 1024], replicated, may hold values from 0 to 1023, each once within a row
- gate_a: bfloat16 [2, 1024, 1024], P(None, 'mode'), may hold values from -0.125 to 0.125
- gate_b: bfloat16 [2, 1024, 1024], P(None, 'mode'), may hold values from -0.125 to 0.125
Outputs:
- joined: bfloat16 [2, 512, 2, 128], P(None, ('cuts', 'mode'))
The draws below stay inside these ranges and needn't reach their ends.
Inputs may be any that keep to these rules, and one draw needn't show every extreme that they name: Each row of column_order names every column state once.
All inputs are finite; a program needn't handle non-finite values.
Results may differ from the reference program's by a relative error of at most 0.014.
Values may be sent and summed in bfloat16 or wider, within the bound.
No kernel may reach another device: no remote copies, remote signals or barrier semaphores. Data moves between devices by JAX's collectives and lax.ppermute only.
A program may use at most 128 MiB of HBM per device.

```python
import jax
import jax.numpy as jnp

C = 1024
SHARED = 4096
RD = 64
KEPT = 4
CYCLES = 2
ROWS = 2048
GROUP = 32
JOIN = 128
N_MODE = 32


def level_of(rng, dims, cuts, smallest, high):
    factor_of = 1.0
    for position, shards_of in cuts:
        draws = jax.random.uniform(jax.random.fold_in(jax.random.fold_in(rng, 6), position), (shards_of,), jnp.float32, smallest / len(cuts), high / len(cuts))
        factor_of = factor_of * jnp.repeat(jnp.exp(draws), dims[position] // shards_of).reshape((-1,) + (1,) * (len(dims) - 1 - position))
    return factor_of


def normal_values(own_key, shape, scale, most, cuts=(), dtype=jnp.bfloat16):
    result = scale * jax.random.normal(own_key, shape, jnp.float32)
    if cuts:
        result = result * level_of(own_key, shape, cuts, -0.22, 0.18)
    return jnp.clip(result, -most, most).astype(dtype)


def setup_inputs(seed: int = 0, part: int = 0) -> dict:
    key_list = jax.random.split(jax.random.key(seed), 5)
    part_keys = jax.random.split(jax.random.fold_in(key_list[4], part), 5)
    return {
        "branch_in": normal_values(part_keys[0], (4, 2, ROWS, C), 1.0, 6.0, ((2, 32),)),
        "column_order": jax.vmap(lambda own: jax.random.permutation(own, C))(jax.random.split(key_list[1], 4)).reshape((4, C)).astype(jnp.int32),
        "gate_a": normal_values(key_list[2], (2, C, C), (2 * C) ** -0.5, 0.125, ((1, 32),)),
        "gate_b": normal_values(key_list[3], (2, C, C), (2 * C) ** -0.5, 0.125, ((1, 32),)),
    }


def complex_product(pair_tensor, layer_block):
    real_part = jnp.dot(pair_tensor[0], layer_block[0], preferred_element_type=jnp.float32) - jnp.dot(pair_tensor[1], layer_block[1], preferred_element_type=jnp.float32)
    imag_part = jnp.dot(pair_tensor[0], layer_block[1], preferred_element_type=jnp.float32) + jnp.dot(pair_tensor[1], layer_block[0], preferred_element_type=jnp.float32)
    return jnp.stack([real_part, imag_part]).astype(jnp.bfloat16)


def regroup(pair_tensor):
    pieces = pair_tensor.reshape(2, N_MODE, RD, N_MODE, GROUP)
    return jnp.transpose(pieces, (0, 3, 2, 1, 4)).reshape(2, ROWS, C)


def reference(branch_in, column_order, gate_a, gate_b):
    join_scale = (2.0 * SHARED) ** -0.5
    finals = []
    for branch in range(4):
        state = jnp.take(branch_in[branch], column_order[branch].astype(jnp.int32), axis=2)
        for layer_number in range(2 * CYCLES):
            if layer_number > 0:
                state = regroup(state)
            layer_block = gate_a if layer_number % 2 == 0 else gate_b
            state = complex_product(state, layer_block)
        finals.append(state)
    results = []
    for pair_number in range(2):
        left_part = finals[2 * pair_number].reshape(2, KEPT, JOIN, SHARED)
        right_part = finals[2 * pair_number + 1].reshape(2, SHARED, KEPT, JOIN)
        blocks = []
        for batch in range(KEPT):
            left_real = left_part[0, batch]
            left_imag = left_part[1, batch]
            right_real = right_part[0, :, batch, :]
            right_imag = right_part[1, :, batch, :]
            real_part = jnp.dot(left_real, right_real, preferred_element_type=jnp.float32) - jnp.dot(left_imag, right_imag, preferred_element_type=jnp.float32)
            imag_part = jnp.dot(left_real, right_imag, preferred_element_type=jnp.float32) + jnp.dot(left_imag, right_real, preferred_element_type=jnp.float32)
            blocks.append(jnp.stack([real_part, imag_part], axis=1))
        stacked = jnp.concatenate(blocks, axis=0)
        results.append((stacked * join_scale).astype(jnp.bfloat16))
    return jnp.stack(results)
```

```python
import functools

import jax
import jax.numpy as jnp
from jax import lax
from jax.experimental import pallas as pl
from jax.experimental.pallas import tpu as pltpu
from jax.sharding import PartitionSpec as P

SHARED = 4096
KEPT = 4
CYCLES = 2
LANES = 128
VMEM_LIMIT = 56 * 1024 * 1024


def whole(count):
    return [pl.BlockSpec(memory_space=pltpu.VMEM)] * count


def one_hot(shape, axis, wanted):
    return (lax.broadcasted_iota(jnp.int32, shape, axis) == wanted).astype(jnp.bfloat16)


def exact_dot(left, right):
    return jnp.dot(left, right, preferred_element_type=jnp.float32)


def order_kernel(order_ref, x_ref, o_ref):
    width = x_ref.shape[1]
    step = min(256, width)
    for start in range(0, width, step):
        picks = one_hot((width, step), 0, order_ref[:, start : start + step])
        o_ref[:, start : start + step] = exact_dot(x_ref[...], picks).astype(jnp.bfloat16)


def swap_sign(tiles, qs):
    turned = pltpu.roll(tiles, qs, 1)
    row = lax.broadcasted_iota(jnp.int32, tiles.shape, 1)
    return jnp.where(row < qs, -turned, turned)


def regroup_store(acc, first_lane, group, devices, tile_rows, x_ref, h_ref):
    per = LANES // group
    lane = lax.broadcasted_iota(jnp.int32, (tile_rows, LANES), 1) // group
    for offset in range(0, acc.shape[1], LANES):
        tile = acc[:, offset : offset + LANES].reshape(devices, tile_rows, LANES)
        row_start = (first_lane + offset) // group * tile_rows
        for block in range(devices // per):
            parts = [tile[block * per + m] for m in range(per)]
            bit = 1
            while bit < per:
                moved = list(parts)
                keep = (lane // bit) % 2 == 0
                for m in range(per):
                    if m & bit:
                        continue
                    low, high = parts[m], parts[m | bit]
                    moved[m] = jnp.where(keep, low, pltpu.roll(high, bit * group, 1))
                    moved[m | bit] = jnp.where(keep, pltpu.roll(low, LANES - bit * group, 1), high)
                parts = moved
                bit *= 2
            tiles = jnp.stack(parts)
            rows = pl.ds(row_start, per * tile_rows)
            lanes = pl.ds(block * LANES, LANES)
            x_ref[rows, lanes] = tiles.reshape(per * tile_rows, LANES).astype(jnp.bfloat16)
            turned = swap_sign(tiles, tile_rows // 2)
            h_ref[rows, lanes] = turned.reshape(per * tile_rows, LANES).astype(jnp.bfloat16)


def layers_kernel(sizes, is_left, x_ref, a_ref, b_ref, o_ref, xs, hs, last):
    devices, qs, group, rows_each = sizes
    tile_rows = 2 * qs
    rows, width = x_ref.shape
    first = x_ref[...].astype(jnp.float32).reshape(devices, tile_rows, width)
    hs[0] = swap_sign(first, qs).reshape(rows, width).astype(jnp.bfloat16)
    step = 256
    for layer in range(2 * CYCLES):
        gate = a_ref if layer % 2 == 0 else b_ref
        here = x_ref if layer == 0 else xs.at[layer % 2]
        turned = hs.at[layer % 2]
        later = (layer + 1) % 2
        for start in range(0, width, step):
            cols = slice(start, start + step)
            acc = exact_dot(here[...], gate[0, :, cols]) + exact_dot(turned[...], gate[1, :, cols])
            if layer < 2 * CYCLES - 1:
                regroup_store(acc, start, group, devices, tile_rows, xs.at[later], hs.at[later])
            else:
                last[:, cols] = acc.astype(jnp.bfloat16)
    half = rows // 2
    new = lax.broadcasted_iota(jnp.int32, (rows, rows), 0)
    part, inner = new // half, new % half
    if is_left:
        v, r = inner // devices, inner % devices
        picks = one_hot((rows, rows), 1, r * tile_rows + part * qs + v)
        moved = exact_dot(picks, last[...]).astype(jnp.bfloat16)
        span = 2 * rows_each
        each = width * qs // rows_each
        words = width // span
        for start in range(0, width, step):
            place = start + lax.broadcasted_iota(jnp.int32, (width, step), 1)
            e, rest = place // each, place % each
            h, w, qr = rest // (words * qs), rest % (words * qs) // qs, rest % qs
            lanes = one_hot((width, step), 0, w * span + (e * qs + qr) * 2 + h)
            sent = exact_dot(moved, lanes)
            low_lane = lax.broadcasted_iota(jnp.int32, (half, LANES), 1) < LANES // 2
            for offset in range(0, step, LANES):
                real = sent[:half, offset : offset + LANES]
                imag = sent[half:, offset : offset + LANES]
                e0 = (start + offset) // each
                even = jnp.where(low_lane, real, pltpu.roll(imag, LANES // 2, 1))
                odd = jnp.where(low_lane, pltpu.roll(real, LANES // 2, 1), imag)
                o_ref[e0 * half : (e0 + 1) * half, :] = even.astype(jnp.bfloat16)
                o_ref[(e0 + 1) * half : (e0 + 2) * half, :] = odd.astype(jnp.bfloat16)
    else:
        r, q = inner // qs, inner % qs
        picks = one_hot((rows, rows), 1, r * tile_rows + part * qs + q)
        o_ref[...] = exact_dot(picks, last[...]).astype(jnp.bfloat16)


def join_kernel(sizes, left_ref, right_ref, o_ref):
    devices, us, vs = sizes
    rows = us * devices
    free = right_ref.shape[1] // (2 * KEPT)
    left = left_ref[...].reshape(us, vs, devices, LANES)
    left = jnp.concatenate([left[:, v].reshape(rows, LANES) for v in range(vs)], axis=1)
    new = lax.broadcasted_iota(jnp.int32, (rows, rows), 0)
    picks = one_hot((rows, rows), 1, new % us * devices + new // us)
    left = exact_dot(picks, left).astype(jnp.bfloat16)
    half = right_ref.shape[0] // 2
    depth = half // vs
    real, imag = right_ref[:half, :], right_ref[half:, :]
    block = rows // KEPT
    for g in range(KEPT):
        stack = []
        for v in range(vs):
            r = [real[v * depth : (v + 1) * depth, (h * KEPT + g) * free :][:, :free] for h in range(2)]
            i = [imag[v * depth : (v + 1) * depth, (h * KEPT + g) * free :][:, :free] for h in range(2)]
            to_real = jnp.concatenate([r[0], r[1], -i[0], -i[1]], axis=0)
            to_imag = jnp.concatenate([i[0], i[1], r[0], r[1]], axis=0)
            stack.append(jnp.concatenate([to_real, to_imag], axis=1))
        stack = jnp.concatenate(stack, axis=0)
        part = exact_dot(left[g * block : (g + 1) * block, :], stack)
        o_ref[g * block : (g + 1) * block, :] = part.astype(jnp.bfloat16)


def call(kernel, out_shape, inputs, scratch=(), flops=0):
    moved = sum(x.size * x.dtype.itemsize for x in inputs)
    return pl.pallas_call(
        kernel,
        out_shape=jax.ShapeDtypeStruct(out_shape, jnp.bfloat16),
        in_specs=whole(len(inputs)),
        out_specs=whole(1)[0],
        scratch_shapes=list(scratch),
        compiler_params=pltpu.CompilerParams(vmem_limit_bytes=VMEM_LIMIT),
        cost_estimate=pl.CostEstimate(flops=flops, bytes_accessed=moved, transcendentals=0),
    )(*inputs)


def tiles_fit(devices, rows_each, width):
    pair_devices = devices // 2
    if devices < 4 or devices & (devices - 1) or rows_each % pair_devices or width % 256:
        return False
    qs, group = rows_each // pair_devices, width // devices
    return (
        2 * qs == 8
        and LANES % group == 0
        and devices % (LANES // group) == 0
        and qs == SHARED // width
        and devices % 32 == 0
        and 2 * width * qs // rows_each == LANES
        and devices * rows_each * width // SHARED % (KEPT * LANES) == 0
        and 2 * (devices * rows_each * width // SHARED) == width
    )


def fast(branch_in, column_order, gate_a, gate_b):
    devices = lax.axis_size("mode")
    me = lax.axis_index("mode")
    rows_each, width = branch_in.shape[2:]
    halves = devices // 2
    qs, group = rows_each // halves, width // devices
    tile_rows = 2 * qs
    rows = devices * tile_rows
    pair = me // halves
    whole_a, whole_b = gather_gates(gate_a, gate_b)
    cut = branch_in.reshape(2, 2, 2, halves, qs, width).transpose(1, 0, 3, 2, 4, 5)
    cut = cut.reshape(2, devices, tile_rows, width)
    states = []
    for side in range(2):
        got = lax.all_to_all(cut[side], "mode", split_axis=0, concat_axis=0, tiled=True)
        order = lax.dynamic_slice_in_dim(column_order, 2 * pair + side, 1, 0)
        states.append(
            call(order_kernel, (rows, width), (order, got.reshape(rows, width)), flops=2 * rows * width * width)
        )
    sizes = (devices, qs, group, rows_each)
    scratch = [pltpu.VMEM((2, rows, width), jnp.bfloat16)] * 2 + [pltpu.VMEM((rows, width), jnp.bfloat16)]
    work = 2 * CYCLES * 4 * rows * width * width
    left = call(
        functools.partial(layers_kernel, sizes, True),
        (halves * rows // 2, LANES),
        (states[0], whole_a, whole_b),
        scratch,
        work,
    )
    groups = [[h * halves + e for e in range(halves)] for h in range(2)]
    left = lax.all_to_all(
        left.reshape(halves, rows // 2, LANES),
        "mode",
        split_axis=0,
        concat_axis=0,
        axis_index_groups=groups,
        tiled=True,
    )
    right = call(
        functools.partial(layers_kernel, sizes, False), (rows, width), (states[1], whole_a, whole_b), scratch, work
    )
    free = width // (2 * KEPT)
    us = halves
    partial_sums = call(
        functools.partial(join_kernel, (devices, us, qs)),
        (devices * us, 2 * free),
        (left.reshape(halves * rows // 2, LANES), right),
        flops=2 * devices * us * LANES * qs * 2 * free,
    )
    parts = lax.all_to_all(
        partial_sums.reshape(devices, us, 2 * free), "mode", split_axis=0, concat_axis=0, tiled=True
    )
    parts = parts.reshape(2, halves, us, 2 * free).astype(jnp.float32)
    join_scale = (2.0 * SHARED) ** (-0.5)
    return (jnp.sum(parts, axis=1) * join_scale).astype(jnp.bfloat16).reshape(2, us, 2, free)


def gather_gates(gate_a, gate_b):
    return [lax.all_gather(gate, "mode", axis=1, tiled=True) for gate in (gate_a, gate_b)]


def partner(value, axis, bit):
    mask = 2**bit
    pairs = [(source, source ^ mask) for source in range(lax.axis_size(axis))]
    return lax.ppermute(value, axis, pairs)


def product_four(states, layer_block):
    branches, parts, row_count, width = states.shape
    real_in = states[:, 0].reshape(branches * row_count, width)
    imag_in = states[:, 1].reshape(branches * row_count, width)
    real_part = jnp.dot(real_in, layer_block[0], preferred_element_type=jnp.float32) - jnp.dot(
        imag_in, layer_block[1], preferred_element_type=jnp.float32
    )
    imag_part = jnp.dot(real_in, layer_block[1], preferred_element_type=jnp.float32) + jnp.dot(
        imag_in, layer_block[0], preferred_element_type=jnp.float32
    )
    joined_parts = jnp.stack(
        [
            real_part.reshape(branches, row_count, width),
            imag_part.reshape(branches, row_count, width),
        ],
        axis=1,
    )
    return joined_parts.astype(jnp.bfloat16)


def complex_rows(left_real, left_imag, right_real, right_imag):
    real_part = jnp.dot(left_real, right_real, preferred_element_type=jnp.float32) - jnp.dot(
        left_imag, right_imag, preferred_element_type=jnp.float32
    )
    imag_part = jnp.dot(left_real, right_imag, preferred_element_type=jnp.float32) + jnp.dot(
        left_imag, right_real, preferred_element_type=jnp.float32
    )
    return jnp.stack([real_part, imag_part], axis=1)


def read_bit(device_index, bit_number):
    return device_index // 2**bit_number % 2


def trade_axes(buffer, axis_bits, trader, device_index):
    for position, bit_number in enumerate(axis_bits):
        own_bit = read_bit(device_index, bit_number)
        kept_half = lax.dynamic_index_in_dim(buffer, own_bit, position, keepdims=False)
        sent_half = lax.dynamic_index_in_dim(buffer, 1 - own_bit, position, keepdims=False)
        received = trader(sent_half, bit_number)
        first_half = jnp.where(own_bit == 0, kept_half, received)
        second_half = jnp.where(own_bit == 0, received, kept_half)
        buffer = jnp.stack([first_half, second_half], axis=position)
    return buffer


def general(branch_in, column_order, gate_a, gate_b):
    join_scale = (2.0 * SHARED) ** (-0.5)
    devices_mode = lax.axis_size("mode")
    whole_a, whole_b = (
        lax.all_gather(gate_a, "mode", axis=1, tiled=True),
        lax.all_gather(gate_b, "mode", axis=1, tiled=True),
    )
    states = jnp.take_along_axis(branch_in, column_order[:, None, None, :], axis=3)
    for layer_number in range(2 * CYCLES):
        if layer_number > 0:
            states = lax.all_to_all(states, "mode", split_axis=3, concat_axis=3, tiled=True)
        states = product_four(states, whole_a if layer_number % 2 == 0 else whole_b)
    local_cells = states.shape[2] * states.shape[3]
    local_rows = local_cells // SHARED
    shared_rows = SHARED // devices_mode
    join_width = local_cells // (shared_rows * KEPT)
    results = []
    for pair_number in range(2):
        left_part = states[2 * pair_number].reshape(2, local_rows, SHARED)
        right_part = states[2 * pair_number + 1].reshape(2, shared_rows, KEPT, join_width)
        device_index = lax.axis_index("mode")
        total_bits = devices_mode.bit_length() - 1
        group_bits = total_bits - 4
        batch_bits = KEPT.bit_length() - 1
        groups = devices_mode // (4 * KEPT)
        span = 2 * shared_rows
        outer = SHARED // (span * groups)
        half_join = join_width // 2

        def left_trader(piece, bit_number):
            return partner(piece, "mode", bit_number)

        def right_trader(piece, bit_number):
            return partner(piece, "mode", bit_number)

        left_buffer = left_part.reshape(2, local_rows, outer, groups, span).transpose(3, 0, 1, 2, 4)
        left_buffer = left_buffer.reshape((2,) * group_bits + (1, 2, local_rows, outer, span))
        left_buffer = jnp.broadcast_to(
            left_buffer, (2,) * group_bits + (2, 2, local_rows, outer, span)
        )
        left_bits = [group_bits - position for position in range(group_bits)] + [0]
        left_buffer = trade_axes(left_buffer, left_bits, left_trader, device_index)
        left_block = left_buffer.reshape(devices_mode // (2 * KEPT), 2, local_rows, outer * span)
        left_block = left_block.transpose(1, 0, 2, 3).reshape(2, half_join, SHARED // groups)
        right_buffer = right_part.reshape(2, shared_rows, KEPT, 2, half_join).transpose(
            2, 3, 0, 1, 4
        )
        right_buffer = right_buffer.reshape((2,) * batch_bits + (1, 2, 2, shared_rows, half_join))
        right_buffer = jnp.broadcast_to(
            right_buffer, (2,) * batch_bits + (2, 2, 2, shared_rows, half_join)
        )
        right_bits = [total_bits - 1 - position for position in range(batch_bits)] + [
            total_bits - batch_bits - 1,
            0,
        ]
        right_buffer = trade_axes(right_buffer, right_bits, right_trader, device_index)
        right_block = right_buffer.reshape(2 * KEPT, 2, 2, shared_rows, half_join)
        right_block = right_block.transpose(2, 0, 1, 3, 4).reshape(2, SHARED // groups, half_join)
        running = complex_rows(left_block[0], left_block[1], right_block[0], right_block[1])
        for position in range(group_bits):
            bit_number = group_bits - position
            own_bit = read_bit(device_index, bit_number)
            row_count = running.shape[0]
            halves = running.reshape(2, row_count // 2, 2, half_join)
            kept_half = lax.dynamic_index_in_dim(halves, own_bit, 0, keepdims=False)
            sent_half = lax.dynamic_index_in_dim(halves, 1 - own_bit, 0, keepdims=False)
            running = kept_half + partner(
                sent_half.astype(jnp.bfloat16), "mode", bit_number
            ).astype(sent_half.dtype)
        rounded = (running * join_scale).astype(jnp.bfloat16)
        own_bit = read_bit(device_index, 0)
        halves = rounded.reshape(2, local_rows, 2, half_join)
        kept_half = lax.dynamic_index_in_dim(halves, own_bit, 0, keepdims=False)
        sent_half = lax.dynamic_index_in_dim(halves, 1 - own_bit, 0, keepdims=False)
        received = partner(sent_half, "mode", 0)
        first_half = jnp.where(own_bit == 0, kept_half, received)
        second_half = jnp.where(own_bit == 0, received, kept_half)
        finished = jnp.concatenate([first_half, second_half], axis=2)
        results.append(finished)
    return jnp.stack(results)


def local(branch_in, column_order, gate_a, gate_b):
    branches, _, rows_each, width = branch_in.shape
    if branches == 4 and tiles_fit(lax.axis_size("mode"), rows_each, width):
        return fast(branch_in, column_order, gate_a, gate_b)
    return general(branch_in, column_order, gate_a, gate_b)


def solution(mesh):
    in_specs = (
        P(None, None, ("cuts", "mode"), None),
        P(),
        P(None, "mode", None),
        P(None, "mode", None),
    )
    out_specs = P(None, ("cuts", "mode"), None, None)
    return jax.shard_map(local, mesh=mesh, in_specs=in_specs, out_specs=out_specs, check_vma=False)
```

```python
import functools

import jax
import jax.numpy as jnp
from jax import lax
from jax.experimental import pallas as pl
from jax.experimental.pallas import tpu as pltpu
from jax.sharding import PartitionSpec as P

SHARED = 4096
KEPT = 4
CYCLES = 2
LANES = 128
VMEM_LIMIT = 56 * 1024 * 1024


def whole(count):
    return [pl.BlockSpec(memory_space=pltpu.VMEM)] * count


def one_hot(shape, axis, wanted):
    return (lax.broadcasted_iota(jnp.int32, shape, axis) == wanted).astype(jnp.bfloat16)


def exact_dot(left, right):
    return jnp.dot(left, right, preferred_element_type=jnp.float32)


def order_kernel(order_ref, x_ref, o_ref):
    width = x_ref.shape[1]
    step = min(256, width)
    for start in range(0, width, step):
        picks = one_hot((width, step), 0, order_ref[:, start : start + step])
        o_ref[:, start : start + step] = exact_dot(x_ref[...], picks).astype(jnp.bfloat16)


def swap_sign(tiles, qs):
    turned = pltpu.roll(tiles, qs, 1)
    row = lax.broadcasted_iota(jnp.int32, tiles.shape, 1)
    return jnp.where(row < qs, -turned, turned)


def regroup_store(acc, first_lane, group, devices, tile_rows, x_ref, h_ref):
    per = LANES // group
    lane = lax.broadcasted_iota(jnp.int32, (tile_rows, LANES), 1) // group
    for offset in range(0, acc.shape[1], LANES):
        tile = acc[:, offset : offset + LANES].reshape(devices, tile_rows, LANES)
        row_start = (first_lane + offset) // group * tile_rows
        for block in range(devices // per):
            parts = [tile[block * per + m] for m in range(per)]
            bit = 1
            while bit < per:
                moved = list(parts)
                keep = (lane // bit) % 2 == 0
                for m in range(per):
                    if m & bit:
                        continue
                    low, high = parts[m], parts[m | bit]
                    moved[m] = jnp.where(keep, low, pltpu.roll(high, bit * group, 1))
                    moved[m | bit] = jnp.where(keep, pltpu.roll(low, LANES - bit * group, 1), high)
                parts = moved
                bit *= 2
            tiles = jnp.stack(parts)
            rows = pl.ds(row_start, per * tile_rows)
            lanes = pl.ds(block * LANES, LANES)
            x_ref[rows, lanes] = tiles.reshape(per * tile_rows, LANES).astype(jnp.bfloat16)
            turned = swap_sign(tiles, tile_rows // 2)
            h_ref[rows, lanes] = turned.reshape(per * tile_rows, LANES).astype(jnp.bfloat16)


def gate_copies(plan, blocks, whole_ref, sems):
    me = lax.axis_index("mode")
    copies = ([], [])
    for (sources, gates), block in zip(plan, blocks):
        for place, source in enumerate(sources):
            device = me
            for bit in source:
                device = device + (1 - 2 * (me // 2**bit % 2)) * 2**bit
            size = block.shape[3]
            rows = pl.ds(pl.multiple_of(device * size, size), size)
            for position, gate in enumerate(gates):
                sem = sems.at[gate, len(copies[gate])]
                copies[gate].append(
                    pltpu.make_async_copy(block.at[position, place], whole_ref.at[gate, :, rows, :], sem)
                )
    return copies


def layers_kernel(sizes, is_left, plan, x_ref, *refs):
    devices, qs, group, rows_each = sizes
    blocks, (o_ref, xs, hs, last, whole_ref, sems) = refs[: len(plan)], refs[len(plan) :]
    copies = gate_copies(plan, blocks, whole_ref, sems)
    for gate in range(2):
        for copy in copies[gate]:
            copy.start()
    tile_rows = 2 * qs
    rows, width = x_ref.shape
    first = x_ref[...].astype(jnp.float32).reshape(devices, tile_rows, width)
    hs[0] = swap_sign(first, qs).reshape(rows, width).astype(jnp.bfloat16)
    step = 256
    for layer in range(2 * CYCLES):
        if layer < 2:
            for copy in copies[layer]:
                copy.wait()
        gate = whole_ref.at[layer % 2]
        here = x_ref if layer == 0 else xs.at[layer % 2]
        turned = hs.at[layer % 2]
        later = (layer + 1) % 2
        for start in range(0, width, step):
            cols = slice(start, start + step)
            acc = exact_dot(here[...], gate[0, :, cols]) + exact_dot(turned[...], gate[1, :, cols])
            if layer < 2 * CYCLES - 1:
                regroup_store(acc, start, group, devices, tile_rows, xs.at[later], hs.at[later])
            else:
                last[:, cols] = acc.astype(jnp.bfloat16)
    half = rows // 2
    new = lax.broadcasted_iota(jnp.int32, (rows, rows), 0)
    part, inner = new // half, new % half
    if is_left:
        v, r = inner // devices, inner % devices
        picks = one_hot((rows, rows), 1, r * tile_rows + part * qs + v)
        moved = exact_dot(picks, last[...]).astype(jnp.bfloat16)
        span = 2 * rows_each
        each = width * qs // rows_each
        words = width // span
        for start in range(0, width, step):
            place = start + lax.broadcasted_iota(jnp.int32, (width, step), 1)
            e, rest = place // each, place % each
            h, w, qr = rest // (words * qs), rest % (words * qs) // qs, rest % qs
            lanes = one_hot((width, step), 0, w * span + (e * qs + qr) * 2 + h)
            sent = exact_dot(moved, lanes)
            low_lane = lax.broadcasted_iota(jnp.int32, (half, LANES), 1) < LANES // 2
            for offset in range(0, step, LANES):
                real = sent[:half, offset : offset + LANES]
                imag = sent[half:, offset : offset + LANES]
                e0 = (start + offset) // each
                even = jnp.where(low_lane, real, pltpu.roll(imag, LANES // 2, 1))
                odd = jnp.where(low_lane, pltpu.roll(real, LANES // 2, 1), imag)
                o_ref[e0 * half : (e0 + 1) * half, :] = even.astype(jnp.bfloat16)
                o_ref[(e0 + 1) * half : (e0 + 2) * half, :] = odd.astype(jnp.bfloat16)
    else:
        r, q = inner // qs, inner % qs
        picks = one_hot((rows, rows), 1, r * tile_rows + part * qs + q)
        o_ref[...] = exact_dot(picks, last[...]).astype(jnp.bfloat16)


def join_kernel(sizes, left_ref, right_ref, o_ref):
    devices, us, vs = sizes
    rows = us * devices
    free = right_ref.shape[1] // (2 * KEPT)
    left = left_ref[...].reshape(us, vs, devices, LANES)
    left = jnp.concatenate([left[:, v].reshape(rows, LANES) for v in range(vs)], axis=1)
    new = lax.broadcasted_iota(jnp.int32, (rows, rows), 0)
    picks = one_hot((rows, rows), 1, new % us * devices + new // us)
    left = exact_dot(picks, left).astype(jnp.bfloat16)
    half = right_ref.shape[0] // 2
    depth = half // vs
    real, imag = right_ref[:half, :], right_ref[half:, :]
    block = rows // KEPT
    for g in range(KEPT):
        stack = []
        for v in range(vs):
            r = [real[v * depth : (v + 1) * depth, (h * KEPT + g) * free :][:, :free] for h in range(2)]
            i = [imag[v * depth : (v + 1) * depth, (h * KEPT + g) * free :][:, :free] for h in range(2)]
            to_real = jnp.concatenate([r[0], r[1], -i[0], -i[1]], axis=0)
            to_imag = jnp.concatenate([i[0], i[1], r[0], r[1]], axis=0)
            stack.append(jnp.concatenate([to_real, to_imag], axis=1))
        stack = jnp.concatenate(stack, axis=0)
        part = exact_dot(left[g * block : (g + 1) * block, :], stack)
        o_ref[g * block : (g + 1) * block, :] = part.astype(jnp.bfloat16)


def call(kernel, out_shape, inputs, scratch=(), flops=0, blocks=()):
    moved = sum(x.size * x.dtype.itemsize for x in (*inputs, *blocks))
    return pl.pallas_call(
        kernel,
        out_shape=jax.ShapeDtypeStruct(out_shape, jnp.bfloat16),
        in_specs=whole(len(inputs)) + [pl.BlockSpec(memory_space=pl.ANY)] * len(blocks),
        out_specs=whole(1)[0],
        scratch_shapes=list(scratch),
        compiler_params=pltpu.CompilerParams(vmem_limit_bytes=VMEM_LIMIT),
        cost_estimate=pl.CostEstimate(flops=flops, bytes_accessed=moved, transcendentals=0),
    )(*inputs, *blocks)


def tiles_fit(devices, rows_each, width):
    pair_devices = devices // 2
    if devices < 4 or devices & (devices - 1) or rows_each % pair_devices or width % 256:
        return False
    qs, group = rows_each // pair_devices, width // devices
    return (
        2 * qs == 8
        and LANES % group == 0
        and devices % (LANES // group) == 0
        and qs == SHARED // width
        and devices % 32 == 0
        and 2 * width * qs // rows_each == LANES
        and devices * rows_each * width // SHARED % (KEPT * LANES) == 0
        and 2 * (devices * rows_each * width // SHARED) == width
    )


def fast(branch_in, column_order, gate_a, gate_b):
    devices = lax.axis_size("mode")
    me = lax.axis_index("mode")
    rows_each, width = branch_in.shape[2:]
    halves = devices // 2
    qs, group = rows_each // halves, width // devices
    tile_rows = 2 * qs
    rows = devices * tile_rows
    pair = me // halves
    blocks, plan = gather_gates(gate_a, gate_b)
    cut = branch_in.reshape(2, 2, 2, halves, qs, width).transpose(1, 0, 3, 2, 4, 5)
    cut = cut.reshape(2, devices, tile_rows, width)
    states = []
    for side in range(2):
        got = lax.all_to_all(cut[side], "mode", split_axis=0, concat_axis=0, tiled=True)
        order = lax.dynamic_slice_in_dim(column_order, 2 * pair + side, 1, 0)
        states.append(
            call(order_kernel, (rows, width), (order, got.reshape(rows, width)), flops=2 * rows * width * width)
        )
    sizes = (devices, qs, group, rows_each)
    scratch = [pltpu.VMEM((2, rows, width), jnp.bfloat16)] * 2 + [
        pltpu.VMEM((rows, width), jnp.bfloat16),
        pltpu.VMEM((2, 2, width, width), jnp.bfloat16),
        pltpu.SemaphoreType.DMA((2, devices)),
    ]
    work = 2 * CYCLES * 4 * rows * width * width
    left = call(
        functools.partial(layers_kernel, sizes, True, plan),
        (halves * rows // 2, LANES),
        (states[0],),
        scratch,
        work,
        blocks,
    )
    groups = [[h * halves + e for e in range(halves)] for h in range(2)]
    left = lax.all_to_all(
        left.reshape(halves, rows // 2, LANES),
        "mode",
        split_axis=0,
        concat_axis=0,
        axis_index_groups=groups,
        tiled=True,
    )
    right = call(
        functools.partial(layers_kernel, sizes, False, plan), (rows, width), (states[1],), scratch, work, blocks
    )
    free = width // (2 * KEPT)
    us = halves
    partial_sums = call(
        functools.partial(join_kernel, (devices, us, qs)),
        (devices * us, 2 * free),
        (left.reshape(halves * rows // 2, LANES), right),
        flops=2 * devices * us * LANES * qs * 2 * free,
    )
    parts = lax.all_to_all(
        partial_sums.reshape(devices, us, 2 * free), "mode", split_axis=0, concat_axis=0, tiled=True
    )
    parts = parts.reshape(2, halves, us, 2 * free).astype(jnp.float32)
    join_scale = (2.0 * SHARED) ** (-0.5)
    return (jnp.sum(parts, axis=1) * join_scale).astype(jnp.bfloat16).reshape(2, us, 2, free)


def flip(value, bit):
    pairs = [(source, source ^ 2**bit) for source in range(lax.axis_size("mode"))]
    return lax.ppermute(value, "mode", pairs)


def gather_gates(gate_a, gate_b):
    bits = lax.axis_size("mode").bit_length() - 1
    own = jnp.stack([gate_a, gate_b])[:, None]
    sets = [(jnp.concatenate([own, flip(own, 3)], axis=1), ((), (3,)))]
    for bit in range(4, bits):
        sets += [(flip(value, bit), tuple(source + (bit,) for source in sources)) for value, sources in sets]
    blocks = []
    for value, sources in sets:
        over_x, over_y = flip(value, 1), flip(value, 2)
        diagonal = flip(over_x[:1], 2), flip(over_y[1:], 1)
        turned = [tuple(source + more for source in sources) for more in ((1,), (2,), (1, 2))]
        blocks += [
            (value, sources, (0, 1)),
            (over_x, turned[0], (0, 1)),
            (over_y, turned[1], (0, 1)),
            (diagonal[0], turned[2], (0,)),
            (diagonal[1], turned[2], (1,)),
        ]
    blocks += [
        (flip(value, 0), tuple(source + (0,) for source in sources), gates) for value, sources, gates in blocks
    ]
    return [value for value, _, _ in blocks], tuple((sources, gates) for _, sources, gates in blocks)


def partner(value, axis, bit):
    mask = 2**bit
    pairs = [(source, source ^ mask) for source in range(lax.axis_size(axis))]
    return lax.ppermute(value, axis, pairs)


def product_four(states, layer_block):
    branches, parts, row_count, width = states.shape
    real_in = states[:, 0].reshape(branches * row_count, width)
    imag_in = states[:, 1].reshape(branches * row_count, width)
    real_part = jnp.dot(real_in, layer_block[0], preferred_element_type=jnp.float32) - jnp.dot(
        imag_in, layer_block[1], preferred_element_type=jnp.float32
    )
    imag_part = jnp.dot(real_in, layer_block[1], preferred_element_type=jnp.float32) + jnp.dot(
        imag_in, layer_block[0], preferred_element_type=jnp.float32
    )
    joined_parts = jnp.stack(
        [
            real_part.reshape(branches, row_count, width),
            imag_part.reshape(branches, row_count, width),
        ],
        axis=1,
    )
    return joined_parts.astype(jnp.bfloat16)


def complex_rows(left_real, left_imag, right_real, right_imag):
    real_part = jnp.dot(left_real, right_real, preferred_element_type=jnp.float32) - jnp.dot(
        left_imag, right_imag, preferred_element_type=jnp.float32
    )
    imag_part = jnp.dot(left_real, right_imag, preferred_element_type=jnp.float32) + jnp.dot(
        left_imag, right_real, preferred_element_type=jnp.float32
    )
    return jnp.stack([real_part, imag_part], axis=1)


def read_bit(device_index, bit_number):
    return device_index // 2**bit_number % 2


def trade_axes(buffer, axis_bits, trader, device_index):
    for position, bit_number in enumerate(axis_bits):
        own_bit = read_bit(device_index, bit_number)
        kept_half = lax.dynamic_index_in_dim(buffer, own_bit, position, keepdims=False)
        sent_half = lax.dynamic_index_in_dim(buffer, 1 - own_bit, position, keepdims=False)
        received = trader(sent_half, bit_number)
        first_half = jnp.where(own_bit == 0, kept_half, received)
        second_half = jnp.where(own_bit == 0, received, kept_half)
        buffer = jnp.stack([first_half, second_half], axis=position)
    return buffer


def general(branch_in, column_order, gate_a, gate_b):
    join_scale = (2.0 * SHARED) ** (-0.5)
    devices_mode = lax.axis_size("mode")
    whole_a, whole_b = (
        lax.all_gather(gate_a, "mode", axis=1, tiled=True),
        lax.all_gather(gate_b, "mode", axis=1, tiled=True),
    )
    states = jnp.take_along_axis(branch_in, column_order[:, None, None, :], axis=3)
    for layer_number in range(2 * CYCLES):
        if layer_number > 0:
            states = lax.all_to_all(states, "mode", split_axis=3, concat_axis=3, tiled=True)
        states = product_four(states, whole_a if layer_number % 2 == 0 else whole_b)
    local_cells = states.shape[2] * states.shape[3]
    local_rows = local_cells // SHARED
    shared_rows = SHARED // devices_mode
    join_width = local_cells // (shared_rows * KEPT)
    results = []
    for pair_number in range(2):
        left_part = states[2 * pair_number].reshape(2, local_rows, SHARED)
        right_part = states[2 * pair_number + 1].reshape(2, shared_rows, KEPT, join_width)
        device_index = lax.axis_index("mode")
        total_bits = devices_mode.bit_length() - 1
        group_bits = total_bits - 4
        batch_bits = KEPT.bit_length() - 1
        groups = devices_mode // (4 * KEPT)
        span = 2 * shared_rows
        outer = SHARED // (span * groups)
        half_join = join_width // 2

        def left_trader(piece, bit_number):
            return partner(piece, "mode", bit_number)

        def right_trader(piece, bit_number):
            return partner(piece, "mode", bit_number)

        left_buffer = left_part.reshape(2, local_rows, outer, groups, span).transpose(3, 0, 1, 2, 4)
        left_buffer = left_buffer.reshape((2,) * group_bits + (1, 2, local_rows, outer, span))
        left_buffer = jnp.broadcast_to(
            left_buffer, (2,) * group_bits + (2, 2, local_rows, outer, span)
        )
        left_bits = [group_bits - position for position in range(group_bits)] + [0]
        left_buffer = trade_axes(left_buffer, left_bits, left_trader, device_index)
        left_block = left_buffer.reshape(devices_mode // (2 * KEPT), 2, local_rows, outer * span)
        left_block = left_block.transpose(1, 0, 2, 3).reshape(2, half_join, SHARED // groups)
        right_buffer = right_part.reshape(2, shared_rows, KEPT, 2, half_join).transpose(
            2, 3, 0, 1, 4
        )
        right_buffer = right_buffer.reshape((2,) * batch_bits + (1, 2, 2, shared_rows, half_join))
        right_buffer = jnp.broadcast_to(
            right_buffer, (2,) * batch_bits + (2, 2, 2, shared_rows, half_join)
        )
        right_bits = [total_bits - 1 - position for position in range(batch_bits)] + [
            total_bits - batch_bits - 1,
            0,
        ]
        right_buffer = trade_axes(right_buffer, right_bits, right_trader, device_index)
        right_block = right_buffer.reshape(2 * KEPT, 2, 2, shared_rows, half_join)
        right_block = right_block.transpose(2, 0, 1, 3, 4).reshape(2, SHARED // groups, half_join)
        running = complex_rows(left_block[0], left_block[1], right_block[0], right_block[1])
        for position in range(group_bits):
            bit_number = group_bits - position
            own_bit = read_bit(device_index, bit_number)
            row_count = running.shape[0]
            halves = running.reshape(2, row_count // 2, 2, half_join)
            kept_half = lax.dynamic_index_in_dim(halves, own_bit, 0, keepdims=False)
            sent_half = lax.dynamic_index_in_dim(halves, 1 - own_bit, 0, keepdims=False)
            running = kept_half + partner(
                sent_half.astype(jnp.bfloat16), "mode", bit_number
            ).astype(sent_half.dtype)
        rounded = (running * join_scale).astype(jnp.bfloat16)
        own_bit = read_bit(device_index, 0)
        halves = rounded.reshape(2, local_rows, 2, half_join)
        kept_half = lax.dynamic_index_in_dim(halves, own_bit, 0, keepdims=False)
        sent_half = lax.dynamic_index_in_dim(halves, 1 - own_bit, 0, keepdims=False)
        received = partner(sent_half, "mode", 0)
        first_half = jnp.where(own_bit == 0, kept_half, received)
        second_half = jnp.where(own_bit == 0, received, kept_half)
        finished = jnp.concatenate([first_half, second_half], axis=2)
        results.append(finished)
    return jnp.stack(results)


def local(branch_in, column_order, gate_a, gate_b):
    branches, _, rows_each, width = branch_in.shape
    if branches == 4 and tiles_fit(lax.axis_size("mode"), rows_each, width):
        return fast(branch_in, column_order, gate_a, gate_b)
    return general(branch_in, column_order, gate_a, gate_b)


def solution(mesh):
    in_specs = (
        P(None, None, ("cuts", "mode"), None),
        P(),
        P(None, "mode", None),
        P(None, "mode", None),
    )
    out_specs = P(None, ("cuts", "mode"), None, None)
    return jax.shard_map(local, mesh=mesh, in_specs=in_specs, out_specs=out_specs, check_vma=False)
```

```python
import functools

import jax
import jax.numpy as jnp
from jax import lax
from jax.experimental import pallas as pl
from jax.experimental.pallas import tpu as pltpu
from jax.sharding import PartitionSpec as P

SHARED = 4096
KEPT = 4
CYCLES = 2
LANES = 128
VMEM_LIMIT = 56 * 1024 * 1024


def whole(count):
    return [pl.BlockSpec(memory_space=pltpu.VMEM)] * count


def one_hot(shape, axis, wanted):
    return (lax.broadcasted_iota(jnp.int32, shape, axis) == wanted).astype(jnp.bfloat16)


def exact_dot(left, right):
    return jnp.dot(left, right, preferred_element_type=jnp.float32)


def pack_kernel(side, qs, x_ref, order_ref, o_ref):
    _, parts, rows_each, width = x_ref.shape
    rows = parts * rows_each
    step = min(256, width)
    new = lax.broadcasted_iota(jnp.int32, (rows, rows), 0)
    e, k, q = new // (parts * qs), new // qs % parts, new % qs
    pack = one_hot((rows, rows), 1, k * rows_each + e * qs + q)
    for pair in range(x_ref.shape[0] // 2):
        branch = 2 * pair + side
        packed = exact_dot(pack, x_ref[branch].reshape(rows, width)).astype(jnp.bfloat16)
        for start in range(0, width, step):
            picks = one_hot((width, step), 0, order_ref[branch : branch + 1, start : start + step])
            o_ref[pair * rows : (pair + 1) * rows, start : start + step] = exact_dot(packed, picks).astype(jnp.bfloat16)


def swap_sign(tiles, qs):
    turned = pltpu.roll(tiles, qs, 1)
    row = lax.broadcasted_iota(jnp.int32, tiles.shape, 1)
    return jnp.where(row < qs, -turned, turned)


def regroup_store(acc, first_lane, group, devices, tile_rows, x_ref, h_ref):
    per = LANES // group
    lane = lax.broadcasted_iota(jnp.int32, (tile_rows, LANES), 1) // group
    for offset in range(0, acc.shape[1], LANES):
        tile = acc[:, offset : offset + LANES].reshape(devices, tile_rows, LANES)
        row_start = (first_lane + offset) // group * tile_rows
        for block in range(devices // per):
            parts = [tile[block * per + m] for m in range(per)]
            bit = 1
            while bit < per:
                moved = list(parts)
                keep = (lane // bit) % 2 == 0
                for m in range(per):
                    if m & bit:
                        continue
                    low, high = parts[m], parts[m | bit]
                    moved[m] = jnp.where(keep, low, pltpu.roll(high, bit * group, 1))
                    moved[m | bit] = jnp.where(keep, pltpu.roll(low, LANES - bit * group, 1), high)
                parts = moved
                bit *= 2
            tiles = jnp.stack(parts)
            rows = pl.ds(row_start, per * tile_rows)
            lanes = pl.ds(block * LANES, LANES)
            x_ref[rows, lanes] = tiles.reshape(per * tile_rows, LANES).astype(jnp.bfloat16)
            turned = swap_sign(tiles, tile_rows // 2)
            h_ref[rows, lanes] = turned.reshape(per * tile_rows, LANES).astype(jnp.bfloat16)


def gate_copies(plan, blocks, whole_ref, sems):
    me = lax.axis_index("mode")
    copies = ([], [])
    for (sources, gates), block in zip(plan, blocks):
        for place, source in enumerate(sources):
            device = me
            for bit in source:
                device = device + (1 - 2 * (me // 2**bit % 2)) * 2**bit
            size = block.shape[3]
            rows = pl.ds(pl.multiple_of(device * size, size), size)
            for position, gate in enumerate(gates):
                sem = sems.at[gate, len(copies[gate])]
                copies[gate].append(
                    pltpu.make_async_copy(block.at[position, place], whole_ref.at[gate, :, rows, :], sem)
                )
    return copies


def layers_kernel(sizes, is_left, plan, x_ref, *refs):
    devices, qs, group, rows_each = sizes
    blocks, (o_ref, xs, hs, last, whole_ref, sems) = refs[: len(plan)], refs[len(plan) :]
    copies = gate_copies(plan, blocks, whole_ref, sems)
    for gate in range(2):
        for copy in copies[gate]:
            copy.start()
    tile_rows = 2 * qs
    rows, width = x_ref.shape
    first = x_ref[...].astype(jnp.float32).reshape(devices, tile_rows, width)
    hs[0] = swap_sign(first, qs).reshape(rows, width).astype(jnp.bfloat16)
    step = min(512, width)
    for layer in range(2 * CYCLES):
        if layer < 2:
            for copy in copies[layer]:
                copy.wait()
        gate = whole_ref.at[layer % 2]
        here = x_ref if layer == 0 else xs.at[layer % 2]
        turned = hs.at[layer % 2]
        later = (layer + 1) % 2
        for start in range(0, width, step):
            cols = slice(start, start + step)
            acc = exact_dot(here[...], gate[0, :, cols]) + exact_dot(turned[...], gate[1, :, cols])
            if layer < 2 * CYCLES - 1:
                regroup_store(acc, start, group, devices, tile_rows, xs.at[later], hs.at[later])
            else:
                last[:, cols] = acc.astype(jnp.bfloat16)
    half = rows // 2
    new = lax.broadcasted_iota(jnp.int32, (rows, rows), 0)
    part, inner = new // half, new % half
    if is_left:
        v, r = inner // devices, inner % devices
        picks = one_hot((rows, rows), 1, r * tile_rows + part * qs + v)
        moved = exact_dot(picks, last[...]).astype(jnp.bfloat16)
        span = 2 * rows_each
        each = width * qs // rows_each
        words = width // span
        step = min(256, width)
        for start in range(0, width, step):
            place = start + lax.broadcasted_iota(jnp.int32, (width, step), 1)
            e, rest = place // each, place % each
            h, w, qr = rest // (words * qs), rest % (words * qs) // qs, rest % qs
            lanes = one_hot((width, step), 0, w * span + (e * qs + qr) * 2 + h)
            sent = exact_dot(moved, lanes)
            low_lane = lax.broadcasted_iota(jnp.int32, (half, LANES), 1) < LANES // 2
            for offset in range(0, step, LANES):
                real = sent[:half, offset : offset + LANES]
                imag = sent[half:, offset : offset + LANES]
                e0 = (start + offset) // each
                even = jnp.where(low_lane, real, pltpu.roll(imag, LANES // 2, 1))
                odd = jnp.where(low_lane, pltpu.roll(real, LANES // 2, 1), imag)
                o_ref[e0 * half : (e0 + 1) * half, :] = even.astype(jnp.bfloat16)
                o_ref[(e0 + 1) * half : (e0 + 2) * half, :] = odd.astype(jnp.bfloat16)
    else:
        r, q = inner // qs, inner % qs
        picks = one_hot((rows, rows), 1, r * tile_rows + part * qs + q)
        o_ref[...] = exact_dot(picks, last[...]).astype(jnp.bfloat16)


def join_kernel(sizes, left_ref, right_ref, o_ref):
    devices, us, vs = sizes
    rows = us * devices
    free = right_ref.shape[1] // (2 * KEPT)
    left = left_ref[...].reshape(us, vs, devices, LANES)
    left = jnp.concatenate([left[:, v].reshape(rows, LANES) for v in range(vs)], axis=1)
    new = lax.broadcasted_iota(jnp.int32, (rows, rows), 0)
    picks = one_hot((rows, rows), 1, new % us * devices + new // us)
    left = exact_dot(picks, left).astype(jnp.bfloat16)
    half = right_ref.shape[0] // 2
    depth = half // vs
    real, imag = right_ref[:half, :], right_ref[half:, :]
    block = rows // KEPT
    for g in range(KEPT):
        stack = []
        for v in range(vs):
            r = [real[v * depth : (v + 1) * depth, (h * KEPT + g) * free :][:, :free] for h in range(2)]
            i = [imag[v * depth : (v + 1) * depth, (h * KEPT + g) * free :][:, :free] for h in range(2)]
            to_real = jnp.concatenate([r[0], r[1], -i[0], -i[1]], axis=0)
            to_imag = jnp.concatenate([i[0], i[1], r[0], r[1]], axis=0)
            stack.append(jnp.concatenate([to_real, to_imag], axis=1))
        stack = jnp.concatenate(stack, axis=0)
        part = exact_dot(left[g * block : (g + 1) * block, :], stack)
        o_ref[g * block : (g + 1) * block, :] = part.astype(jnp.bfloat16)


def call(kernel, out_shape, inputs, scratch=(), flops=0, blocks=()):
    moved = sum(x.size * x.dtype.itemsize for x in (*inputs, *blocks))
    return pl.pallas_call(
        kernel,
        out_shape=jax.ShapeDtypeStruct(out_shape, jnp.bfloat16),
        in_specs=whole(len(inputs)) + [pl.BlockSpec(memory_space=pl.ANY)] * len(blocks),
        out_specs=whole(1)[0],
        scratch_shapes=list(scratch),
        compiler_params=pltpu.CompilerParams(vmem_limit_bytes=VMEM_LIMIT),
        cost_estimate=pl.CostEstimate(flops=flops, bytes_accessed=moved, transcendentals=0),
    )(*inputs, *blocks)


def tiles_fit(devices, rows_each, width):
    pair_devices = devices // 2
    if devices < 4 or devices & (devices - 1) or rows_each % pair_devices or width % 256:
        return False
    qs, group = rows_each // pair_devices, width // devices
    return (
        2 * qs == 8
        and LANES % group == 0
        and devices % (LANES // group) == 0
        and qs == SHARED // width
        and devices % 32 == 0
        and 2 * width * qs // rows_each == LANES
        and devices * rows_each * width // SHARED % (KEPT * LANES) == 0
        and 2 * (devices * rows_each * width // SHARED) == width
    )


def fast(branch_in, column_order, gate_a, gate_b):
    devices = lax.axis_size("mode")
    rows_each, width = branch_in.shape[2:]
    halves = devices // 2
    qs, group = rows_each // halves, width // devices
    tile_rows = 2 * qs
    rows = devices * tile_rows
    cut = [
        call(
            functools.partial(pack_kernel, side, qs),
            (rows, width),
            (branch_in, column_order),
            flops=2 * rows * width * width,
        ).reshape(devices, tile_rows, width)
        for side in range(2)
    ]
    blocks, plan, *states = spread(gate_a, gate_b, cut)
    states = [state.reshape(rows, width) for state in states]
    sizes = (devices, qs, group, rows_each)
    scratch = [pltpu.VMEM((2, rows, width), jnp.bfloat16)] * 2 + [
        pltpu.VMEM((rows, width), jnp.bfloat16),
        pltpu.VMEM((2, 2, width, width), jnp.bfloat16),
        pltpu.SemaphoreType.DMA((2, devices)),
    ]
    work = 2 * CYCLES * 4 * rows * width * width
    left = call(
        functools.partial(layers_kernel, sizes, True, plan),
        (halves * rows // 2, LANES),
        (states[0],),
        scratch,
        work,
        blocks,
    )
    groups = [[h * halves + e for e in range(halves)] for h in range(2)]
    left = trade(left.reshape(halves, rows // 2, LANES), groups)
    right = call(
        functools.partial(layers_kernel, sizes, False, plan), (rows, width), (states[1],), scratch, work, blocks
    )
    free = width // (2 * KEPT)
    us = halves
    partial_sums = call(
        functools.partial(join_kernel, (devices, us, qs)),
        (devices * us, 2 * free),
        (left.reshape(halves * rows // 2, LANES), right),
        flops=2 * devices * us * LANES * qs * 2 * free,
    )
    parts = trade(partial_sums.reshape(devices, us, 2 * free))
    parts = parts.reshape(2, halves, us, 2 * free).astype(jnp.float32)
    join_scale = (2.0 * SHARED) ** (-0.5)
    return (jnp.sum(parts, axis=1) * join_scale).astype(jnp.bfloat16).reshape(2, us, 2, free)


def flip(value, bit):
    pairs = [(source, source ^ 2**bit) for source in range(lax.axis_size("mode"))]
    return lax.ppermute(value, "mode", pairs)


def plane(value, sources):
    over_x, over_y = flip(value, 1), flip(value, 2)
    diagonal = flip(over_x[:1], 2), flip(over_y[1:], 1)
    turned = [tuple(source + more for source in sources) for more in ((1,), (2,), (1, 2))]
    return [
        (value, sources, (0, 1)),
        (over_x, turned[0], (0, 1)),
        (over_y, turned[1], (0, 1)),
        (diagonal[0], turned[2], (0,)),
        (diagonal[1], turned[2], (1,)),
    ]


def spread(gate_a, gate_b, cut):
    bits = lax.axis_size("mode").bit_length() - 1
    own = jnp.stack([gate_a, gate_b])[:, None]
    sets = [(jnp.concatenate([own, flip(own, 3)], axis=1), ((), (3,)))]
    for bit in range(4, bits):
        sets += [(flip(value, bit), tuple(source + (bit,) for source in sources)) for value, sources in sets]
    blocks, left = [], cut[0]
    for number, (value, sources) in enumerate(sets):
        if number:
            value, left, *_ = lax.optimization_barrier((value, left, blocks[-2][0], blocks[-1][0]))
        blocks += plane(value, sources)
    left = trade(left)
    right, *_ = lax.optimization_barrier((cut[1], blocks[-3][0], blocks[-4][0]))
    right = trade(right)
    blocks += [
        (flip(value, 0), tuple(source + (0,) for source in sources), gates) for value, sources, gates in blocks
    ]
    plan = tuple((sources, gates) for _, sources, gates in blocks)
    return [value for value, _, _ in blocks], plan, left, right


def trade(value, groups=None):
    return lax.all_to_all(value, "mode", split_axis=0, concat_axis=0, axis_index_groups=groups, tiled=True)


def partner(value, axis, bit):
    mask = 2**bit
    pairs = [(source, source ^ mask) for source in range(lax.axis_size(axis))]
    return lax.ppermute(value, axis, pairs)


def product_four(states, layer_block):
    branches, parts, row_count, width = states.shape
    real_in = states[:, 0].reshape(branches * row_count, width)
    imag_in = states[:, 1].reshape(branches * row_count, width)
    real_part = jnp.dot(real_in, layer_block[0], preferred_element_type=jnp.float32) - jnp.dot(
        imag_in, layer_block[1], preferred_element_type=jnp.float32
    )
    imag_part = jnp.dot(real_in, layer_block[1], preferred_element_type=jnp.float32) + jnp.dot(
        imag_in, layer_block[0], preferred_element_type=jnp.float32
    )
    joined_parts = jnp.stack(
        [
            real_part.reshape(branches, row_count, width),
            imag_part.reshape(branches, row_count, width),
        ],
        axis=1,
    )
    return joined_parts.astype(jnp.bfloat16)


def complex_rows(left_real, left_imag, right_real, right_imag):
    real_part = jnp.dot(left_real, right_real, preferred_element_type=jnp.float32) - jnp.dot(
        left_imag, right_imag, preferred_element_type=jnp.float32
    )
    imag_part = jnp.dot(left_real, right_imag, preferred_element_type=jnp.float32) + jnp.dot(
        left_imag, right_real, preferred_element_type=jnp.float32
    )
    return jnp.stack([real_part, imag_part], axis=1)


def read_bit(device_index, bit_number):
    return device_index // 2**bit_number % 2


def trade_axes(buffer, axis_bits, trader, device_index):
    for position, bit_number in enumerate(axis_bits):
        own_bit = read_bit(device_index, bit_number)
        kept_half = lax.dynamic_index_in_dim(buffer, own_bit, position, keepdims=False)
        sent_half = lax.dynamic_index_in_dim(buffer, 1 - own_bit, position, keepdims=False)
        received = trader(sent_half, bit_number)
        first_half = jnp.where(own_bit == 0, kept_half, received)
        second_half = jnp.where(own_bit == 0, received, kept_half)
        buffer = jnp.stack([first_half, second_half], axis=position)
    return buffer


def general(branch_in, column_order, gate_a, gate_b):
    join_scale = (2.0 * SHARED) ** (-0.5)
    devices_mode = lax.axis_size("mode")
    whole_a, whole_b = (
        lax.all_gather(gate_a, "mode", axis=1, tiled=True),
        lax.all_gather(gate_b, "mode", axis=1, tiled=True),
    )
    states = jnp.take_along_axis(branch_in, column_order[:, None, None, :], axis=3)
    for layer_number in range(2 * CYCLES):
        if layer_number > 0:
            states = lax.all_to_all(states, "mode", split_axis=3, concat_axis=3, tiled=True)
        states = product_four(states, whole_a if layer_number % 2 == 0 else whole_b)
    local_cells = states.shape[2] * states.shape[3]
    local_rows = local_cells // SHARED
    shared_rows = SHARED // devices_mode
    join_width = local_cells // (shared_rows * KEPT)
    results = []
    for pair_number in range(2):
        left_part = states[2 * pair_number].reshape(2, local_rows, SHARED)
        right_part = states[2 * pair_number + 1].reshape(2, shared_rows, KEPT, join_width)
        device_index = lax.axis_index("mode")
        total_bits = devices_mode.bit_length() - 1
        group_bits = total_bits - 4
        batch_bits = KEPT.bit_length() - 1
        groups = devices_mode // (4 * KEPT)
        span = 2 * shared_rows
        outer = SHARED // (span * groups)
        half_join = join_width // 2

        def left_trader(piece, bit_number):
            return partner(piece, "mode", bit_number)

        def right_trader(piece, bit_number):
            return partner(piece, "mode", bit_number)

        left_buffer = left_part.reshape(2, local_rows, outer, groups, span).transpose(3, 0, 1, 2, 4)
        left_buffer = left_buffer.reshape((2,) * group_bits + (1, 2, local_rows, outer, span))
        left_buffer = jnp.broadcast_to(
            left_buffer, (2,) * group_bits + (2, 2, local_rows, outer, span)
        )
        left_bits = [group_bits - position for position in range(group_bits)] + [0]
        left_buffer = trade_axes(left_buffer, left_bits, left_trader, device_index)
        left_block = left_buffer.reshape(devices_mode // (2 * KEPT), 2, local_rows, outer * span)
        left_block = left_block.transpose(1, 0, 2, 3).reshape(2, half_join, SHARED // groups)
        right_buffer = right_part.reshape(2, shared_rows, KEPT, 2, half_join).transpose(
            2, 3, 0, 1, 4
        )
        right_buffer = right_buffer.reshape((2,) * batch_bits + (1, 2, 2, shared_rows, half_join))
        right_buffer = jnp.broadcast_to(
            right_buffer, (2,) * batch_bits + (2, 2, 2, shared_rows, half_join)
        )
        right_bits = [total_bits - 1 - position for position in range(batch_bits)] + [
            total_bits - batch_bits - 1,
            0,
        ]
        right_buffer = trade_axes(right_buffer, right_bits, right_trader, device_index)
        right_block = right_buffer.reshape(2 * KEPT, 2, 2, shared_rows, half_join)
        right_block = right_block.transpose(2, 0, 1, 3, 4).reshape(2, SHARED // groups, half_join)
        running = complex_rows(left_block[0], left_block[1], right_block[0], right_block[1])
        for position in range(group_bits):
            bit_number = group_bits - position
            own_bit = read_bit(device_index, bit_number)
            row_count = running.shape[0]
            halves = running.reshape(2, row_count // 2, 2, half_join)
            kept_half = lax.dynamic_index_in_dim(halves, own_bit, 0, keepdims=False)
            sent_half = lax.dynamic_index_in_dim(halves, 1 - own_bit, 0, keepdims=False)
            running = kept_half + partner(
                sent_half.astype(jnp.bfloat16), "mode", bit_number
            ).astype(sent_half.dtype)
        rounded = (running * join_scale).astype(jnp.bfloat16)
        own_bit = read_bit(device_index, 0)
        halves = rounded.reshape(2, local_rows, 2, half_join)
        kept_half = lax.dynamic_index_in_dim(halves, own_bit, 0, keepdims=False)
        sent_half = lax.dynamic_index_in_dim(halves, 1 - own_bit, 0, keepdims=False)
        received = partner(sent_half, "mode", 0)
        first_half = jnp.where(own_bit == 0, kept_half, received)
        second_half = jnp.where(own_bit == 0, received, kept_half)
        finished = jnp.concatenate([first_half, second_half], axis=2)
        results.append(finished)
    return jnp.stack(results)


def local(branch_in, column_order, gate_a, gate_b):
    branches, _, rows_each, width = branch_in.shape
    if branches == 4 and tiles_fit(lax.axis_size("mode"), rows_each, width):
        return fast(branch_in, column_order, gate_a, gate_b)
    return general(branch_in, column_order, gate_a, gate_b)


def solution(mesh):
    in_specs = (
        P(None, None, ("cuts", "mode"), None),
        P(),
        P(None, "mode", None),
        P(None, "mode", None),
    )
    out_specs = P(None, ("cuts", "mode"), None, None)
    return jax.shard_map(local, mesh=mesh, in_specs=in_specs, out_specs=out_specs, check_vma=False)
```

```python
import functools

import jax
import jax.numpy as jnp
from jax import lax
from jax.experimental import pallas as pl
from jax.experimental.pallas import tpu as pltpu
from jax.sharding import PartitionSpec as P

SHARED = 4096
KEPT = 4
CYCLES = 2
LANES = 128
VMEM_LIMIT = 56 * 1024 * 1024


def whole(count):
    return [pl.BlockSpec(memory_space=pltpu.VMEM)] * count


def one_hot(shape, axis, wanted):
    return (lax.broadcasted_iota(jnp.int32, shape, axis) == wanted).astype(jnp.bfloat16)


def exact_dot(left, right):
    return jnp.dot(left, right, preferred_element_type=jnp.float32)


def pack_kernel(qs, x_ref, order_ref, o_ref, ordered):
    _, parts, rows_each, width = x_ref.shape
    rows = parts * rows_each
    step = min(256, width)
    new = lax.broadcasted_iota(jnp.int32, (2 * rows, 2 * rows), 0)
    e, side = new // (2 * parts * qs), new // (parts * qs) % 2
    k, q = new // qs % parts, new % qs
    pack = one_hot((2 * rows, 2 * rows), 1, side * rows + k * rows_each + e * qs + q)
    for pair in range(x_ref.shape[0] // 2):
        for side in range(2):
            branch = 2 * pair + side
            values = x_ref[branch].reshape(rows, width)
            for start in range(0, width, step):
                picks = one_hot((width, step), 0, order_ref[branch : branch + 1, start : start + step])
                found = exact_dot(values, picks).astype(jnp.bfloat16)
                ordered[side * rows : (side + 1) * rows, start : start + step] = found
        packed = exact_dot(pack, ordered[...]).astype(jnp.bfloat16)
        o_ref[2 * pair * rows : 2 * (pair + 1) * rows, :] = packed


def swap_sign(tiles, qs):
    turned = pltpu.roll(tiles, qs, 1)
    row = lax.broadcasted_iota(jnp.int32, tiles.shape, 1)
    return jnp.where(row < qs, -turned, turned)


def regroup_store(acc, first_lane, group, devices, tile_rows, x_ref, h_ref):
    per = LANES // group
    lane = lax.broadcasted_iota(jnp.int32, (tile_rows, LANES), 1) // group
    for offset in range(0, acc.shape[1], LANES):
        tile = acc[:, offset : offset + LANES].reshape(devices, tile_rows, LANES)
        row_start = (first_lane + offset) // group * tile_rows
        for block in range(devices // per):
            parts = [tile[block * per + m] for m in range(per)]
            bit = 1
            while bit < per:
                moved = list(parts)
                keep = (lane // bit) % 2 == 0
                for m in range(per):
                    if m & bit:
                        continue
                    low, high = parts[m], parts[m | bit]
                    moved[m] = jnp.where(keep, low, pltpu.roll(high, bit * group, 1))
                    moved[m | bit] = jnp.where(keep, pltpu.roll(low, LANES - bit * group, 1), high)
                parts = moved
                bit *= 2
            tiles = jnp.stack(parts)
            rows = pl.ds(row_start, per * tile_rows)
            lanes = pl.ds(block * LANES, LANES)
            x_ref[rows, lanes] = tiles.reshape(per * tile_rows, LANES).astype(jnp.bfloat16)
            turned = swap_sign(tiles, tile_rows // 2)
            h_ref[rows, lanes] = turned.reshape(per * tile_rows, LANES).astype(jnp.bfloat16)


def gate_copies(plan, blocks, whole_ref, sems):
    me = lax.axis_index("mode")
    copies = ([], [])
    for (sources, gates), block in zip(plan, blocks):
        for place, source in enumerate(sources):
            device = me
            for bit in source:
                device = device + (1 - 2 * (me // 2**bit % 2)) * 2**bit
            size = block.shape[3]
            rows = pl.ds(pl.multiple_of(device * size, size), size)
            for position, gate in enumerate(gates):
                sem = sems.at[gate, len(copies[gate])]
                copies[gate].append(
                    pltpu.make_async_copy(block.at[position, place], whole_ref.at[gate, :, rows, :], sem)
                )
    return copies


def layers_kernel(sizes, is_left, plan, x_ref, *refs):
    devices, qs, group, rows_each = sizes
    blocks, (o_ref, xs, hs, last, whole_ref, sems) = refs[: len(plan)], refs[len(plan) :]
    copies = gate_copies(plan, blocks, whole_ref, sems)
    for gate in range(2):
        for copy in copies[gate]:
            copy.start()
    tile_rows = 2 * qs
    rows, width = x_ref.shape[0] // 2, x_ref.shape[1]
    first = x_ref[...].astype(jnp.float32).reshape(devices, 2 * tile_rows, width)
    first = first[:, :tile_rows] if is_left else first[:, tile_rows:]
    xs[0] = first.reshape(rows, width).astype(jnp.bfloat16)
    hs[0] = swap_sign(first, qs).reshape(rows, width).astype(jnp.bfloat16)
    step = min(512, width)
    for layer in range(2 * CYCLES):
        if layer < 2:
            for copy in copies[layer]:
                copy.wait()
        gate = whole_ref.at[layer % 2]
        here, turned = xs.at[layer % 2], hs.at[layer % 2]
        later = (layer + 1) % 2
        for start in range(0, width, step):
            cols = slice(start, start + step)
            acc = exact_dot(here[...], gate[0, :, cols]) + exact_dot(turned[...], gate[1, :, cols])
            if layer < 2 * CYCLES - 1:
                regroup_store(acc, start, group, devices, tile_rows, xs.at[later], hs.at[later])
            else:
                last[:, cols] = acc.astype(jnp.bfloat16)
    half = rows // 2
    new = lax.broadcasted_iota(jnp.int32, (rows, rows), 0)
    part, inner = new // half, new % half
    if is_left:
        v, r = inner // devices, inner % devices
        picks = one_hot((rows, rows), 1, r * tile_rows + part * qs + v)
        moved = exact_dot(picks, last[...]).astype(jnp.bfloat16)
        span = 2 * rows_each
        each = width * qs // rows_each
        words = width // span
        step = min(256, width)
        for start in range(0, width, step):
            place = start + lax.broadcasted_iota(jnp.int32, (width, step), 1)
            e, rest = place // each, place % each
            h, w, qr = rest // (words * qs), rest % (words * qs) // qs, rest % qs
            lanes = one_hot((width, step), 0, w * span + (e * qs + qr) * 2 + h)
            sent = exact_dot(moved, lanes)
            low_lane = lax.broadcasted_iota(jnp.int32, (half, LANES), 1) < LANES // 2
            for offset in range(0, step, LANES):
                real = sent[:half, offset : offset + LANES]
                imag = sent[half:, offset : offset + LANES]
                e0 = (start + offset) // each
                even = jnp.where(low_lane, real, pltpu.roll(imag, LANES // 2, 1))
                odd = jnp.where(low_lane, pltpu.roll(real, LANES // 2, 1), imag)
                o_ref[e0 * half : (e0 + 1) * half, :] = even.astype(jnp.bfloat16)
                o_ref[(e0 + 1) * half : (e0 + 2) * half, :] = odd.astype(jnp.bfloat16)
    else:
        r, q = inner // qs, inner % qs
        picks = one_hot((rows, rows), 1, r * tile_rows + part * qs + q)
        o_ref[...] = exact_dot(picks, last[...]).astype(jnp.bfloat16)


def join_kernel(sizes, left_ref, right_ref, o_ref):
    devices, us, vs = sizes
    rows = us * devices
    free = right_ref.shape[1] // (2 * KEPT)
    left = left_ref[...].reshape(us, vs, devices, LANES)
    left = jnp.concatenate([left[:, v].reshape(rows, LANES) for v in range(vs)], axis=1)
    new = lax.broadcasted_iota(jnp.int32, (rows, rows), 0)
    picks = one_hot((rows, rows), 1, new % us * devices + new // us)
    left = exact_dot(picks, left).astype(jnp.bfloat16)
    half = right_ref.shape[0] // 2
    depth = half // vs
    real, imag = right_ref[:half, :], right_ref[half:, :]
    block = rows // KEPT
    for g in range(KEPT):
        stack = []
        for v in range(vs):
            r = [real[v * depth : (v + 1) * depth, (h * KEPT + g) * free :][:, :free] for h in range(2)]
            i = [imag[v * depth : (v + 1) * depth, (h * KEPT + g) * free :][:, :free] for h in range(2)]
            to_real = jnp.concatenate([r[0], r[1], -i[0], -i[1]], axis=0)
            to_imag = jnp.concatenate([i[0], i[1], r[0], r[1]], axis=0)
            stack.append(jnp.concatenate([to_real, to_imag], axis=1))
        stack = jnp.concatenate(stack, axis=0)
        part = exact_dot(left[g * block : (g + 1) * block, :], stack)
        o_ref[g * block : (g + 1) * block, :] = part.astype(jnp.bfloat16)


def call(kernel, out_shape, inputs, scratch=(), flops=0, blocks=()):
    moved = sum(x.size * x.dtype.itemsize for x in (*inputs, *blocks))
    return pl.pallas_call(
        kernel,
        out_shape=jax.ShapeDtypeStruct(out_shape, jnp.bfloat16),
        in_specs=whole(len(inputs)) + [pl.BlockSpec(memory_space=pl.ANY)] * len(blocks),
        out_specs=whole(1)[0],
        scratch_shapes=list(scratch),
        compiler_params=pltpu.CompilerParams(vmem_limit_bytes=VMEM_LIMIT),
        cost_estimate=pl.CostEstimate(flops=flops, bytes_accessed=moved, transcendentals=0),
    )(*inputs, *blocks)


def tiles_fit(devices, rows_each, width):
    pair_devices = devices // 2
    if devices < 4 or devices & (devices - 1) or rows_each % pair_devices or width % 256:
        return False
    qs, group = rows_each // pair_devices, width // devices
    return (
        2 * qs == 8
        and LANES % group == 0
        and devices % (LANES // group) == 0
        and qs == SHARED // width
        and devices % 32 == 0
        and 2 * width * qs // rows_each == LANES
        and devices * rows_each * width // SHARED % (KEPT * LANES) == 0
        and 2 * (devices * rows_each * width // SHARED) == width
    )


def fast(branch_in, column_order, gate_a, gate_b):
    devices = lax.axis_size("mode")
    rows_each, width = branch_in.shape[2:]
    halves = devices // 2
    qs, group = rows_each // halves, width // devices
    tile_rows = 2 * qs
    rows = devices * tile_rows
    packed = call(
        functools.partial(pack_kernel, qs),
        (2 * rows, width),
        (branch_in, column_order),
        [pltpu.VMEM((4 * rows_each, width), jnp.bfloat16)],
        8 * rows * width * width,
    )
    blocks, plan, states = spread(gate_a, gate_b, packed.reshape(devices, 2 * tile_rows, width))
    states = states.reshape(2 * rows, width)
    sizes = (devices, qs, group, rows_each)
    scratch = [pltpu.VMEM((2, rows, width), jnp.bfloat16)] * 2 + [
        pltpu.VMEM((rows, width), jnp.bfloat16),
        pltpu.VMEM((2, 2, width, width), jnp.bfloat16),
        pltpu.SemaphoreType.DMA((2, devices)),
    ]
    work = 2 * CYCLES * 4 * rows * width * width
    left = call(
        functools.partial(layers_kernel, sizes, True, plan),
        (halves * rows // 2, LANES),
        (states,),
        scratch,
        work,
        blocks,
    )
    groups = [[h * halves + e for e in range(halves)] for h in range(2)]
    left = trade(left.reshape(halves, rows // 2, LANES), groups)
    right = call(
        functools.partial(layers_kernel, sizes, False, plan), (rows, width), (states,), scratch, work, blocks
    )
    free = width // (2 * KEPT)
    us = halves
    partial_sums = call(
        functools.partial(join_kernel, (devices, us, qs)),
        (devices * us, 2 * free),
        (left.reshape(halves * rows // 2, LANES), right),
        flops=2 * devices * us * LANES * qs * 2 * free,
    )
    parts = trade(partial_sums.reshape(devices, us, 2 * free))
    parts = parts.reshape(2, halves, us, 2 * free).astype(jnp.float32)
    join_scale = (2.0 * SHARED) ** (-0.5)
    return (jnp.sum(parts, axis=1) * join_scale).astype(jnp.bfloat16).reshape(2, us, 2, free)


def flip(value, *bits):
    mask = sum(2**bit for bit in bits)
    pairs = [(source, source ^ mask) for source in range(lax.axis_size("mode"))]
    return lax.ppermute(value, "mode", pairs)


def plane(value, sources):
    over_x, over_y = flip(value, 1), flip(value, 2)
    diagonal = flip(over_x[:1], 2), flip(over_y[1:], 1)
    turned = [tuple(source + more for source in sources) for more in ((1,), (2,), (1, 2))]
    return [
        (value, sources, (0, 1)),
        (over_x, turned[0], (0, 1)),
        (over_y, turned[1], (0, 1)),
        (diagonal[0], turned[2], (0,)),
        (diagonal[1], turned[2], (1,)),
    ]


def spread(gate_a, gate_b, packed):
    bits = lax.axis_size("mode").bit_length() - 1
    own = jnp.stack([gate_a, gate_b])[:, None]
    sets = [(jnp.concatenate([own, flip(own, 3)], axis=1), ((), (3,)))]
    for bit in range(4, bits):
        far = [flip(own, *source, bit) for _, sources in sets for source in sources]
        if bit == 4:
            first, far[0], packed = lax.optimization_barrier((sets[0][0], far[0], packed))
            sets = [(first, sets[0][1])]
        more = [tuple(source + (bit,) for source in sources) for _, sources in sets]
        sets += [(jnp.concatenate(far[2 * n : 2 * n + 2], axis=1), sources) for n, sources in enumerate(more)]
    blocks = []
    for number, (value, sources) in enumerate(sets):
        if number:
            value, *_ = lax.optimization_barrier((value, blocks[-2][0], blocks[-1][0]))
        blocks += plane(value, sources)
    near = [(flip(value, 0), tuple(source + (0,) for source in sources), gates) for value, sources, gates in blocks]
    packed, _ = lax.optimization_barrier((packed, near[-5][0]))
    blocks += near
    plan = tuple((sources, gates) for _, sources, gates in blocks)
    return [value for value, _, _ in blocks], plan, trade(packed)


def trade(value, groups=None):
    return lax.all_to_all(value, "mode", split_axis=0, concat_axis=0, axis_index_groups=groups, tiled=True)


def partner(value, axis, bit):
    mask = 2**bit
    pairs = [(source, source ^ mask) for source in range(lax.axis_size(axis))]
    return lax.ppermute(value, axis, pairs)


def product_four(states, layer_block):
    branches, parts, row_count, width = states.shape
    real_in = states[:, 0].reshape(branches * row_count, width)
    imag_in = states[:, 1].reshape(branches * row_count, width)
    real_part = jnp.dot(real_in, layer_block[0], preferred_element_type=jnp.float32) - jnp.dot(
        imag_in, layer_block[1], preferred_element_type=jnp.float32
    )
    imag_part = jnp.dot(real_in, layer_block[1], preferred_element_type=jnp.float32) + jnp.dot(
        imag_in, layer_block[0], preferred_element_type=jnp.float32
    )
    joined_parts = jnp.stack(
        [
            real_part.reshape(branches, row_count, width),
            imag_part.reshape(branches, row_count, width),
        ],
        axis=1,
    )
    return joined_parts.astype(jnp.bfloat16)


def complex_rows(left_real, left_imag, right_real, right_imag):
    real_part = jnp.dot(left_real, right_real, preferred_element_type=jnp.float32) - jnp.dot(
        left_imag, right_imag, preferred_element_type=jnp.float32
    )
    imag_part = jnp.dot(left_real, right_imag, preferred_element_type=jnp.float32) + jnp.dot(
        left_imag, right_real, preferred_element_type=jnp.float32
    )
    return jnp.stack([real_part, imag_part], axis=1)


def read_bit(device_index, bit_number):
    return device_index // 2**bit_number % 2


def trade_axes(buffer, axis_bits, trader, device_index):
    for position, bit_number in enumerate(axis_bits):
        own_bit = read_bit(device_index, bit_number)
        kept_half = lax.dynamic_index_in_dim(buffer, own_bit, position, keepdims=False)
        sent_half = lax.dynamic_index_in_dim(buffer, 1 - own_bit, position, keepdims=False)
        received = trader(sent_half, bit_number)
        first_half = jnp.where(own_bit == 0, kept_half, received)
        second_half = jnp.where(own_bit == 0, received, kept_half)
        buffer = jnp.stack([first_half, second_half], axis=position)
    return buffer


def general(branch_in, column_order, gate_a, gate_b):
    join_scale = (2.0 * SHARED) ** (-0.5)
    devices_mode = lax.axis_size("mode")
    whole_a, whole_b = (
        lax.all_gather(gate_a, "mode", axis=1, tiled=True),
        lax.all_gather(gate_b, "mode", axis=1, tiled=True),
    )
    states = jnp.take_along_axis(branch_in, column_order[:, None, None, :], axis=3)
    for layer_number in range(2 * CYCLES):
        if layer_number > 0:
            states = lax.all_to_all(states, "mode", split_axis=3, concat_axis=3, tiled=True)
        states = product_four(states, whole_a if layer_number % 2 == 0 else whole_b)
    local_cells = states.shape[2] * states.shape[3]
    local_rows = local_cells // SHARED
    shared_rows = SHARED // devices_mode
    join_width = local_cells // (shared_rows * KEPT)
    results = []
    for pair_number in range(2):
        left_part = states[2 * pair_number].reshape(2, local_rows, SHARED)
        right_part = states[2 * pair_number + 1].reshape(2, shared_rows, KEPT, join_width)
        device_index = lax.axis_index("mode")
        total_bits = devices_mode.bit_length() - 1
        group_bits = total_bits - 4
        batch_bits = KEPT.bit_length() - 1
        groups = devices_mode // (4 * KEPT)
        span = 2 * shared_rows
        outer = SHARED // (span * groups)
        half_join = join_width // 2

        def left_trader(piece, bit_number):
            return partner(piece, "mode", bit_number)

        def right_trader(piece, bit_number):
            return partner(piece, "mode", bit_number)

        left_buffer = left_part.reshape(2, local_rows, outer, groups, span).transpose(3, 0, 1, 2, 4)
        left_buffer = left_buffer.reshape((2,) * group_bits + (1, 2, local_rows, outer, span))
        left_buffer = jnp.broadcast_to(
            left_buffer, (2,) * group_bits + (2, 2, local_rows, outer, span)
        )
        left_bits = [group_bits - position for position in range(group_bits)] + [0]
        left_buffer = trade_axes(left_buffer, left_bits, left_trader, device_index)
        left_block = left_buffer.reshape(devices_mode // (2 * KEPT), 2, local_rows, outer * span)
        left_block = left_block.transpose(1, 0, 2, 3).reshape(2, half_join, SHARED // groups)
        right_buffer = right_part.reshape(2, shared_rows, KEPT, 2, half_join).transpose(
            2, 3, 0, 1, 4
        )
        right_buffer = right_buffer.reshape((2,) * batch_bits + (1, 2, 2, shared_rows, half_join))
        right_buffer = jnp.broadcast_to(
            right_buffer, (2,) * batch_bits + (2, 2, 2, shared_rows, half_join)
        )
        right_bits = [total_bits - 1 - position for position in range(batch_bits)] + [
            total_bits - batch_bits - 1,
            0,
        ]
        right_buffer = trade_axes(right_buffer, right_bits, right_trader, device_index)
        right_block = right_buffer.reshape(2 * KEPT, 2, 2, shared_rows, half_join)
        right_block = right_block.transpose(2, 0, 1, 3, 4).reshape(2, SHARED // groups, half_join)
        running = complex_rows(left_block[0], left_block[1], right_block[0], right_block[1])
        for position in range(group_bits):
            bit_number = group_bits - position
            own_bit = read_bit(device_index, bit_number)
            row_count = running.shape[0]
            halves = running.reshape(2, row_count // 2, 2, half_join)
            kept_half = lax.dynamic_index_in_dim(halves, own_bit, 0, keepdims=False)
            sent_half = lax.dynamic_index_in_dim(halves, 1 - own_bit, 0, keepdims=False)
            running = kept_half + partner(
                sent_half.astype(jnp.bfloat16), "mode", bit_number
            ).astype(sent_half.dtype)
        rounded = (running * join_scale).astype(jnp.bfloat16)
        own_bit = read_bit(device_index, 0)
        halves = rounded.reshape(2, local_rows, 2, half_join)
        kept_half = lax.dynamic_index_in_dim(halves, own_bit, 0, keepdims=False)
        sent_half = lax.dynamic_index_in_dim(halves, 1 - own_bit, 0, keepdims=False)
        received = partner(sent_half, "mode", 0)
        first_half = jnp.where(own_bit == 0, kept_half, received)
        second_half = jnp.where(own_bit == 0, received, kept_half)
        finished = jnp.concatenate([first_half, second_half], axis=2)
        results.append(finished)
    return jnp.stack(results)


def local(branch_in, column_order, gate_a, gate_b):
    branches, _, rows_each, width = branch_in.shape
    if branches == 4 and tiles_fit(lax.axis_size("mode"), rows_each, width):
        return fast(branch_in, column_order, gate_a, gate_b)
    return general(branch_in, column_order, gate_a, gate_b)


def solution(mesh):
    in_specs = (
        P(None, None, ("cuts", "mode"), None),
        P(),
        P(None, "mode", None),
        P(None, "mode", None),
    )
    out_specs = P(None, ("cuts", "mode"), None, None)
    return jax.shard_map(local, mesh=mesh, in_specs=in_specs, out_specs=out_specs, check_vma=False)
```

```python
import functools

import jax
import jax.numpy as jnp
from jax import lax
from jax.experimental import pallas as pl
from jax.experimental.pallas import tpu as pltpu
from jax.sharding import PartitionSpec as P

SHARED = 4096
KEPT = 4
CYCLES = 2
LANES = 128
VMEM_LIMIT = 56 * 1024 * 1024


def whole(count):
    return [pl.BlockSpec(memory_space=pltpu.VMEM)] * count


def one_hot(shape, axis, wanted):
    return (lax.broadcasted_iota(jnp.int32, shape, axis) == wanted).astype(jnp.bfloat16)


def exact_dot(left, right):
    return jnp.dot(left, right, preferred_element_type=jnp.float32)


def pack_kernel(qs, x_ref, order_ref, o_ref, ordered):
    _, parts, rows_each, width = x_ref.shape
    rows = parts * rows_each
    step = min(256, width)
    new = lax.broadcasted_iota(jnp.int32, (2 * rows, 2 * rows), 0)
    e, side = new // (2 * parts * qs), new // (parts * qs) % 2
    k, q = new // qs % parts, new % qs
    pack = one_hot((2 * rows, 2 * rows), 1, side * rows + k * rows_each + e * qs + q)
    for pair in range(x_ref.shape[0] // 2):
        for side in range(2):
            branch = 2 * pair + side
            values = x_ref[branch].reshape(rows, width)
            for start in range(0, width, step):
                picks = one_hot((width, step), 0, order_ref[branch : branch + 1, start : start + step])
                found = exact_dot(values, picks).astype(jnp.bfloat16)
                ordered[side * rows : (side + 1) * rows, start : start + step] = found
        packed = exact_dot(pack, ordered[...]).astype(jnp.bfloat16)
        o_ref[2 * pair * rows : 2 * (pair + 1) * rows, :] = packed


def swap_sign(tiles, qs):
    turned = pltpu.roll(tiles, qs, 1)
    row = lax.broadcasted_iota(jnp.int32, tiles.shape, 1)
    return jnp.where(row < qs, -turned, turned)


def regroup_store(acc, first_lane, group, devices, tile_rows, x_ref, h_ref):
    per = LANES // group
    lane = lax.broadcasted_iota(jnp.int32, (tile_rows, LANES), 1) // group
    for offset in range(0, acc.shape[1], LANES):
        tile = acc[:, offset : offset + LANES].reshape(devices, tile_rows, LANES)
        row_start = (first_lane + offset) // group * tile_rows
        for block in range(devices // per):
            parts = [tile[block * per + m] for m in range(per)]
            bit = 1
            while bit < per:
                moved = list(parts)
                keep = (lane // bit) % 2 == 0
                for m in range(per):
                    if m & bit:
                        continue
                    low, high = parts[m], parts[m | bit]
                    moved[m] = jnp.where(keep, low, pltpu.roll(high, bit * group, 1))
                    moved[m | bit] = jnp.where(keep, pltpu.roll(low, LANES - bit * group, 1), high)
                parts = moved
                bit *= 2
            tiles = jnp.stack(parts)
            rows = pl.ds(row_start, per * tile_rows)
            lanes = pl.ds(block * LANES, LANES)
            x_ref[rows, lanes] = tiles.reshape(per * tile_rows, LANES).astype(jnp.bfloat16)
            turned = swap_sign(tiles, tile_rows // 2)
            h_ref[rows, lanes] = turned.reshape(per * tile_rows, LANES).astype(jnp.bfloat16)


def gate_copies(plan, blocks, whole_ref, sems):
    me = lax.axis_index("mode")
    copies = ([], [])
    for (sources, gates), block in zip(plan, blocks):
        for place, source in enumerate(sources):
            device = me
            for bit in source:
                device = device + (1 - 2 * (me // 2**bit % 2)) * 2**bit
            size = block.shape[3]
            rows = pl.ds(pl.multiple_of(device * size, size), size)
            for position, gate in enumerate(gates):
                sem = sems.at[gate, len(copies[gate])]
                copies[gate].append(
                    pltpu.make_async_copy(block.at[position, place], whole_ref.at[gate, :, rows, :], sem)
                )
    return copies


def layers_kernel(sizes, is_left, plan, x_ref, *refs):
    devices, qs, group, rows_each = sizes
    blocks, (o_ref, xs, hs, last, whole_ref, sems) = refs[: len(plan)], refs[len(plan) :]
    copies = gate_copies(plan, blocks, whole_ref, sems)
    for gate in range(2):
        for copy in copies[gate]:
            copy.start()
    tile_rows = 2 * qs
    rows, width = x_ref.shape[0] // 2, x_ref.shape[1]
    first = x_ref[...].astype(jnp.float32).reshape(devices, 2 * tile_rows, width)
    first = first[:, :tile_rows] if is_left else first[:, tile_rows:]
    xs[0] = first.reshape(rows, width).astype(jnp.bfloat16)
    hs[0] = swap_sign(first, qs).reshape(rows, width).astype(jnp.bfloat16)
    step = min(512, width)
    for layer in range(2 * CYCLES):
        if layer < 2:
            for copy in copies[layer]:
                copy.wait()
        gate = whole_ref.at[layer % 2]
        here, turned = xs.at[layer % 2], hs.at[layer % 2]
        later = (layer + 1) % 2
        for start in range(0, width, step):
            cols = slice(start, start + step)
            acc = exact_dot(here[...], gate[0, :, cols]) + exact_dot(turned[...], gate[1, :, cols])
            if layer < 2 * CYCLES - 1:
                regroup_store(acc, start, group, devices, tile_rows, xs.at[later], hs.at[later])
            else:
                last[:, cols] = acc.astype(jnp.bfloat16)
    half = rows // 2
    new = lax.broadcasted_iota(jnp.int32, (rows, rows), 0)
    part, inner = new // half, new % half
    if is_left:
        v, r = inner // devices, inner % devices
        picks = one_hot((rows, rows), 1, r * tile_rows + part * qs + v)
        moved = exact_dot(picks, last[...]).astype(jnp.bfloat16)
        span = 2 * rows_each
        each = width * qs // rows_each
        words = width // span
        step = min(256, width)
        for start in range(0, width, step):
            place = start + lax.broadcasted_iota(jnp.int32, (width, step), 1)
            e, rest = place // each, place % each
            h, w, qr = rest // (words * qs), rest % (words * qs) // qs, rest % qs
            lanes = one_hot((width, step), 0, w * span + (e * qs + qr) * 2 + h)
            sent = exact_dot(moved, lanes)
            low_lane = lax.broadcasted_iota(jnp.int32, (half, LANES), 1) < LANES // 2
            for offset in range(0, step, LANES):
                real = sent[:half, offset : offset + LANES]
                imag = sent[half:, offset : offset + LANES]
                e0 = (start + offset) // each
                even = jnp.where(low_lane, real, pltpu.roll(imag, LANES // 2, 1))
                odd = jnp.where(low_lane, pltpu.roll(real, LANES // 2, 1), imag)
                o_ref[e0 * half : (e0 + 1) * half, :] = even.astype(jnp.bfloat16)
                o_ref[(e0 + 1) * half : (e0 + 2) * half, :] = odd.astype(jnp.bfloat16)
    else:
        r, q = inner // qs, inner % qs
        picks = one_hot((rows, rows), 1, r * tile_rows + part * qs + q)
        o_ref[...] = exact_dot(picks, last[...]).astype(jnp.bfloat16)


def join_kernel(sizes, left_ref, right_ref, o_ref):
    devices, us, vs = sizes
    rows = us * devices
    free = right_ref.shape[1] // (2 * KEPT)
    left = left_ref[...].reshape(us, vs, devices, LANES)
    left = jnp.concatenate([left[:, v].reshape(rows, LANES) for v in range(vs)], axis=1)
    new = lax.broadcasted_iota(jnp.int32, (rows, rows), 0)
    picks = one_hot((rows, rows), 1, new % us * devices + new // us)
    left = exact_dot(picks, left).astype(jnp.bfloat16)
    half = right_ref.shape[0] // 2
    depth = half // vs
    real, imag = right_ref[:half, :], right_ref[half:, :]
    block = rows // KEPT
    for g in range(KEPT):
        stack = []
        for v in range(vs):
            r = [real[v * depth : (v + 1) * depth, (h * KEPT + g) * free :][:, :free] for h in range(2)]
            i = [imag[v * depth : (v + 1) * depth, (h * KEPT + g) * free :][:, :free] for h in range(2)]
            to_real = jnp.concatenate([r[0], r[1], -i[0], -i[1]], axis=0)
            to_imag = jnp.concatenate([i[0], i[1], r[0], r[1]], axis=0)
            stack.append(jnp.concatenate([to_real, to_imag], axis=1))
        stack = jnp.concatenate(stack, axis=0)
        part = exact_dot(left[g * block : (g + 1) * block, :], stack)
        o_ref[g * block : (g + 1) * block, :] = part.astype(jnp.bfloat16)


def call(kernel, out_shape, inputs, scratch=(), flops=0, blocks=()):
    moved = sum(x.size * x.dtype.itemsize for x in (*inputs, *blocks))
    return pl.pallas_call(
        kernel,
        out_shape=jax.ShapeDtypeStruct(out_shape, jnp.bfloat16),
        in_specs=whole(len(inputs)) + [pl.BlockSpec(memory_space=pl.ANY)] * len(blocks),
        out_specs=whole(1)[0],
        scratch_shapes=list(scratch),
        compiler_params=pltpu.CompilerParams(vmem_limit_bytes=VMEM_LIMIT),
        cost_estimate=pl.CostEstimate(flops=flops, bytes_accessed=moved, transcendentals=0),
    )(*inputs, *blocks)


def tiles_fit(devices, rows_each, width):
    pair_devices = devices // 2
    if devices < 4 or devices & (devices - 1) or rows_each % pair_devices or width % 256:
        return False
    qs, group = rows_each // pair_devices, width // devices
    return (
        2 * qs == 8
        and LANES % group == 0
        and devices % (LANES // group) == 0
        and qs == SHARED // width
        and devices % 32 == 0
        and 2 * width * qs // rows_each == LANES
        and devices * rows_each * width // SHARED % (KEPT * LANES) == 0
        and 2 * (devices * rows_each * width // SHARED) == width
    )


def fast(branch_in, column_order, gate_a, gate_b):
    devices = lax.axis_size("mode")
    rows_each, width = branch_in.shape[2:]
    halves = devices // 2
    qs, group = rows_each // halves, width // devices
    tile_rows = 2 * qs
    rows = devices * tile_rows
    packed = call(
        functools.partial(pack_kernel, qs),
        (2 * rows, width),
        (branch_in, column_order),
        [pltpu.VMEM((4 * rows_each, width), jnp.bfloat16)],
        8 * rows * width * width,
    )
    blocks, plan, states = spread(gate_a, gate_b, packed.reshape(devices, 2 * tile_rows, width))
    states = states.reshape(2 * rows, width)
    sizes = (devices, qs, group, rows_each)
    scratch = [pltpu.VMEM((2, rows, width), jnp.bfloat16)] * 2 + [
        pltpu.VMEM((rows, width), jnp.bfloat16),
        pltpu.VMEM((2, 2, width, width), jnp.bfloat16),
        pltpu.SemaphoreType.DMA((2, devices)),
    ]
    work = 2 * CYCLES * 4 * rows * width * width
    left = call(
        functools.partial(layers_kernel, sizes, True, plan),
        (halves * rows // 2, LANES),
        (states,),
        scratch,
        work,
        blocks,
    )
    groups = [[h * halves + e for e in range(halves)] for h in range(2)]
    left = trade(left.reshape(halves, rows // 2, LANES), groups)
    right = call(
        functools.partial(layers_kernel, sizes, False, plan), (rows, width), (states,), scratch, work, blocks
    )
    free = width // (2 * KEPT)
    us = halves
    partial_sums = call(
        functools.partial(join_kernel, (devices, us, qs)),
        (devices * us, 2 * free),
        (left.reshape(halves * rows // 2, LANES), right),
        flops=2 * devices * us * LANES * qs * 2 * free,
    )
    parts = trade(partial_sums.reshape(devices, us, 2 * free))
    parts = parts.reshape(2, halves, us, 2 * free).astype(jnp.float32)
    join_scale = (2.0 * SHARED) ** (-0.5)
    return (jnp.sum(parts, axis=1) * join_scale).astype(jnp.bfloat16).reshape(2, us, 2, free)


def flip(value, *bits):
    mask = sum(2**bit for bit in bits)
    pairs = [(source, source ^ mask) for source in range(lax.axis_size("mode"))]
    return lax.ppermute(value, "mode", pairs)


def plane(value, sources, early):
    over_x, over_y, *_ = lax.optimization_barrier((flip(value, 1), flip(value, 2), *early))
    diagonal = flip(over_x[:1], 2), flip(over_y[1:], 1)
    turned = [tuple(source + more for source in sources) for more in ((1,), (2,), (1, 2))]
    return [
        (value, sources, (0, 1)),
        (over_x, turned[0], (0, 1)),
        (over_y, turned[1], (0, 1)),
        (diagonal[0], turned[2], (0,)),
        (diagonal[1], turned[2], (1,)),
    ]


def spread(gate_a, gate_b, packed):
    bits = lax.axis_size("mode").bit_length() - 1
    own = jnp.stack([gate_a, gate_b])[:, None]
    far = [()]
    for bit in range(3, bits):
        far += [source + (bit,) for source in far]
    far = sorted(far[1:], key=len)
    came = [flip(own, *source) for source in far]
    sets = [(own, ((),))]
    for start in range(0, len(far), 2):
        value = jnp.concatenate(came[start : start + 2], axis=1)
        sets.append((value, tuple(far[start : start + 2])))
    blocks = []
    for number, (value, sources) in enumerate(sets):
        if number == 1:
            value, packed, *_ = lax.optimization_barrier((value, packed, blocks[-2][0], blocks[-1][0]))
        elif number:
            value, *_ = lax.optimization_barrier((value, blocks[-4][0], blocks[-3][0]))
        early = [later for later, _ in sets[2:]] if number == 1 else []
        blocks += plane(value, sources, early)
    blocks += [
        (flip(value, 0), tuple(source + (0,) for source in sources), gates) for value, sources, gates in blocks
    ]
    plan = tuple((sources, gates) for _, sources, gates in blocks)
    return [value for value, _, _ in blocks], plan, trade(packed)


def trade(value, groups=None):
    return lax.all_to_all(value, "mode", split_axis=0, concat_axis=0, axis_index_groups=groups, tiled=True)


def partner(value, axis, bit):
    mask = 2**bit
    pairs = [(source, source ^ mask) for source in range(lax.axis_size(axis))]
    return lax.ppermute(value, axis, pairs)


def product_four(states, layer_block):
    branches, parts, row_count, width = states.shape
    real_in = states[:, 0].reshape(branches * row_count, width)
    imag_in = states[:, 1].reshape(branches * row_count, width)
    real_part = jnp.dot(real_in, layer_block[0], preferred_element_type=jnp.float32) - jnp.dot(
        imag_in, layer_block[1], preferred_element_type=jnp.float32
    )
    imag_part = jnp.dot(real_in, layer_block[1], preferred_element_type=jnp.float32) + jnp.dot(
        imag_in, layer_block[0], preferred_element_type=jnp.float32
    )
    joined_parts = jnp.stack(
        [
            real_part.reshape(branches, row_count, width),
            imag_part.reshape(branches, row_count, width),
        ],
        axis=1,
    )
    return joined_parts.astype(jnp.bfloat16)


def complex_rows(left_real, left_imag, right_real, right_imag):
    real_part = jnp.dot(left_real, right_real, preferred_element_type=jnp.float32) - jnp.dot(
        left_imag, right_imag, preferred_element_type=jnp.float32
    )
    imag_part = jnp.dot(left_real, right_imag, preferred_element_type=jnp.float32) + jnp.dot(
        left_imag, right_real, preferred_element_type=jnp.float32
    )
    return jnp.stack([real_part, imag_part], axis=1)


def read_bit(device_index, bit_number):
    return device_index // 2**bit_number % 2


def trade_axes(buffer, axis_bits, trader, device_index):
    for position, bit_number in enumerate(axis_bits):
        own_bit = read_bit(device_index, bit_number)
        kept_half = lax.dynamic_index_in_dim(buffer, own_bit, position, keepdims=False)
        sent_half = lax.dynamic_index_in_dim(buffer, 1 - own_bit, position, keepdims=False)
        received = trader(sent_half, bit_number)
        first_half = jnp.where(own_bit == 0, kept_half, received)
        second_half = jnp.where(own_bit == 0, received, kept_half)
        buffer = jnp.stack([first_half, second_half], axis=position)
    return buffer


def general(branch_in, column_order, gate_a, gate_b):
    join_scale = (2.0 * SHARED) ** (-0.5)
    devices_mode = lax.axis_size("mode")
    whole_a, whole_b = (
        lax.all_gather(gate_a, "mode", axis=1, tiled=True),
        lax.all_gather(gate_b, "mode", axis=1, tiled=True),
    )
    states = jnp.take_along_axis(branch_in, column_order[:, None, None, :], axis=3)
    for layer_number in range(2 * CYCLES):
        if layer_number > 0:
            states = lax.all_to_all(states, "mode", split_axis=3, concat_axis=3, tiled=True)
        states = product_four(states, whole_a if layer_number % 2 == 0 else whole_b)
    local_cells = states.shape[2] * states.shape[3]
    local_rows = local_cells // SHARED
    shared_rows = SHARED // devices_mode
    join_width = local_cells // (shared_rows * KEPT)
    results = []
    for pair_number in range(2):
        left_part = states[2 * pair_number].reshape(2, local_rows, SHARED)
        right_part = states[2 * pair_number + 1].reshape(2, shared_rows, KEPT, join_width)
        device_index = lax.axis_index("mode")
        total_bits = devices_mode.bit_length() - 1
        group_bits = total_bits - 4
        batch_bits = KEPT.bit_length() - 1
        groups = devices_mode // (4 * KEPT)
        span = 2 * shared_rows
        outer = SHARED // (span * groups)
        half_join = join_width // 2

        def left_trader(piece, bit_number):
            return partner(piece, "mode", bit_number)

        def right_trader(piece, bit_number):
            return partner(piece, "mode", bit_number)

        left_buffer = left_part.reshape(2, local_rows, outer, groups, span).transpose(3, 0, 1, 2, 4)
        left_buffer = left_buffer.reshape((2,) * group_bits + (1, 2, local_rows, outer, span))
        left_buffer = jnp.broadcast_to(
            left_buffer, (2,) * group_bits + (2, 2, local_rows, outer, span)
        )
        left_bits = [group_bits - position for position in range(group_bits)] + [0]
        left_buffer = trade_axes(left_buffer, left_bits, left_trader, device_index)
        left_block = left_buffer.reshape(devices_mode // (2 * KEPT), 2, local_rows, outer * span)
        left_block = left_block.transpose(1, 0, 2, 3).reshape(2, half_join, SHARED // groups)
        right_buffer = right_part.reshape(2, shared_rows, KEPT, 2, half_join).transpose(
            2, 3, 0, 1, 4
        )
        right_buffer = right_buffer.reshape((2,) * batch_bits + (1, 2, 2, shared_rows, half_join))
        right_buffer = jnp.broadcast_to(
            right_buffer, (2,) * batch_bits + (2, 2, 2, shared_rows, half_join)
        )
        right_bits = [total_bits - 1 - position for position in range(batch_bits)] + [
            total_bits - batch_bits - 1,
            0,
        ]
        right_buffer = trade_axes(right_buffer, right_bits, right_trader, device_index)
        right_block = right_buffer.reshape(2 * KEPT, 2, 2, shared_rows, half_join)
        right_block = right_block.transpose(2, 0, 1, 3, 4).reshape(2, SHARED // groups, half_join)
        running = complex_rows(left_block[0], left_block[1], right_block[0], right_block[1])
        for position in range(group_bits):
            bit_number = group_bits - position
            own_bit = read_bit(device_index, bit_number)
            row_count = running.shape[0]
            halves = running.reshape(2, row_count // 2, 2, half_join)
            kept_half = lax.dynamic_index_in_dim(halves, own_bit, 0, keepdims=False)
            sent_half = lax.dynamic_index_in_dim(halves, 1 - own_bit, 0, keepdims=False)
            running = kept_half + partner(
                sent_half.astype(jnp.bfloat16), "mode", bit_number
            ).astype(sent_half.dtype)
        rounded = (running * join_scale).astype(jnp.bfloat16)
        own_bit = read_bit(device_index, 0)
        halves = rounded.reshape(2, local_rows, 2, half_join)
        kept_half = lax.dynamic_index_in_dim(halves, own_bit, 0, keepdims=False)
        sent_half = lax.dynamic_index_in_dim(halves, 1 - own_bit, 0, keepdims=False)
        received = partner(sent_half, "mode", 0)
        first_half = jnp.where(own_bit == 0, kept_half, received)
        second_half = jnp.where(own_bit == 0, received, kept_half)
        finished = jnp.concatenate([first_half, second_half], axis=2)
        results.append(finished)
    return jnp.stack(results)


def local(branch_in, column_order, gate_a, gate_b):
    branches, _, rows_each, width = branch_in.shape
    if branches == 4 and tiles_fit(lax.axis_size("mode"), rows_each, width):
        return fast(branch_in, column_order, gate_a, gate_b)
    return general(branch_in, column_order, gate_a, gate_b)


def solution(mesh):
    in_specs = (
        P(None, None, ("cuts", "mode"), None),
        P(),
        P(None, "mode", None),
        P(None, "mode", None),
    )
    out_specs = P(None, ("cuts", "mode"), None, None)
    return jax.shard_map(local, mesh=mesh, in_specs=in_specs, out_specs=out_specs, check_vma=False)
```

```python
import functools

import jax
import jax.numpy as jnp
from jax import lax
from jax.experimental import pallas as pl
from jax.experimental.pallas import tpu as pltpu
from jax.sharding import PartitionSpec as P

SHARED = 4096
KEPT = 4
CYCLES = 2
LANES = 128
VMEM_LIMIT = 24 * 1024 * 1024


def whole(count):
    return [pl.BlockSpec(memory_space=pltpu.VMEM)] * count


def one_hot(shape, axis, wanted):
    return (lax.broadcasted_iota(jnp.int32, shape, axis) == wanted).astype(jnp.bfloat16)


def exact_dot(left, right):
    return jnp.dot(left, right, preferred_element_type=jnp.float32)


def pack_kernel(qs, x_ref, order_ref, o_ref, ordered):
    _, parts, rows_each, width = x_ref.shape
    rows = parts * rows_each
    step = min(256, width)
    new = lax.broadcasted_iota(jnp.int32, (2 * rows, 2 * rows), 0)
    e, side = new // (2 * parts * qs), new // (parts * qs) % 2
    k, q = new // qs % parts, new % qs
    pack = one_hot((2 * rows, 2 * rows), 1, side * rows + k * rows_each + e * qs + q)
    for pair in range(x_ref.shape[0] // 2):
        for side in range(2):
            branch = 2 * pair + side
            values = x_ref[branch].reshape(rows, width)
            for start in range(0, width, step):
                picks = one_hot((width, step), 0, order_ref[branch : branch + 1, start : start + step])
                found = exact_dot(values, picks).astype(jnp.bfloat16)
                ordered[side * rows : (side + 1) * rows, start : start + step] = found
        packed = exact_dot(pack, ordered[...]).astype(jnp.bfloat16)
        o_ref[2 * pair * rows : 2 * (pair + 1) * rows, :] = packed


def swap_sign(tiles, qs):
    turned = pltpu.roll(tiles, qs, 1)
    row = lax.broadcasted_iota(jnp.int32, tiles.shape, 1)
    return jnp.where(row < qs, -turned, turned)


def regroup_store(acc, first_lane, group, devices, tile_rows, x_ref, h_ref):
    per = LANES // group
    lane = lax.broadcasted_iota(jnp.int32, (tile_rows, LANES), 1) // group
    for offset in range(0, acc.shape[1], LANES):
        tile = acc[:, offset : offset + LANES].reshape(devices, tile_rows, LANES)
        row_start = (first_lane + offset) // group * tile_rows
        for block in range(devices // per):
            parts = [tile[block * per + m] for m in range(per)]
            bit = 1
            while bit < per:
                moved = list(parts)
                keep = (lane // bit) % 2 == 0
                for m in range(per):
                    if m & bit:
                        continue
                    low, high = parts[m], parts[m | bit]
                    moved[m] = jnp.where(keep, low, pltpu.roll(high, bit * group, 1))
                    moved[m | bit] = jnp.where(keep, pltpu.roll(low, LANES - bit * group, 1), high)
                parts = moved
                bit *= 2
            tiles = jnp.stack(parts)
            rows = pl.ds(row_start, per * tile_rows)
            lanes = pl.ds(block * LANES, LANES)
            x_ref[rows, lanes] = tiles.reshape(per * tile_rows, LANES).astype(jnp.bfloat16)
            turned = swap_sign(tiles, tile_rows // 2)
            h_ref[rows, lanes] = turned.reshape(per * tile_rows, LANES).astype(jnp.bfloat16)


def gate_copies(plan, blocks, whole_ref, sems):
    me = lax.axis_index("mode")
    copies = ([], [])
    for (sources, gates), block in zip(plan, blocks):
        for place, source in enumerate(sources):
            device = me
            for bit in source:
                device = device + (1 - 2 * (me // 2**bit % 2)) * 2**bit
            size = block.shape[3]
            rows = pl.ds(pl.multiple_of(device * size, size), size)
            for position, gate in enumerate(gates):
                sem = sems.at[gate, len(copies[gate])]
                copies[gate].append(
                    pltpu.make_async_copy(block.at[position, place], whole_ref.at[gate, :, rows, :], sem)
                )
    return copies


def layers_kernel(sizes, is_left, plan, x_ref, *refs):
    devices, qs, group, rows_each = sizes
    blocks, (o_ref, xs, hs, last, whole_ref, sems) = refs[: len(plan)], refs[len(plan) :]
    copies = gate_copies(plan, blocks, whole_ref, sems)
    for gate in range(2):
        for copy in copies[gate]:
            copy.start()
    tile_rows = 2 * qs
    rows, width = x_ref.shape[0] // 2, x_ref.shape[1]
    first = x_ref[...].astype(jnp.float32).reshape(devices, 2 * tile_rows, width)
    first = first[:, :tile_rows] if is_left else first[:, tile_rows:]
    xs[0] = first.reshape(rows, width).astype(jnp.bfloat16)
    hs[0] = swap_sign(first, qs).reshape(rows, width).astype(jnp.bfloat16)
    step = min(512, width)
    for layer in range(2 * CYCLES):
        if layer < 2:
            for copy in copies[layer]:
                copy.wait()
        gate = whole_ref.at[layer % 2]
        here, turned = xs.at[layer % 2], hs.at[layer % 2]
        later = (layer + 1) % 2
        for start in range(0, width, step):
            cols = slice(start, start + step)
            acc = exact_dot(here[...], gate[0, :, cols]) + exact_dot(turned[...], gate[1, :, cols])
            if layer < 2 * CYCLES - 1:
                regroup_store(acc, start, group, devices, tile_rows, xs.at[later], hs.at[later])
            else:
                last[:, cols] = acc.astype(jnp.bfloat16)
    half = rows // 2
    new = lax.broadcasted_iota(jnp.int32, (rows, rows), 0)
    part, inner = new // half, new % half
    if is_left:
        v, r = inner // devices, inner % devices
        picks = one_hot((rows, rows), 1, r * tile_rows + part * qs + v)
        moved = exact_dot(picks, last[...]).astype(jnp.bfloat16)
        span = 2 * rows_each
        each = width * qs // rows_each
        words = width // span
        step = min(256, width)
        for start in range(0, width, step):
            place = start + lax.broadcasted_iota(jnp.int32, (width, step), 1)
            e, rest = place // each, place % each
            h, w, qr = rest // (words * qs), rest % (words * qs) // qs, rest % qs
            lanes = one_hot((width, step), 0, w * span + (e * qs + qr) * 2 + h)
            sent = exact_dot(moved, lanes)
            low_lane = lax.broadcasted_iota(jnp.int32, (half, LANES), 1) < LANES // 2
            for offset in range(0, step, LANES):
                real = sent[:half, offset : offset + LANES]
                imag = sent[half:, offset : offset + LANES]
                e0 = (start + offset) // each
                even = jnp.where(low_lane, real, pltpu.roll(imag, LANES // 2, 1))
                odd = jnp.where(low_lane, pltpu.roll(real, LANES // 2, 1), imag)
                o_ref[e0 * half : (e0 + 1) * half, :] = even.astype(jnp.bfloat16)
                o_ref[(e0 + 1) * half : (e0 + 2) * half, :] = odd.astype(jnp.bfloat16)
    else:
        r, q = inner // qs, inner % qs
        picks = one_hot((rows, rows), 1, r * tile_rows + part * qs + q)
        o_ref[...] = exact_dot(picks, last[...]).astype(jnp.bfloat16)


def join_kernel(sizes, left_ref, right_ref, o_ref):
    devices, us, vs = sizes
    rows = us * devices
    free = right_ref.shape[1] // (2 * KEPT)
    left = left_ref[...].reshape(us, vs, devices, LANES)
    left = jnp.concatenate([left[:, v].reshape(rows, LANES) for v in range(vs)], axis=1)
    new = lax.broadcasted_iota(jnp.int32, (rows, rows), 0)
    picks = one_hot((rows, rows), 1, new % us * devices + new // us)
    left = exact_dot(picks, left).astype(jnp.bfloat16)
    half = right_ref.shape[0] // 2
    depth = half // vs
    real, imag = right_ref[:half, :], right_ref[half:, :]
    block = rows // KEPT
    for g in range(KEPT):
        stack = []
        for v in range(vs):
            r = [real[v * depth : (v + 1) * depth, (h * KEPT + g) * free :][:, :free] for h in range(2)]
            i = [imag[v * depth : (v + 1) * depth, (h * KEPT + g) * free :][:, :free] for h in range(2)]
            to_real = jnp.concatenate([r[0], r[1], -i[0], -i[1]], axis=0)
            to_imag = jnp.concatenate([i[0], i[1], r[0], r[1]], axis=0)
            stack.append(jnp.concatenate([to_real, to_imag], axis=1))
        stack = jnp.concatenate(stack, axis=0)
        part = exact_dot(left[g * block : (g + 1) * block, :], stack)
        o_ref[g * block : (g + 1) * block, :] = part.astype(jnp.bfloat16)


def call(kernel, out_shape, inputs, scratch=(), flops=0, blocks=()):
    moved = sum(x.size * x.dtype.itemsize for x in (*inputs, *blocks))
    return pl.pallas_call(
        kernel,
        out_shape=jax.ShapeDtypeStruct(out_shape, jnp.bfloat16),
        in_specs=whole(len(inputs)) + [pl.BlockSpec(memory_space=pl.ANY)] * len(blocks),
        out_specs=whole(1)[0],
        scratch_shapes=list(scratch),
        compiler_params=pltpu.CompilerParams(vmem_limit_bytes=VMEM_LIMIT),
        cost_estimate=pl.CostEstimate(flops=flops, bytes_accessed=moved, transcendentals=0),
    )(*inputs, *blocks)


def tiles_fit(devices, rows_each, width):
    pair_devices = devices // 2
    if devices < 4 or devices & (devices - 1) or rows_each % pair_devices or width % 256:
        return False
    qs, group = rows_each // pair_devices, width // devices
    return (
        2 * qs == 8
        and LANES % group == 0
        and devices % (LANES // group) == 0
        and qs == SHARED // width
        and devices % 32 == 0
        and 2 * width * qs // rows_each == LANES
        and devices * rows_each * width // SHARED % (KEPT * LANES) == 0
        and 2 * (devices * rows_each * width // SHARED) == width
    )


def fast(branch_in, column_order, gate_a, gate_b):
    devices = lax.axis_size("mode")
    rows_each, width = branch_in.shape[2:]
    halves = devices // 2
    qs, group = rows_each // halves, width // devices
    tile_rows = 2 * qs
    rows = devices * tile_rows
    packed = call(
        functools.partial(pack_kernel, qs),
        (2 * rows, width),
        (branch_in, column_order),
        [pltpu.VMEM((4 * rows_each, width), jnp.bfloat16)],
        8 * rows * width * width,
    )
    blocks, plan, states = spread(gate_a, gate_b, packed.reshape(devices, 2 * tile_rows, width))
    states = states.reshape(2 * rows, width)
    sizes = (devices, qs, group, rows_each)
    scratch = [pltpu.VMEM((2, rows, width), jnp.bfloat16)] * 2 + [
        pltpu.VMEM((rows, width), jnp.bfloat16),
        pltpu.VMEM((2, 2, width, width), jnp.bfloat16),
        pltpu.SemaphoreType.DMA((2, devices)),
    ]
    work = 2 * CYCLES * 4 * rows * width * width
    left = call(
        functools.partial(layers_kernel, sizes, True, plan),
        (halves * rows // 2, LANES),
        (states,),
        scratch,
        work,
        blocks,
    )
    groups = [[h * halves + e for e in range(halves)] for h in range(2)]
    left = trade(left.reshape(halves, rows // 2, LANES), groups)
    right = call(
        functools.partial(layers_kernel, sizes, False, plan), (rows, width), (states,), scratch, work, blocks
    )
    free = width // (2 * KEPT)
    us = halves
    partial_sums = call(
        functools.partial(join_kernel, (devices, us, qs)),
        (devices * us, 2 * free),
        (left.reshape(halves * rows // 2, LANES), right),
        flops=2 * devices * us * LANES * qs * 2 * free,
    )
    parts = trade(partial_sums.reshape(devices, us, 2 * free))
    parts = parts.reshape(2, halves, us, 2 * free).astype(jnp.float32)
    join_scale = (2.0 * SHARED) ** (-0.5)
    return (jnp.sum(parts, axis=1) * join_scale).astype(jnp.bfloat16).reshape(2, us, 2, free)


def flip(value, *bits):
    mask = sum(2**bit for bit in bits)
    pairs = [(source, source ^ mask) for source in range(lax.axis_size("mode"))]
    return lax.ppermute(value, "mode", pairs)


def plane(value, sources):
    over_x, over_y = flip(value, 1), flip(value, 2)
    diagonal = flip(over_x[:1], 2), flip(over_y[1:], 1)
    turned = [tuple(source + more for source in sources) for more in ((1,), (2,), (1, 2))]
    return [
        (value, sources, (0, 1)),
        (over_x, turned[0], (0, 1)),
        (over_y, turned[1], (0, 1)),
        (diagonal[0], turned[2], (0,)),
        (diagonal[1], turned[2], (1,)),
    ]


def spread(gate_a, gate_b, packed):
    bits = lax.axis_size("mode").bit_length() - 1
    own = jnp.stack([gate_a, gate_b])[:, None]
    blocks = plane(own, ((),))
    far = [()]
    for bit in range(3, bits):
        far += [source + (bit,) for source in far]
    far = tuple(far[1:])
    value = jnp.concatenate([flip(own, *source) for source in far], axis=1)
    value, packed, *_ = lax.optimization_barrier((value, packed, blocks[-2][0], blocks[-1][0]))
    blocks += plane(value, far)
    near = []
    for number, (value, sources, gates) in enumerate(blocks):
        if number >= len(blocks) - 2:
            value, *_ = lax.optimization_barrier((value, *[earlier for earlier, _, _ in near[: len(blocks) - 2]]))
        near.append((flip(value, 0), tuple(source + (0,) for source in sources), gates))
    blocks += near
    plan = tuple((sources, gates) for _, sources, gates in blocks)
    return [value for value, _, _ in blocks], plan, trade(packed)


def trade(value, groups=None):
    return lax.all_to_all(value, "mode", split_axis=0, concat_axis=0, axis_index_groups=groups, tiled=True)


def partner(value, axis, bit):
    mask = 2**bit
    pairs = [(source, source ^ mask) for source in range(lax.axis_size(axis))]
    return lax.ppermute(value, axis, pairs)


def product_four(states, layer_block):
    branches, parts, row_count, width = states.shape
    real_in = states[:, 0].reshape(branches * row_count, width)
    imag_in = states[:, 1].reshape(branches * row_count, width)
    real_part = jnp.dot(real_in, layer_block[0], preferred_element_type=jnp.float32) - jnp.dot(
        imag_in, layer_block[1], preferred_element_type=jnp.float32
    )
    imag_part = jnp.dot(real_in, layer_block[1], preferred_element_type=jnp.float32) + jnp.dot(
        imag_in, layer_block[0], preferred_element_type=jnp.float32
    )
    joined_parts = jnp.stack(
        [
            real_part.reshape(branches, row_count, width),
            imag_part.reshape(branches, row_count, width),
        ],
        axis=1,
    )
    return joined_parts.astype(jnp.bfloat16)


def complex_rows(left_real, left_imag, right_real, right_imag):
    real_part = jnp.dot(left_real, right_real, preferred_element_type=jnp.float32) - jnp.dot(
        left_imag, right_imag, preferred_element_type=jnp.float32
    )
    imag_part = jnp.dot(left_real, right_imag, preferred_element_type=jnp.float32) + jnp.dot(
        left_imag, right_real, preferred_element_type=jnp.float32
    )
    return jnp.stack([real_part, imag_part], axis=1)


def read_bit(device_index, bit_number):
    return device_index // 2**bit_number % 2


def trade_axes(buffer, axis_bits, trader, device_index):
    for position, bit_number in enumerate(axis_bits):
        own_bit = read_bit(device_index, bit_number)
        kept_half = lax.dynamic_index_in_dim(buffer, own_bit, position, keepdims=False)
        sent_half = lax.dynamic_index_in_dim(buffer, 1 - own_bit, position, keepdims=False)
        received = trader(sent_half, bit_number)
        first_half = jnp.where(own_bit == 0, kept_half, received)
        second_half = jnp.where(own_bit == 0, received, kept_half)
        buffer = jnp.stack([first_half, second_half], axis=position)
    return buffer


def general(branch_in, column_order, gate_a, gate_b):
    join_scale = (2.0 * SHARED) ** (-0.5)
    devices_mode = lax.axis_size("mode")
    whole_a, whole_b = (
        lax.all_gather(gate_a, "mode", axis=1, tiled=True),
        lax.all_gather(gate_b, "mode", axis=1, tiled=True),
    )
    states = jnp.take_along_axis(branch_in, column_order[:, None, None, :], axis=3)
    for layer_number in range(2 * CYCLES):
        if layer_number > 0:
            states = lax.all_to_all(states, "mode", split_axis=3, concat_axis=3, tiled=True)
        states = product_four(states, whole_a if layer_number % 2 == 0 else whole_b)
    local_cells = states.shape[2] * states.shape[3]
    local_rows = local_cells // SHARED
    shared_rows = SHARED // devices_mode
    join_width = local_cells // (shared_rows * KEPT)
    results = []
    for pair_number in range(2):
        left_part = states[2 * pair_number].reshape(2, local_rows, SHARED)
        right_part = states[2 * pair_number + 1].reshape(2, shared_rows, KEPT, join_width)
        device_index = lax.axis_index("mode")
        total_bits = devices_mode.bit_length() - 1
        group_bits = total_bits - 4
        batch_bits = KEPT.bit_length() - 1
        groups = devices_mode // (4 * KEPT)
        span = 2 * shared_rows
        outer = SHARED // (span * groups)
        half_join = join_width // 2

        def left_trader(piece, bit_number):
            return partner(piece, "mode", bit_number)

        def right_trader(piece, bit_number):
            return partner(piece, "mode", bit_number)

        left_buffer = left_part.reshape(2, local_rows, outer, groups, span).transpose(3, 0, 1, 2, 4)
        left_buffer = left_buffer.reshape((2,) * group_bits + (1, 2, local_rows, outer, span))
        left_buffer = jnp.broadcast_to(
            left_buffer, (2,) * group_bits + (2, 2, local_rows, outer, span)
        )
        left_bits = [group_bits - position for position in range(group_bits)] + [0]
        left_buffer = trade_axes(left_buffer, left_bits, left_trader, device_index)
        left_block = left_buffer.reshape(devices_mode // (2 * KEPT), 2, local_rows, outer * span)
        left_block = left_block.transpose(1, 0, 2, 3).reshape(2, half_join, SHARED // groups)
        right_buffer = right_part.reshape(2, shared_rows, KEPT, 2, half_join).transpose(
            2, 3, 0, 1, 4
        )
        right_buffer = right_buffer.reshape((2,) * batch_bits + (1, 2, 2, shared_rows, half_join))
        right_buffer = jnp.broadcast_to(
            right_buffer, (2,) * batch_bits + (2, 2, 2, shared_rows, half_join)
        )
        right_bits = [total_bits - 1 - position for position in range(batch_bits)] + [
            total_bits - batch_bits - 1,
            0,
        ]
        right_buffer = trade_axes(right_buffer, right_bits, right_trader, device_index)
        right_block = right_buffer.reshape(2 * KEPT, 2, 2, shared_rows, half_join)
        right_block = right_block.transpose(2, 0, 1, 3, 4).reshape(2, SHARED // groups, half_join)
        running = complex_rows(left_block[0], left_block[1], right_block[0], right_block[1])
        for position in range(group_bits):
            bit_number = group_bits - position
            own_bit = read_bit(device_index, bit_number)
            row_count = running.shape[0]
            halves = running.reshape(2, row_count // 2, 2, half_join)
            kept_half = lax.dynamic_index_in_dim(halves, own_bit, 0, keepdims=False)
            sent_half = lax.dynamic_index_in_dim(halves, 1 - own_bit, 0, keepdims=False)
            running = kept_half + partner(
                sent_half.astype(jnp.bfloat16), "mode", bit_number
            ).astype(sent_half.dtype)
        rounded = (running * join_scale).astype(jnp.bfloat16)
        own_bit = read_bit(device_index, 0)
        halves = rounded.reshape(2, local_rows, 2, half_join)
        kept_half = lax.dynamic_index_in_dim(halves, own_bit, 0, keepdims=False)
        sent_half = lax.dynamic_index_in_dim(halves, 1 - own_bit, 0, keepdims=False)
        received = partner(sent_half, "mode", 0)
        first_half = jnp.where(own_bit == 0, kept_half, received)
        second_half = jnp.where(own_bit == 0, received, kept_half)
        finished = jnp.concatenate([first_half, second_half], axis=2)
        results.append(finished)
    return jnp.stack(results)


def local(branch_in, column_order, gate_a, gate_b):
    branches, _, rows_each, width = branch_in.shape
    if branches == 4 and tiles_fit(lax.axis_size("mode"), rows_each, width):
        return fast(branch_in, column_order, gate_a, gate_b)
    return general(branch_in, column_order, gate_a, gate_b)


def solution(mesh):
    in_specs = (
        P(None, None, ("cuts", "mode"), None),
        P(),
        P(None, "mode", None),
        P(None, "mode", None),
    )
    out_specs = P(None, ("cuts", "mode"), None, None)
    return jax.shard_map(local, mesh=mesh, in_specs=in_specs, out_specs=out_specs, check_vma=False)
```

```python
import functools

import jax
import jax.numpy as jnp
from jax import lax
from jax.experimental import pallas as pl
from jax.experimental.pallas import tpu as pltpu
from jax.sharding import PartitionSpec as P

SHARED = 4096
KEPT = 4
CYCLES = 2
LANES = 128
MEBI = 1024 * 1024


def whole(count):
    return [pl.BlockSpec(memory_space=pltpu.VMEM)] * count


def one_hot(shape, axis, wanted):
    return (lax.broadcasted_iota(jnp.int32, shape, axis) == wanted).astype(jnp.bfloat16)


def exact_dot(left, right):
    return jnp.dot(left, right, preferred_element_type=jnp.float32)


def pack_kernel(qs, x_ref, order_ref, o_ref, ordered):
    _, parts, rows_each, width = x_ref.shape
    rows = parts * rows_each
    step = min(256, width)
    new = lax.broadcasted_iota(jnp.int32, (2 * rows, 2 * rows), 0)
    e, side = new // (2 * parts * qs), new // (parts * qs) % 2
    k, q = new // qs % parts, new % qs
    pack = one_hot((2 * rows, 2 * rows), 1, side * rows + k * rows_each + e * qs + q)
    for pair in range(x_ref.shape[0] // 2):
        for side in range(2):
            branch = 2 * pair + side
            values = x_ref[branch].reshape(rows, width)
            for start in range(0, width, step):
                picks = one_hot((width, step), 0, order_ref[branch : branch + 1, start : start + step])
                found = exact_dot(values, picks).astype(jnp.bfloat16)
                ordered[side * rows : (side + 1) * rows, start : start + step] = found
        packed = exact_dot(pack, ordered[...]).astype(jnp.bfloat16)
        o_ref[2 * pair * rows : 2 * (pair + 1) * rows, :] = packed


def swap_sign(tiles, qs):
    turned = pltpu.roll(tiles, qs, 1)
    row = lax.broadcasted_iota(jnp.int32, tiles.shape, 1)
    return jnp.where(row < qs, -turned, turned)


def regroup_store(acc, first_lane, group, devices, tile_rows, x_ref):
    width = x_ref.shape[1] // 2
    per = LANES // group
    lane = lax.broadcasted_iota(jnp.int32, (tile_rows, LANES), 1) // group
    for offset in range(0, acc.shape[1], LANES):
        tile = acc[:, offset : offset + LANES].reshape(devices, tile_rows, LANES)
        row_start = (first_lane + offset) // group * tile_rows
        for block in range(devices // per):
            parts = [tile[block * per + m] for m in range(per)]
            bit = 1
            while bit < per:
                moved = list(parts)
                keep = (lane // bit) % 2 == 0
                for m in range(per):
                    if m & bit:
                        continue
                    low, high = parts[m], parts[m | bit]
                    moved[m] = jnp.where(keep, low, pltpu.roll(high, bit * group, 1))
                    moved[m | bit] = jnp.where(keep, pltpu.roll(low, LANES - bit * group, 1), high)
                parts = moved
                bit *= 2
            tiles = jnp.stack(parts)
            rows = pl.ds(row_start, per * tile_rows)
            lanes = pl.ds(block * LANES, LANES)
            x_ref[rows, lanes] = tiles.reshape(per * tile_rows, LANES).astype(jnp.bfloat16)
            turned = swap_sign(tiles, tile_rows // 2)
            x_ref[rows, pl.ds(width + block * LANES, LANES)] = turned.reshape(per * tile_rows, LANES).astype(jnp.bfloat16)


def gate_copies(plan, blocks, whole_ref, sems):
    me = lax.axis_index("mode")
    copies = ([], [])
    for (sources, gates), block in zip(plan, blocks):
        for place, source in enumerate(sources):
            device = me
            for bit in source:
                device = device + (1 - 2 * (me // 2**bit % 2)) * 2**bit
            size = block.shape[3]
            rows = pl.ds(pl.multiple_of(device * size, size), size)
            for position, gate in enumerate(gates):
                sem = sems.at[gate, len(copies[gate])]
                copies[gate].append(
                    pltpu.make_async_copy(block.at[position, place], whole_ref.at[gate, :, rows, :], sem)
                )
    return copies


def layers_kernel(sizes, is_left, plan, x_ref, *refs):
    devices, qs, group, rows_each = sizes
    blocks, (o_ref, xs, last, whole_ref, sems) = refs[: len(plan)], refs[len(plan) :]
    copies = gate_copies(plan, blocks, whole_ref, sems)
    for gate in range(2):
        for copy in copies[gate]:
            copy.start()
    tile_rows = 2 * qs
    rows, width = x_ref.shape[0] // 2, x_ref.shape[1]
    first = x_ref[...].astype(jnp.float32).reshape(devices, 2 * tile_rows, width)
    first = first[:, :tile_rows] if is_left else first[:, tile_rows:]
    xs[0, :, :width] = first.reshape(rows, width).astype(jnp.bfloat16)
    xs[0, :, width:] = swap_sign(first, qs).reshape(rows, width).astype(jnp.bfloat16)
    step = min(512, width)
    for layer in range(2 * CYCLES):
        if layer < 2:
            for copy in copies[layer]:
                copy.wait()
        gate = whole_ref.at[layer % 2]
        here, later = xs.at[layer % 2], xs.at[(layer + 1) % 2]
        for start in range(0, width, step):
            cols = slice(start, start + step)
            acc = exact_dot(here[...], gate[:, :, cols].reshape(2 * width, step))
            if layer < 2 * CYCLES - 1:
                regroup_store(acc, start, group, devices, tile_rows, later)
            else:
                last[:, cols] = acc.astype(jnp.bfloat16)
    half = rows // 2
    new = lax.broadcasted_iota(jnp.int32, (rows, rows), 0)
    part, inner = new // half, new % half
    if is_left:
        v, r = inner // devices, inner % devices
        picks = one_hot((rows, rows), 1, r * tile_rows + part * qs + v)
        moved = exact_dot(picks, last[...]).astype(jnp.bfloat16)
        span = 2 * rows_each
        each = width * qs // rows_each
        words = width // span
        step = min(256, width)
        for start in range(0, width, step):
            place = start + lax.broadcasted_iota(jnp.int32, (width, step), 1)
            e, rest = place // each, place % each
            h, w, qr = rest // (words * qs), rest % (words * qs) // qs, rest % qs
            lanes = one_hot((width, step), 0, w * span + (e * qs + qr) * 2 + h)
            sent = exact_dot(moved, lanes)
            low_lane = lax.broadcasted_iota(jnp.int32, (half, LANES), 1) < LANES // 2
            for offset in range(0, step, LANES):
                real = sent[:half, offset : offset + LANES]
                imag = sent[half:, offset : offset + LANES]
                e0 = (start + offset) // each
                even = jnp.where(low_lane, real, pltpu.roll(imag, LANES // 2, 1))
                odd = jnp.where(low_lane, pltpu.roll(real, LANES // 2, 1), imag)
                o_ref[e0 * half : (e0 + 1) * half, :] = even.astype(jnp.bfloat16)
                o_ref[(e0 + 1) * half : (e0 + 2) * half, :] = odd.astype(jnp.bfloat16)
    else:
        r, q = inner // qs, inner % qs
        picks = one_hot((rows, rows), 1, r * tile_rows + part * qs + q)
        o_ref[...] = exact_dot(picks, last[...]).astype(jnp.bfloat16)


def join_kernel(sizes, left_ref, right_ref, o_ref):
    devices, us, vs = sizes
    rows = us * devices
    free = right_ref.shape[1] // (2 * KEPT)
    left = left_ref[...].reshape(us, vs, devices, LANES)
    left = jnp.concatenate([left[:, v].reshape(rows, LANES) for v in range(vs)], axis=1)
    new = lax.broadcasted_iota(jnp.int32, (rows, rows), 0)
    picks = one_hot((rows, rows), 1, new % us * devices + new // us)
    left = exact_dot(picks, left).astype(jnp.bfloat16)
    half = right_ref.shape[0] // 2
    depth = half // vs
    real, imag = right_ref[:half, :], right_ref[half:, :]
    block = rows // KEPT
    for g in range(KEPT):
        stack = []
        for v in range(vs):
            r = [real[v * depth : (v + 1) * depth, (h * KEPT + g) * free :][:, :free] for h in range(2)]
            i = [imag[v * depth : (v + 1) * depth, (h * KEPT + g) * free :][:, :free] for h in range(2)]
            to_real = jnp.concatenate([r[0], r[1], -i[0], -i[1]], axis=0)
            to_imag = jnp.concatenate([i[0], i[1], r[0], r[1]], axis=0)
            stack.append(jnp.concatenate([to_real, to_imag], axis=1))
        stack = jnp.concatenate(stack, axis=0)
        part = exact_dot(left[g * block : (g + 1) * block, :], stack)
        o_ref[g * block : (g + 1) * block, :] = part.astype(jnp.bfloat16)


def call(kernel, out_shape, inputs, scratch=(), flops=0, blocks=(), grant=24):
    moved = sum(x.size * x.dtype.itemsize for x in (*inputs, *blocks))
    return pl.pallas_call(
        kernel,
        out_shape=jax.ShapeDtypeStruct(out_shape, jnp.bfloat16),
        in_specs=whole(len(inputs)) + [pl.BlockSpec(memory_space=pl.ANY)] * len(blocks),
        out_specs=whole(1)[0],
        scratch_shapes=list(scratch),
        compiler_params=pltpu.CompilerParams(vmem_limit_bytes=grant * MEBI),
        cost_estimate=pl.CostEstimate(flops=flops, bytes_accessed=moved, transcendentals=0),
    )(*inputs, *blocks)


def tiles_fit(devices, rows_each, width):
    pair_devices = devices // 2
    if devices < 4 or devices & (devices - 1) or rows_each % pair_devices or width % 256:
        return False
    qs, group = rows_each // pair_devices, width // devices
    return (
        2 * qs == 8
        and LANES % group == 0
        and devices % (LANES // group) == 0
        and qs == SHARED // width
        and devices % 32 == 0
        and 2 * width * qs // rows_each == LANES
        and devices * rows_each * width // SHARED % (KEPT * LANES) == 0
        and 2 * (devices * rows_each * width // SHARED) == width
    )


def fast(branch_in, column_order, gate_a, gate_b):
    devices = lax.axis_size("mode")
    rows_each, width = branch_in.shape[2:]
    halves = devices // 2
    qs, group = rows_each // halves, width // devices
    tile_rows = 2 * qs
    rows = devices * tile_rows
    packed = call(
        functools.partial(pack_kernel, qs),
        (2 * rows, width),
        (branch_in, column_order),
        [pltpu.VMEM((4 * rows_each, width), jnp.bfloat16)],
        8 * rows * width * width,
    )
    blocks, plan, states = spread(gate_a, gate_b, packed.reshape(devices, 2 * tile_rows, width))
    states = states.reshape(2 * rows, width)
    sizes = (devices, qs, group, rows_each)
    scratch = [
        pltpu.VMEM((2, rows, 2 * width), jnp.bfloat16),
        pltpu.VMEM((rows, width), jnp.bfloat16),
        pltpu.VMEM((2, 2, width, width), jnp.bfloat16),
        pltpu.SemaphoreType.DMA((2, devices)),
    ]
    work = 2 * CYCLES * 4 * rows * width * width
    left = call(
        functools.partial(layers_kernel, sizes, True, plan),
        (halves * rows // 2, LANES),
        (states,),
        scratch,
        work,
        blocks,
        56,
    )
    groups = [[h * halves + e for e in range(halves)] for h in range(2)]
    left = trade(left.reshape(halves, rows // 2, LANES), groups)
    right = call(
        functools.partial(layers_kernel, sizes, False, plan), (rows, width), (states,), scratch, work, blocks, 56
    )
    free = width // (2 * KEPT)
    us = halves
    partial_sums = call(
        functools.partial(join_kernel, (devices, us, qs)),
        (devices * us, 2 * free),
        (left.reshape(halves * rows // 2, LANES), right),
        flops=2 * devices * us * LANES * qs * 2 * free,
    )
    parts = trade(partial_sums.reshape(devices, us, 2 * free))
    parts = parts.reshape(2, halves, us, 2 * free).astype(jnp.float32)
    join_scale = (2.0 * SHARED) ** (-0.5)
    return (jnp.sum(parts, axis=1) * join_scale).astype(jnp.bfloat16).reshape(2, us, 2, free)


def flip(value, *bits):
    mask = sum(2**bit for bit in bits)
    pairs = [(source, source ^ mask) for source in range(lax.axis_size("mode"))]
    return lax.ppermute(value, "mode", pairs)


def plane(value, sources, early):
    over_x, over_y, *_ = lax.optimization_barrier((flip(value, 1), flip(value, 2), *early))
    diagonal = flip(over_x[:1], 2), flip(over_y[1:], 1)
    turned = [tuple(source + more for source in sources) for more in ((1,), (2,), (1, 2))]
    return [
        (value, sources, (0, 1)),
        (over_x, turned[0], (0, 1)),
        (over_y, turned[1], (0, 1)),
        (diagonal[0], turned[2], (0,)),
        (diagonal[1], turned[2], (1,)),
    ]


def spread(gate_a, gate_b, packed):
    bits = lax.axis_size("mode").bit_length() - 1
    own = jnp.stack([gate_a, gate_b])[:, None]
    far = [()]
    for bit in range(3, bits):
        far += [source + (bit,) for source in far]
    far = sorted(far[1:], key=len)
    came = [flip(own, *source) for source in far]
    sets = [(own, ((),))]
    for start in range(0, len(far), 2):
        value = jnp.concatenate(came[start : start + 2], axis=1)
        sets.append((value, tuple(far[start : start + 2])))
    blocks = []
    for number, (value, sources) in enumerate(sets):
        if number == 1:
            value, packed, *_ = lax.optimization_barrier((value, packed, blocks[-2][0], blocks[-1][0]))
        elif number:
            value, *_ = lax.optimization_barrier((value, blocks[-2][0], blocks[-1][0]))
        early = [later for later, _ in sets[2:]] if number == 1 else []
        blocks += plane(value, sources, early)
    packed, *_ = lax.optimization_barrier((packed, *[value for value, _ in sets[1:]]))
    last = [len(blocks) - 2, len(blocks) - 1]
    near = {}
    for number in [number for number in range(len(blocks)) if number not in last] + last:
        value, sources, gates = blocks[number]
        if number in last:
            value, *_ = lax.optimization_barrier((value, *[near[n][0] for n in near if n not in last]))
        near[number] = (flip(value, 0), tuple(source + (0,) for source in sources), gates)
    blocks += near.values()
    plan = tuple((sources, gates) for _, sources, gates in blocks)
    return [value for value, _, _ in blocks], plan, trade(packed)


def trade(value, groups=None):
    return lax.all_to_all(value, "mode", split_axis=0, concat_axis=0, axis_index_groups=groups, tiled=True)


def partner(value, axis, bit):
    mask = 2**bit
    pairs = [(source, source ^ mask) for source in range(lax.axis_size(axis))]
    return lax.ppermute(value, axis, pairs)


def product_four(states, layer_block):
    branches, parts, row_count, width = states.shape
    real_in = states[:, 0].reshape(branches * row_count, width)
    imag_in = states[:, 1].reshape(branches * row_count, width)
    real_part = jnp.dot(real_in, layer_block[0], preferred_element_type=jnp.float32) - jnp.dot(
        imag_in, layer_block[1], preferred_element_type=jnp.float32
    )
    imag_part = jnp.dot(real_in, layer_block[1], preferred_element_type=jnp.float32) + jnp.dot(
        imag_in, layer_block[0], preferred_element_type=jnp.float32
    )
    joined_parts = jnp.stack(
        [
            real_part.reshape(branches, row_count, width),
            imag_part.reshape(branches, row_count, width),
        ],
        axis=1,
    )
    return joined_parts.astype(jnp.bfloat16)


def complex_rows(left_real, left_imag, right_real, right_imag):
    real_part = jnp.dot(left_real, right_real, preferred_element_type=jnp.float32) - jnp.dot(
        left_imag, right_imag, preferred_element_type=jnp.float32
    )
    imag_part = jnp.dot(left_real, right_imag, preferred_element_type=jnp.float32) + jnp.dot(
        left_imag, right_real, preferred_element_type=jnp.float32
    )
    return jnp.stack([real_part, imag_part], axis=1)


def read_bit(device_index, bit_number):
    return device_index // 2**bit_number % 2


def trade_axes(buffer, axis_bits, trader, device_index):
    for position, bit_number in enumerate(axis_bits):
        own_bit = read_bit(device_index, bit_number)
        kept_half = lax.dynamic_index_in_dim(buffer, own_bit, position, keepdims=False)
        sent_half = lax.dynamic_index_in_dim(buffer, 1 - own_bit, position, keepdims=False)
        received = trader(sent_half, bit_number)
        first_half = jnp.where(own_bit == 0, kept_half, received)
        second_half = jnp.where(own_bit == 0, received, kept_half)
        buffer = jnp.stack([first_half, second_half], axis=position)
    return buffer


def general(branch_in, column_order, gate_a, gate_b):
    join_scale = (2.0 * SHARED) ** (-0.5)
    devices_mode = lax.axis_size("mode")
    whole_a, whole_b = (
        lax.all_gather(gate_a, "mode", axis=1, tiled=True),
        lax.all_gather(gate_b, "mode", axis=1, tiled=True),
    )
    states = jnp.take_along_axis(branch_in, column_order[:, None, None, :], axis=3)
    for layer_number in range(2 * CYCLES):
        if layer_number > 0:
            states = lax.all_to_all(states, "mode", split_axis=3, concat_axis=3, tiled=True)
        states = product_four(states, whole_a if layer_number % 2 == 0 else whole_b)
    local_cells = states.shape[2] * states.shape[3]
    local_rows = local_cells // SHARED
    shared_rows = SHARED // devices_mode
    join_width = local_cells // (shared_rows * KEPT)
    results = []
    for pair_number in range(2):
        left_part = states[2 * pair_number].reshape(2, local_rows, SHARED)
        right_part = states[2 * pair_number + 1].reshape(2, shared_rows, KEPT, join_width)
        device_index = lax.axis_index("mode")
        total_bits = devices_mode.bit_length() - 1
        group_bits = total_bits - 4
        batch_bits = KEPT.bit_length() - 1
        groups = devices_mode // (4 * KEPT)
        span = 2 * shared_rows
        outer = SHARED // (span * groups)
        half_join = join_width // 2

        def left_trader(piece, bit_number):
            return partner(piece, "mode", bit_number)

        def right_trader(piece, bit_number):
            return partner(piece, "mode", bit_number)

        left_buffer = left_part.reshape(2, local_rows, outer, groups, span).transpose(3, 0, 1, 2, 4)
        left_buffer = left_buffer.reshape((2,) * group_bits + (1, 2, local_rows, outer, span))
        left_buffer = jnp.broadcast_to(
            left_buffer, (2,) * group_bits + (2, 2, local_rows, outer, span)
        )
        left_bits = [group_bits - position for position in range(group_bits)] + [0]
        left_buffer = trade_axes(left_buffer, left_bits, left_trader, device_index)
        left_block = left_buffer.reshape(devices_mode // (2 * KEPT), 2, local_rows, outer * span)
        left_block = left_block.transpose(1, 0, 2, 3).reshape(2, half_join, SHARED // groups)
        right_buffer = right_part.reshape(2, shared_rows, KEPT, 2, half_join).transpose(
            2, 3, 0, 1, 4
        )
        right_buffer = right_buffer.reshape((2,) * batch_bits + (1, 2, 2, shared_rows, half_join))
        right_buffer = jnp.broadcast_to(
            right_buffer, (2,) * batch_bits + (2, 2, 2, shared_rows, half_join)
        )
        right_bits = [total_bits - 1 - position for position in range(batch_bits)] + [
            total_bits - batch_bits - 1,
            0,
        ]
        right_buffer = trade_axes(right_buffer, right_bits, right_trader, device_index)
        right_block = right_buffer.reshape(2 * KEPT, 2, 2, shared_rows, half_join)
        right_block = right_block.transpose(2, 0, 1, 3, 4).reshape(2, SHARED // groups, half_join)
        running = complex_rows(left_block[0], left_block[1], right_block[0], right_block[1])
        for position in range(group_bits):
            bit_number = group_bits - position
            own_bit = read_bit(device_index, bit_number)
            row_count = running.shape[0]
            halves = running.reshape(2, row_count // 2, 2, half_join)
            kept_half = lax.dynamic_index_in_dim(halves, own_bit, 0, keepdims=False)
            sent_half = lax.dynamic_index_in_dim(halves, 1 - own_bit, 0, keepdims=False)
            running = kept_half + partner(
                sent_half.astype(jnp.bfloat16), "mode", bit_number
            ).astype(sent_half.dtype)
        rounded = (running * join_scale).astype(jnp.bfloat16)
        own_bit = read_bit(device_index, 0)
        halves = rounded.reshape(2, local_rows, 2, half_join)
        kept_half = lax.dynamic_index_in_dim(halves, own_bit, 0, keepdims=False)
        sent_half = lax.dynamic_index_in_dim(halves, 1 - own_bit, 0, keepdims=False)
        received = partner(sent_half, "mode", 0)
        first_half = jnp.where(own_bit == 0, kept_half, received)
        second_half = jnp.where(own_bit == 0, received, kept_half)
        finished = jnp.concatenate([first_half, second_half], axis=2)
        results.append(finished)
    return jnp.stack(results)


def local(branch_in, column_order, gate_a, gate_b):
    branches, _, rows_each, width = branch_in.shape
    if branches == 4 and tiles_fit(lax.axis_size("mode"), rows_each, width):
        return fast(branch_in, column_order, gate_a, gate_b)
    return general(branch_in, column_order, gate_a, gate_b)


def solution(mesh):
    in_specs = (
        P(None, None, ("cuts", "mode"), None),
        P(),
        P(None, "mode", None),
        P(None, "mode", None),
    )
    out_specs = P(None, ("cuts", "mode"), None, None)
    return jax.shard_map(local, mesh=mesh, in_specs=in_specs, out_specs=out_specs, check_vma=False)
```

```python
import functools

import jax
import jax.numpy as jnp
from jax import lax
from jax.experimental import pallas as pl
from jax.experimental.pallas import tpu as pltpu
from jax.sharding import PartitionSpec as P

SHARED = 4096
KEPT = 4
CYCLES = 2
LANES = 128
MEBI = 1024 * 1024


def whole(count):
    return [pl.BlockSpec(memory_space=pltpu.VMEM)] * count


def one_hot(shape, axis, wanted):
    return (lax.broadcasted_iota(jnp.int32, shape, axis) == wanted).astype(jnp.bfloat16)


def exact_dot(left, right):
    return jnp.dot(left, right, preferred_element_type=jnp.float32)


def pack_kernel(qs, x_ref, order_ref, o_ref, ordered):
    _, parts, rows_each, width = x_ref.shape
    rows = parts * rows_each
    step = min(256, width)
    new = lax.broadcasted_iota(jnp.int32, (2 * rows, 2 * rows), 0)
    e, side = new // (2 * parts * qs), new // (parts * qs) % 2
    k, q = new // qs % parts, new % qs
    pack = one_hot((2 * rows, 2 * rows), 1, side * rows + k * rows_each + e * qs + q)
    for pair in range(x_ref.shape[0] // 2):
        for side in range(2):
            branch = 2 * pair + side
            values = x_ref[branch].reshape(rows, width)
            for start in range(0, width, step):
                picks = one_hot((width, step), 0, order_ref[branch : branch + 1, start : start + step])
                found = exact_dot(values, picks).astype(jnp.bfloat16)
                ordered[side * rows : (side + 1) * rows, start : start + step] = found
        packed = exact_dot(pack, ordered[...]).astype(jnp.bfloat16)
        o_ref[2 * pair * rows : 2 * (pair + 1) * rows, :] = packed


def swap_sign(tiles, qs):
    turned = pltpu.roll(tiles, qs, 1)
    row = lax.broadcasted_iota(jnp.int32, (1,) + tiles.shape[1:], 1)
    return turned * jnp.where(row < qs, -1.0, 1.0)


def regroup_store(acc, first_lane, group, devices, tile_rows, x_ref):
    width = x_ref.shape[1] // 2
    per = LANES // group
    lane = lax.broadcasted_iota(jnp.int32, (tile_rows, LANES), 1) // group
    for offset in range(0, acc.shape[1], LANES):
        tile = acc[:, offset : offset + LANES].reshape(devices, tile_rows, LANES)
        row_start = (first_lane + offset) // group * tile_rows
        for block in range(devices // per):
            parts = [tile[block * per + m] for m in range(per)]
            bit = 1
            while bit < per:
                moved = list(parts)
                keep = (lane // bit) % 2 == 0
                for m in range(per):
                    if m & bit:
                        continue
                    low, high = parts[m], parts[m | bit]
                    if 2 * bit * group == LANES:
                        up = down = pltpu.roll(jnp.where(keep, high, low), LANES // 2, 1)
                    else:
                        up, down = pltpu.roll(high, bit * group, 1), pltpu.roll(low, LANES - bit * group, 1)
                    moved[m] = jnp.where(keep, low, up)
                    moved[m | bit] = jnp.where(keep, down, high)
                parts = moved
                bit *= 2
            tiles = jnp.stack(parts)
            rows = pl.ds(row_start, per * tile_rows)
            lanes = pl.ds(block * LANES, LANES)
            x_ref[rows, lanes] = tiles.reshape(per * tile_rows, LANES).astype(jnp.bfloat16)
            turned = swap_sign(tiles, tile_rows // 2)
            x_ref[rows, pl.ds(width + block * LANES, LANES)] = turned.reshape(per * tile_rows, LANES).astype(jnp.bfloat16)


def gate_copies(plan, blocks, whole_ref, sems):
    me = lax.axis_index("mode")
    copies = ([], [])
    for (sources, gates), block in zip(plan, blocks):
        for place, source in enumerate(sources):
            device = me
            for bit in source:
                device = device + (1 - 2 * (me // 2**bit % 2)) * 2**bit
            size = block.shape[3]
            rows = pl.ds(pl.multiple_of(device * size, size), size)
            for position, gate in enumerate(gates):
                sem = sems.at[gate, len(copies[gate])]
                copies[gate].append(
                    pltpu.make_async_copy(block.at[position, place], whole_ref.at[gate, :, rows, :], sem)
                )
    return copies


def layers_kernel(sizes, is_left, plan, x_ref, *refs):
    devices, qs, group, rows_each = sizes
    blocks, (o_ref, xs, last, whole_ref, sems) = refs[: len(plan)], refs[len(plan) :]
    copies = gate_copies(plan, blocks, whole_ref, sems)
    for gate in range(2):
        for copy in copies[gate]:
            copy.start()
    tile_rows = 2 * qs
    rows, width = x_ref.shape[0] // 2, x_ref.shape[1]
    first = x_ref[...].astype(jnp.float32).reshape(devices, 2 * tile_rows, width)
    first = first[:, :tile_rows] if is_left else first[:, tile_rows:]
    xs[0, :, :width] = first.reshape(rows, width).astype(jnp.bfloat16)
    xs[0, :, width:] = swap_sign(first, qs).reshape(rows, width).astype(jnp.bfloat16)
    step = min(512, width)
    for layer in range(2 * CYCLES):
        if layer < 2:
            for copy in copies[layer]:
                copy.wait()
        gate = whole_ref.at[layer % 2]
        here, later = xs.at[layer % 2], xs.at[(layer + 1) % 2]
        for start in range(0, width, step):
            cols = slice(start, start + step)
            acc = exact_dot(here[...], gate[:, :, cols].reshape(2 * width, step))
            if layer < 2 * CYCLES - 1:
                regroup_store(acc, start, group, devices, tile_rows, later)
            else:
                last[:, cols] = acc.astype(jnp.bfloat16)
    half = rows // 2
    new = lax.broadcasted_iota(jnp.int32, (rows, rows), 0)
    part, inner = new // half, new % half
    if is_left:
        v, r = inner // devices, inner % devices
        picks = one_hot((rows, rows), 1, r * tile_rows + part * qs + v)
        moved = exact_dot(picks, last[...]).astype(jnp.bfloat16)
        span = 2 * rows_each
        each = width * qs // rows_each
        words = width // span
        step = min(256, width)
        for start in range(0, width, step):
            place = start + lax.broadcasted_iota(jnp.int32, (width, step), 1)
            e, rest = place // each, place % each
            h, w, qr = rest // (words * qs), rest % (words * qs) // qs, rest % qs
            lanes = one_hot((width, step), 0, w * span + (e * qs + qr) * 2 + h)
            sent = exact_dot(moved, lanes)
            low_lane = lax.broadcasted_iota(jnp.int32, (half, LANES), 1) < LANES // 2
            for offset in range(0, step, LANES):
                real = sent[:half, offset : offset + LANES]
                imag = sent[half:, offset : offset + LANES]
                e0 = (start + offset) // each
                even = jnp.where(low_lane, real, pltpu.roll(imag, LANES // 2, 1))
                odd = jnp.where(low_lane, pltpu.roll(real, LANES // 2, 1), imag)
                o_ref[e0 * half : (e0 + 1) * half, :] = even.astype(jnp.bfloat16)
                o_ref[(e0 + 1) * half : (e0 + 2) * half, :] = odd.astype(jnp.bfloat16)
    else:
        r, q = inner // qs, inner % qs
        picks = one_hot((rows, rows), 1, r * tile_rows + part * qs + q)
        o_ref[...] = exact_dot(picks, last[...]).astype(jnp.bfloat16)


def join_kernel(sizes, left_ref, right_ref, o_ref):
    devices, us, vs = sizes
    rows = us * devices
    free = right_ref.shape[1] // (2 * KEPT)
    left = left_ref[...].reshape(us, vs, devices, LANES)
    left = jnp.concatenate([left[:, v].reshape(rows, LANES) for v in range(vs)], axis=1)
    new = lax.broadcasted_iota(jnp.int32, (rows, rows), 0)
    picks = one_hot((rows, rows), 1, new % us * devices + new // us)
    left = exact_dot(picks, left).astype(jnp.bfloat16)
    half = right_ref.shape[0] // 2
    depth = half // vs
    real, imag = right_ref[:half, :], right_ref[half:, :]
    block = rows // KEPT
    for g in range(KEPT):
        stack = []
        for v in range(vs):
            r = [real[v * depth : (v + 1) * depth, (h * KEPT + g) * free :][:, :free] for h in range(2)]
            i = [imag[v * depth : (v + 1) * depth, (h * KEPT + g) * free :][:, :free] for h in range(2)]
            to_real = jnp.concatenate([r[0], r[1], -i[0], -i[1]], axis=0)
            to_imag = jnp.concatenate([i[0], i[1], r[0], r[1]], axis=0)
            stack.append(jnp.concatenate([to_real, to_imag], axis=1))
        stack = jnp.concatenate(stack, axis=0)
        part = exact_dot(left[g * block : (g + 1) * block, :], stack)
        o_ref[g * block : (g + 1) * block, :] = part.astype(jnp.bfloat16)


def call(kernel, out_shape, inputs, scratch=(), flops=0, blocks=(), grant=24):
    moved = sum(x.size * x.dtype.itemsize for x in (*inputs, *blocks))
    return pl.pallas_call(
        kernel,
        out_shape=jax.ShapeDtypeStruct(out_shape, jnp.bfloat16),
        in_specs=whole(len(inputs)) + [pl.BlockSpec(memory_space=pl.ANY)] * len(blocks),
        out_specs=whole(1)[0],
        scratch_shapes=list(scratch),
        compiler_params=pltpu.CompilerParams(vmem_limit_bytes=grant * MEBI),
        cost_estimate=pl.CostEstimate(flops=flops, bytes_accessed=moved, transcendentals=0),
    )(*inputs, *blocks)


def tiles_fit(devices, rows_each, width):
    pair_devices = devices // 2
    if devices < 4 or devices & (devices - 1) or rows_each % pair_devices or width % 256:
        return False
    qs, group = rows_each // pair_devices, width // devices
    return (
        2 * qs == 8
        and LANES % group == 0
        and devices % (LANES // group) == 0
        and qs == SHARED // width
        and devices % 32 == 0
        and 2 * width * qs // rows_each == LANES
        and devices * rows_each * width // SHARED % (KEPT * LANES) == 0
        and 2 * (devices * rows_each * width // SHARED) == width
    )


def fast(branch_in, column_order, gate_a, gate_b):
    devices = lax.axis_size("mode")
    rows_each, width = branch_in.shape[2:]
    halves = devices // 2
    qs, group = rows_each // halves, width // devices
    tile_rows = 2 * qs
    rows = devices * tile_rows
    packed = call(
        functools.partial(pack_kernel, qs),
        (2 * rows, width),
        (branch_in, column_order),
        [pltpu.VMEM((4 * rows_each, width), jnp.bfloat16)],
        8 * rows * width * width,
    )
    blocks, plan, states = spread(gate_a, gate_b, packed.reshape(devices, 2 * tile_rows, width))
    states = states.reshape(2 * rows, width)
    sizes = (devices, qs, group, rows_each)
    scratch = [
        pltpu.VMEM((2, rows, 2 * width), jnp.bfloat16),
        pltpu.VMEM((rows, width), jnp.bfloat16),
        pltpu.VMEM((2, 2, width, width), jnp.bfloat16),
        pltpu.SemaphoreType.DMA((2, devices)),
    ]
    work = 2 * CYCLES * 4 * rows * width * width
    left = call(
        functools.partial(layers_kernel, sizes, True, plan),
        (halves * rows // 2, LANES),
        (states,),
        scratch,
        work,
        blocks,
        56,
    )
    groups = [[h * halves + e for e in range(halves)] for h in range(2)]
    left = trade(left.reshape(halves, rows // 2, LANES), groups)
    right = call(
        functools.partial(layers_kernel, sizes, False, plan), (rows, width), (states,), scratch, work, blocks, 56
    )
    free = width // (2 * KEPT)
    us = halves
    partial_sums = call(
        functools.partial(join_kernel, (devices, us, qs)),
        (devices * us, 2 * free),
        (left.reshape(halves * rows // 2, LANES), right),
        flops=2 * devices * us * LANES * qs * 2 * free,
    )
    parts = trade(partial_sums.reshape(devices, us, 2 * free))
    parts = parts.reshape(2, halves, us, 2 * free).astype(jnp.float32)
    join_scale = (2.0 * SHARED) ** (-0.5)
    return (jnp.sum(parts, axis=1) * join_scale).astype(jnp.bfloat16).reshape(2, us, 2, free)


def flip(value, *bits):
    mask = sum(2**bit for bit in bits)
    pairs = [(source, source ^ mask) for source in range(lax.axis_size("mode"))]
    return lax.ppermute(value, "mode", pairs)


def plane(value, sources):
    over_x, over_y = flip(value, 1), flip(value, 2)
    diagonal = flip(over_x[:1], 2), flip(over_y[1:], 1)
    turned = [tuple(source + more for source in sources) for more in ((1,), (2,), (1, 2))]
    return [
        (value, sources, (0, 1)),
        (over_x, turned[0], (0, 1)),
        (over_y, turned[1], (0, 1)),
        (diagonal[0], turned[2], (0,)),
        (diagonal[1], turned[2], (1,)),
    ]


def spread(gate_a, gate_b, packed):
    bits = lax.axis_size("mode").bit_length() - 1
    own = jnp.stack([gate_a, gate_b])[:, None]
    blocks = plane(own, ((),))
    far = [()]
    for bit in range(3, bits):
        far += [source + (bit,) for source in far]
    far = tuple(far[1:])
    value = jnp.concatenate([flip(own, *source) for source in far], axis=1)
    states = trade(packed)
    value, *_ = lax.optimization_barrier((value, packed, blocks[-2][0], blocks[-1][0]))
    blocks += plane(value, far)
    near = []
    for number, (value, sources, gates) in enumerate(blocks):
        if number >= len(blocks) - 2:
            value, states, *_ = lax.optimization_barrier(
                (value, states, *[earlier for earlier, _, _ in near[: len(blocks) - 2]])
            )
        near.append((flip(value, 0), tuple(source + (0,) for source in sources), gates))
    blocks += near
    plan = tuple((sources, gates) for _, sources, gates in blocks)
    return [value for value, _, _ in blocks], plan, states


def trade(value, groups=None):
    return lax.all_to_all(value, "mode", split_axis=0, concat_axis=0, axis_index_groups=groups, tiled=True)


def partner(value, axis, bit):
    mask = 2**bit
    pairs = [(source, source ^ mask) for source in range(lax.axis_size(axis))]
    return lax.ppermute(value, axis, pairs)


def product_four(states, layer_block):
    branches, parts, row_count, width = states.shape
    real_in = states[:, 0].reshape(branches * row_count, width)
    imag_in = states[:, 1].reshape(branches * row_count, width)
    real_part = jnp.dot(real_in, layer_block[0], preferred_element_type=jnp.float32) - jnp.dot(
        imag_in, layer_block[1], preferred_element_type=jnp.float32
    )
    imag_part = jnp.dot(real_in, layer_block[1], preferred_element_type=jnp.float32) + jnp.dot(
        imag_in, layer_block[0], preferred_element_type=jnp.float32
    )
    joined_parts = jnp.stack(
        [
            real_part.reshape(branches, row_count, width),
            imag_part.reshape(branches, row_count, width),
        ],
        axis=1,
    )
    return joined_parts.astype(jnp.bfloat16)


def complex_rows(left_real, left_imag, right_real, right_imag):
    real_part = jnp.dot(left_real, right_real, preferred_element_type=jnp.float32) - jnp.dot(
        left_imag, right_imag, preferred_element_type=jnp.float32
    )
    imag_part = jnp.dot(left_real, right_imag, preferred_element_type=jnp.float32) + jnp.dot(
        left_imag, right_real, preferred_element_type=jnp.float32
    )
    return jnp.stack([real_part, imag_part], axis=1)


def read_bit(device_index, bit_number):
    return device_index // 2**bit_number % 2


def trade_axes(buffer, axis_bits, trader, device_index):
    for position, bit_number in enumerate(axis_bits):
        own_bit = read_bit(device_index, bit_number)
        kept_half = lax.dynamic_index_in_dim(buffer, own_bit, position, keepdims=False)
        sent_half = lax.dynamic_index_in_dim(buffer, 1 - own_bit, position, keepdims=False)
        received = trader(sent_half, bit_number)
        first_half = jnp.where(own_bit == 0, kept_half, received)
        second_half = jnp.where(own_bit == 0, received, kept_half)
        buffer = jnp.stack([first_half, second_half], axis=position)
    return buffer


def general(branch_in, column_order, gate_a, gate_b):
    join_scale = (2.0 * SHARED) ** (-0.5)
    devices_mode = lax.axis_size("mode")
    whole_a, whole_b = (
        lax.all_gather(gate_a, "mode", axis=1, tiled=True),
        lax.all_gather(gate_b, "mode", axis=1, tiled=True),
    )
    states = jnp.take_along_axis(branch_in, column_order[:, None, None, :], axis=3)
    for layer_number in range(2 * CYCLES):
        if layer_number > 0:
            states = lax.all_to_all(states, "mode", split_axis=3, concat_axis=3, tiled=True)
        states = product_four(states, whole_a if layer_number % 2 == 0 else whole_b)
    local_cells = states.shape[2] * states.shape[3]
    local_rows = local_cells // SHARED
    shared_rows = SHARED // devices_mode
    join_width = local_cells // (shared_rows * KEPT)
    results = []
    for pair_number in range(2):
        left_part = states[2 * pair_number].reshape(2, local_rows, SHARED)
        right_part = states[2 * pair_number + 1].reshape(2, shared_rows, KEPT, join_width)
        device_index = lax.axis_index("mode")
        total_bits = devices_mode.bit_length() - 1
        group_bits = total_bits - 4
        batch_bits = KEPT.bit_length() - 1
        groups = devices_mode // (4 * KEPT)
        span = 2 * shared_rows
        outer = SHARED // (span * groups)
        half_join = join_width // 2

        def left_trader(piece, bit_number):
            return partner(piece, "mode", bit_number)

        def right_trader(piece, bit_number):
            return partner(piece, "mode", bit_number)

        left_buffer = left_part.reshape(2, local_rows, outer, groups, span).transpose(3, 0, 1, 2, 4)
        left_buffer = left_buffer.reshape((2,) * group_bits + (1, 2, local_rows, outer, span))
        left_buffer = jnp.broadcast_to(
            left_buffer, (2,) * group_bits + (2, 2, local_rows, outer, span)
        )
        left_bits = [group_bits - position for position in range(group_bits)] + [0]
        left_buffer = trade_axes(left_buffer, left_bits, left_trader, device_index)
        left_block = left_buffer.reshape(devices_mode // (2 * KEPT), 2, local_rows, outer * span)
        left_block = left_block.transpose(1, 0, 2, 3).reshape(2, half_join, SHARED // groups)
        right_buffer = right_part.reshape(2, shared_rows, KEPT, 2, half_join).transpose(
            2, 3, 0, 1, 4
        )
        right_buffer = right_buffer.reshape((2,) * batch_bits + (1, 2, 2, shared_rows, half_join))
        right_buffer = jnp.broadcast_to(
            right_buffer, (2,) * batch_bits + (2, 2, 2, shared_rows, half_join)
        )
        right_bits = [total_bits - 1 - position for position in range(batch_bits)] + [
            total_bits - batch_bits - 1,
            0,
        ]
        right_buffer = trade_axes(right_buffer, right_bits, right_trader, device_index)
        right_block = right_buffer.reshape(2 * KEPT, 2, 2, shared_rows, half_join)
        right_block = right_block.transpose(2, 0, 1, 3, 4).reshape(2, SHARED // groups, half_join)
        running = complex_rows(left_block[0], left_block[1], right_block[0], right_block[1])
        for position in range(group_bits):
            bit_number = group_bits - position
            own_bit = read_bit(device_index, bit_number)
            row_count = running.shape[0]
            halves = running.reshape(2, row_count // 2, 2, half_join)
            kept_half = lax.dynamic_index_in_dim(halves, own_bit, 0, keepdims=False)
            sent_half = lax.dynamic_index_in_dim(halves, 1 - own_bit, 0, keepdims=False)
            running = kept_half + partner(
                sent_half.astype(jnp.bfloat16), "mode", bit_number
            ).astype(sent_half.dtype)
        rounded = (running * join_scale).astype(jnp.bfloat16)
        own_bit = read_bit(device_index, 0)
        halves = rounded.reshape(2, local_rows, 2, half_join)
        kept_half = lax.dynamic_index_in_dim(halves, own_bit, 0, keepdims=False)
        sent_half = lax.dynamic_index_in_dim(halves, 1 - own_bit, 0, keepdims=False)
        received = partner(sent_half, "mode", 0)
        first_half = jnp.where(own_bit == 0, kept_half, received)
        second_half = jnp.where(own_bit == 0, received, kept_half)
        finished = jnp.concatenate([first_half, second_half], axis=2)
        results.append(finished)
    return jnp.stack(results)


def local(branch_in, column_order, gate_a, gate_b):
    branches, _, rows_each, width = branch_in.shape
    if branches == 4 and tiles_fit(lax.axis_size("mode"), rows_each, width):
        return fast(branch_in, column_order, gate_a, gate_b)
    return general(branch_in, column_order, gate_a, gate_b)


def solution(mesh):
    in_specs = (
        P(None, None, ("cuts", "mode"), None),
        P(),
        P(None, "mode", None),
        P(None, "mode", None),
    )
    out_specs = P(None, ("cuts", "mode"), None, None)
    return jax.shard_map(local, mesh=mesh, in_specs=in_specs, out_specs=out_specs, check_vma=False)
```

```python
import functools

import jax
import jax.numpy as jnp
from jax import lax
from jax.experimental import pallas as pl
from jax.experimental.pallas import tpu as pltpu
from jax.sharding import PartitionSpec as P

SHARED = 4096
KEPT = 4
CYCLES = 2
LANES = 128
MEBI = 1024 * 1024


def whole(count):
    return [pl.BlockSpec(memory_space=pltpu.VMEM)] * count


def one_hot(shape, axis, wanted):
    return (lax.broadcasted_iota(jnp.int32, shape, axis) == wanted).astype(jnp.bfloat16)


def exact_dot(left, right):
    return jnp.dot(left, right, preferred_element_type=jnp.float32)


def pack_kernel(qs, x_ref, order_ref, left_ref, right_ref):
    _, parts, rows_each, width = x_ref.shape
    rows = parts * rows_each
    step = min(256, width)
    new = lax.broadcasted_iota(jnp.int32, (rows, rows), 0)
    e, k, q = new // (parts * qs), new // qs % parts, new % qs
    pack = one_hot((rows, rows), 1, k * rows_each + e * qs + q)
    for branch in range(x_ref.shape[0]):
        o_ref = (left_ref, right_ref)[branch % 2]
        place = branch // 2 * rows
        packed = exact_dot(pack, x_ref[branch].reshape(rows, width)).astype(jnp.bfloat16)
        for start in range(0, width, step):
            picks = one_hot((width, step), 0, order_ref[branch : branch + 1, start : start + step])
            o_ref[place : place + rows, start : start + step] = exact_dot(packed, picks).astype(jnp.bfloat16)


def swap_sign(tiles, qs):
    turned = pltpu.roll(tiles, qs, 1)
    row = lax.broadcasted_iota(jnp.int32, (1,) + tiles.shape[1:], 1)
    return turned * jnp.where(row < qs, -1.0, 1.0)


def regroup_store(acc, first_lane, group, devices, tile_rows, x_ref):
    width = x_ref.shape[1] // 2
    per = LANES // group
    lane = lax.broadcasted_iota(jnp.int32, (tile_rows, LANES), 1) // group
    for offset in range(0, acc.shape[1], LANES):
        tile = acc[:, offset : offset + LANES].reshape(devices, tile_rows, LANES)
        row_start = (first_lane + offset) // group * tile_rows
        for block in range(devices // per):
            parts = [tile[block * per + m] for m in range(per)]
            bit = 1
            while bit < per:
                moved = list(parts)
                keep = (lane // bit) % 2 == 0
                for m in range(per):
                    if m & bit:
                        continue
                    low, high = parts[m], parts[m | bit]
                    if 2 * bit * group == LANES:
                        up = down = pltpu.roll(jnp.where(keep, high, low), LANES // 2, 1)
                    else:
                        up, down = pltpu.roll(high, bit * group, 1), pltpu.roll(low, LANES - bit * group, 1)
                    moved[m] = jnp.where(keep, low, up)
                    moved[m | bit] = jnp.where(keep, down, high)
                parts = moved
                bit *= 2
            tiles = jnp.stack(parts)
            rows = pl.ds(row_start, per * tile_rows)
            lanes = pl.ds(block * LANES, LANES)
            x_ref[rows, lanes] = tiles.reshape(per * tile_rows, LANES).astype(jnp.bfloat16)
            turned = swap_sign(tiles, tile_rows // 2)
            x_ref[rows, pl.ds(width + block * LANES, LANES)] = turned.reshape(per * tile_rows, LANES).astype(jnp.bfloat16)


def gate_copies(plan, blocks, whole_ref, sems):
    me = lax.axis_index("mode")
    copies = ([], [])
    for (sources, gates), block in zip(plan, blocks):
        for place, source in enumerate(sources):
            device = me
            for bit in source:
                device = device + (1 - 2 * (me // 2**bit % 2)) * 2**bit
            size = block.shape[3]
            rows = pl.ds(pl.multiple_of(device * size, size), size)
            for position, gate in enumerate(gates):
                sem = sems.at[gate, len(copies[gate])]
                copies[gate].append(
                    pltpu.make_async_copy(block.at[position, place], whole_ref.at[gate, :, rows, :], sem)
                )
    return copies


def layers_kernel(sizes, is_left, plan, x_ref, *refs):
    devices, qs, group, rows_each = sizes
    blocks, (o_ref, xs, last, whole_ref, sems) = refs[: len(plan)], refs[len(plan) :]
    copies = gate_copies(plan, blocks, whole_ref, sems)
    for gate in range(2):
        for copy in copies[gate]:
            copy.start()
    tile_rows = 2 * qs
    rows, width = x_ref.shape
    first = x_ref[...].astype(jnp.float32).reshape(devices, tile_rows, width)
    xs[0, :, :width] = x_ref[...]
    xs[0, :, width:] = swap_sign(first, qs).reshape(rows, width).astype(jnp.bfloat16)
    step = min(512, width)
    for layer in range(2 * CYCLES):
        if layer < 2:
            for copy in copies[layer]:
                copy.wait()
        gate = whole_ref.at[layer % 2]
        here, later = xs.at[layer % 2], xs.at[(layer + 1) % 2]
        for start in range(0, width, step):
            cols = slice(start, start + step)
            acc = exact_dot(here[...], gate[:, :, cols].reshape(2 * width, step))
            if layer < 2 * CYCLES - 1:
                regroup_store(acc, start, group, devices, tile_rows, later)
            else:
                last[:, cols] = acc.astype(jnp.bfloat16)
    half = rows // 2
    new = lax.broadcasted_iota(jnp.int32, (rows, rows), 0)
    part, inner = new // half, new % half
    if is_left:
        v, r = inner // devices, inner % devices
        picks = one_hot((rows, rows), 1, r * tile_rows + part * qs + v)
        moved = exact_dot(picks, last[...]).astype(jnp.bfloat16)
        span = 2 * rows_each
        each = width * qs // rows_each
        words = width // span
        step = min(256, width)
        for start in range(0, width, step):
            place = start + lax.broadcasted_iota(jnp.int32, (width, step), 1)
            e, rest = place // each, place % each
            h, w, qr = rest // (words * qs), rest % (words * qs) // qs, rest % qs
            lanes = one_hot((width, step), 0, w * span + (e * qs + qr) * 2 + h)
            sent = exact_dot(moved, lanes)
            low_lane = lax.broadcasted_iota(jnp.int32, (half, LANES), 1) < LANES // 2
            for offset in range(0, step, LANES):
                real = sent[:half, offset : offset + LANES]
                imag = sent[half:, offset : offset + LANES]
                e0 = (start + offset) // each
                even = jnp.where(low_lane, real, pltpu.roll(imag, LANES // 2, 1))
                odd = jnp.where(low_lane, pltpu.roll(real, LANES // 2, 1), imag)
                o_ref[e0 * half : (e0 + 1) * half, :] = even.astype(jnp.bfloat16)
                o_ref[(e0 + 1) * half : (e0 + 2) * half, :] = odd.astype(jnp.bfloat16)
    else:
        r, q = inner // qs, inner % qs
        picks = one_hot((rows, rows), 1, r * tile_rows + part * qs + q)
        o_ref[...] = exact_dot(picks, last[...]).astype(jnp.bfloat16)


def join_kernel(sizes, left_ref, right_ref, o_ref):
    devices, us, vs = sizes
    rows = us * devices
    free = right_ref.shape[1] // (2 * KEPT)
    left = left_ref[...].reshape(us, vs, devices, LANES)
    left = jnp.concatenate([left[:, v].reshape(rows, LANES) for v in range(vs)], axis=1)
    new = lax.broadcasted_iota(jnp.int32, (rows, rows), 0)
    picks = one_hot((rows, rows), 1, new % us * devices + new // us)
    left = exact_dot(picks, left).astype(jnp.bfloat16)
    half = right_ref.shape[0] // 2
    depth = half // vs
    real, imag = right_ref[:half, :], right_ref[half:, :]
    block = rows // KEPT
    for g in range(KEPT):
        stack = []
        for v in range(vs):
            r = [real[v * depth : (v + 1) * depth, (h * KEPT + g) * free :][:, :free] for h in range(2)]
            i = [imag[v * depth : (v + 1) * depth, (h * KEPT + g) * free :][:, :free] for h in range(2)]
            to_real = jnp.concatenate([r[0], r[1], -i[0], -i[1]], axis=0)
            to_imag = jnp.concatenate([i[0], i[1], r[0], r[1]], axis=0)
            stack.append(jnp.concatenate([to_real, to_imag], axis=1))
        stack = jnp.concatenate(stack, axis=0)
        part = exact_dot(left[g * block : (g + 1) * block, :], stack)
        o_ref[g * block : (g + 1) * block, :] = part.astype(jnp.bfloat16)


def call(kernel, out_shape, inputs, scratch=(), flops=0, blocks=(), grant=24, outputs=0):
    moved = sum(x.size * x.dtype.itemsize for x in (*inputs, *blocks))
    out = jax.ShapeDtypeStruct(out_shape, jnp.bfloat16)
    return pl.pallas_call(
        kernel,
        out_shape=[out] * outputs if outputs else out,
        in_specs=whole(len(inputs)) + [pl.BlockSpec(memory_space=pl.ANY)] * len(blocks),
        out_specs=whole(outputs) if outputs else whole(1)[0],
        scratch_shapes=list(scratch),
        compiler_params=pltpu.CompilerParams(vmem_limit_bytes=grant * MEBI),
        cost_estimate=pl.CostEstimate(flops=flops, bytes_accessed=moved, transcendentals=0),
    )(*inputs, *blocks)


def tiles_fit(devices, rows_each, width):
    pair_devices = devices // 2
    if devices < 4 or devices & (devices - 1) or rows_each % pair_devices or width % 256:
        return False
    qs, group = rows_each // pair_devices, width // devices
    return (
        2 * qs == 8
        and LANES % group == 0
        and devices % (LANES // group) == 0
        and qs == SHARED // width
        and devices % 32 == 0
        and 2 * width * qs // rows_each == LANES
        and devices * rows_each * width // SHARED % (KEPT * LANES) == 0
        and 2 * (devices * rows_each * width // SHARED) == width
    )


def fast(branch_in, column_order, gate_a, gate_b):
    devices = lax.axis_size("mode")
    rows_each, width = branch_in.shape[2:]
    halves = devices // 2
    qs, group = rows_each // halves, width // devices
    tile_rows = 2 * qs
    rows = devices * tile_rows
    packed = call(
        functools.partial(pack_kernel, qs),
        (rows, width),
        (branch_in, column_order),
        flops=8 * rows * width * width,
        outputs=2,
    )
    packed = [side.reshape(devices, tile_rows, width) for side in packed]
    blocks, plan, *states = spread(gate_a, gate_b, packed)
    states = [state.reshape(rows, width) for state in states]
    sizes = (devices, qs, group, rows_each)
    scratch = [
        pltpu.VMEM((2, rows, 2 * width), jnp.bfloat16),
        pltpu.VMEM((rows, width), jnp.bfloat16),
        pltpu.VMEM((2, 2, width, width), jnp.bfloat16),
        pltpu.SemaphoreType.DMA((2, devices)),
    ]
    work = 2 * CYCLES * 4 * rows * width * width
    left = call(
        functools.partial(layers_kernel, sizes, True, plan),
        (halves * rows // 2, LANES),
        (states[0],),
        scratch,
        work,
        blocks,
        56,
    )
    groups = [[h * halves + e for e in range(halves)] for h in range(2)]
    left = trade(left.reshape(halves, rows // 2, LANES), groups)
    right = call(
        functools.partial(layers_kernel, sizes, False, plan), (rows, width), (states[1],), scratch, work, blocks, 56
    )
    free = width // (2 * KEPT)
    us = halves
    partial_sums = call(
        functools.partial(join_kernel, (devices, us, qs)),
        (devices * us, 2 * free),
        (left.reshape(halves * rows // 2, LANES), right),
        flops=2 * devices * us * LANES * qs * 2 * free,
    )
    parts = trade(partial_sums.reshape(devices, us, 2 * free))
    parts = parts.reshape(2, halves, us, 2 * free).astype(jnp.float32)
    join_scale = (2.0 * SHARED) ** (-0.5)
    return (jnp.sum(parts, axis=1) * join_scale).astype(jnp.bfloat16).reshape(2, us, 2, free)


def flip(value, *bits):
    mask = sum(2**bit for bit in bits)
    pairs = [(source, source ^ mask) for source in range(lax.axis_size("mode"))]
    return lax.ppermute(value, "mode", pairs)


def plane(value, sources):
    over_x, over_y = flip(value, 1), flip(value, 2)
    diagonal = flip(over_x[:1], 2), flip(over_y[1:], 1)
    turned = [tuple(source + more for source in sources) for more in ((1,), (2,), (1, 2))]
    return [
        (value, sources, (0, 1)),
        (over_x, turned[0], (0, 1)),
        (over_y, turned[1], (0, 1)),
        (diagonal[0], turned[2], (0,)),
        (diagonal[1], turned[2], (1,)),
    ]


def spread(gate_a, gate_b, packed):
    bits = lax.axis_size("mode").bit_length() - 1
    own = jnp.stack([gate_a, gate_b])[:, None]
    far = [()]
    for bit in range(3, bits):
        far += [source + (bit,) for source in far]
    came = [flip(own, *source) for source in far[1:]]
    left, *rest = lax.optimization_barrier((packed[0], *came[1:]))
    sets = [(own, ((),)), (came[0], tuple(far[1:2]))]
    if rest:
        sets.append((jnp.concatenate(rest, axis=1), tuple(far[2:])))
    blocks = []
    for number, (value, sources) in enumerate(sets):
        if number:
            value, *_ = lax.optimization_barrier((value, *packed, blocks[-2][0], blocks[-1][0]))
        blocks += plane(value, sources)
    right, *_ = lax.optimization_barrier((packed[1], blocks[-4][0], blocks[-3][0]))
    last = len(blocks) - 2
    near = []
    for number, (value, sources, gates) in enumerate(blocks):
        if number >= last:
            value, *_ = lax.optimization_barrier((value, *[earlier for earlier, _, _ in near[:last]]))
        near.append((flip(value, 0), tuple(source + (0,) for source in sources), gates))
    blocks += near
    plan = tuple((sources, gates) for _, sources, gates in blocks)
    return [value for value, _, _ in blocks], plan, trade(left), trade(right)


def trade(value, groups=None):
    return lax.all_to_all(value, "mode", split_axis=0, concat_axis=0, axis_index_groups=groups, tiled=True)


def partner(value, axis, bit):
    mask = 2**bit
    pairs = [(source, source ^ mask) for source in range(lax.axis_size(axis))]
    return lax.ppermute(value, axis, pairs)


def product_four(states, layer_block):
    branches, parts, row_count, width = states.shape
    real_in = states[:, 0].reshape(branches * row_count, width)
    imag_in = states[:, 1].reshape(branches * row_count, width)
    real_part = jnp.dot(real_in, layer_block[0], preferred_element_type=jnp.float32) - jnp.dot(
        imag_in, layer_block[1], preferred_element_type=jnp.float32
    )
    imag_part = jnp.dot(real_in, layer_block[1], preferred_element_type=jnp.float32) + jnp.dot(
        imag_in, layer_block[0], preferred_element_type=jnp.float32
    )
    joined_parts = jnp.stack(
        [
            real_part.reshape(branches, row_count, width),
            imag_part.reshape(branches, row_count, width),
        ],
        axis=1,
    )
    return joined_parts.astype(jnp.bfloat16)


def complex_rows(left_real, left_imag, right_real, right_imag):
    real_part = jnp.dot(left_real, right_real, preferred_element_type=jnp.float32) - jnp.dot(
        left_imag, right_imag, preferred_element_type=jnp.float32
    )
    imag_part = jnp.dot(left_real, right_imag, preferred_element_type=jnp.float32) + jnp.dot(
        left_imag, right_real, preferred_element_type=jnp.float32
    )
    return jnp.stack([real_part, imag_part], axis=1)


def read_bit(device_index, bit_number):
    return device_index // 2**bit_number % 2


def trade_axes(buffer, axis_bits, trader, device_index):
    for position, bit_number in enumerate(axis_bits):
        own_bit = read_bit(device_index, bit_number)
        kept_half = lax.dynamic_index_in_dim(buffer, own_bit, position, keepdims=False)
        sent_half = lax.dynamic_index_in_dim(buffer, 1 - own_bit, position, keepdims=False)
        received = trader(sent_half, bit_number)
        first_half = jnp.where(own_bit == 0, kept_half, received)
        second_half = jnp.where(own_bit == 0, received, kept_half)
        buffer = jnp.stack([first_half, second_half], axis=position)
    return buffer


def general(branch_in, column_order, gate_a, gate_b):
    join_scale = (2.0 * SHARED) ** (-0.5)
    devices_mode = lax.axis_size("mode")
    whole_a, whole_b = (
        lax.all_gather(gate_a, "mode", axis=1, tiled=True),
        lax.all_gather(gate_b, "mode", axis=1, tiled=True),
    )
    states = jnp.take_along_axis(branch_in, column_order[:, None, None, :], axis=3)
    for layer_number in range(2 * CYCLES):
        if layer_number > 0:
            states = lax.all_to_all(states, "mode", split_axis=3, concat_axis=3, tiled=True)
        states = product_four(states, whole_a if layer_number % 2 == 0 else whole_b)
    local_cells = states.shape[2] * states.shape[3]
    local_rows = local_cells // SHARED
    shared_rows = SHARED // devices_mode
    join_width = local_cells // (shared_rows * KEPT)
    results = []
    for pair_number in range(2):
        left_part = states[2 * pair_number].reshape(2, local_rows, SHARED)
        right_part = states[2 * pair_number + 1].reshape(2, shared_rows, KEPT, join_width)
        device_index = lax.axis_index("mode")
        total_bits = devices_mode.bit_length() - 1
        group_bits = total_bits - 4
        batch_bits = KEPT.bit_length() - 1
        groups = devices_mode // (4 * KEPT)
        span = 2 * shared_rows
        outer = SHARED // (span * groups)
        half_join = join_width // 2

        def left_trader(piece, bit_number):
            return partner(piece, "mode", bit_number)

        def right_trader(piece, bit_number):
            return partner(piece, "mode", bit_number)

        left_buffer = left_part.reshape(2, local_rows, outer, groups, span).transpose(3, 0, 1, 2, 4)
        left_buffer = left_buffer.reshape((2,) * group_bits + (1, 2, local_rows, outer, span))
        left_buffer = jnp.broadcast_to(
            left_buffer, (2,) * group_bits + (2, 2, local_rows, outer, span)
        )
        left_bits = [group_bits - position for position in range(group_bits)] + [0]
        left_buffer = trade_axes(left_buffer, left_bits, left_trader, device_index)
        left_block = left_buffer.reshape(devices_mode // (2 * KEPT), 2, local_rows, outer * span)
        left_block = left_block.transpose(1, 0, 2, 3).reshape(2, half_join, SHARED // groups)
        right_buffer = right_part.reshape(2, shared_rows, KEPT, 2, half_join).transpose(
            2, 3, 0, 1, 4
        )
        right_buffer = right_buffer.reshape((2,) * batch_bits + (1, 2, 2, shared_rows, half_join))
        right_buffer = jnp.broadcast_to(
            right_buffer, (2,) * batch_bits + (2, 2, 2, shared_rows, half_join)
        )
        right_bits = [total_bits - 1 - position for position in range(batch_bits)] + [
            total_bits - batch_bits - 1,
            0,
        ]
        right_buffer = trade_axes(right_buffer, right_bits, right_trader, device_index)
        right_block = right_buffer.reshape(2 * KEPT, 2, 2, shared_rows, half_join)
        right_block = right_block.transpose(2, 0, 1, 3, 4).reshape(2, SHARED // groups, half_join)
        running = complex_rows(left_block[0], left_block[1], right_block[0], right_block[1])
        for position in range(group_bits):
            bit_number = group_bits - position
            own_bit = read_bit(device_index, bit_number)
            row_count = running.shape[0]
            halves = running.reshape(2, row_count // 2, 2, half_join)
            kept_half = lax.dynamic_index_in_dim(halves, own_bit, 0, keepdims=False)
            sent_half = lax.dynamic_index_in_dim(halves, 1 - own_bit, 0, keepdims=False)
            running = kept_half + partner(
                sent_half.astype(jnp.bfloat16), "mode", bit_number
            ).astype(sent_half.dtype)
        rounded = (running * join_scale).astype(jnp.bfloat16)
        own_bit = read_bit(device_index, 0)
        halves = rounded.reshape(2, local_rows, 2, half_join)
        kept_half = lax.dynamic_index_in_dim(halves, own_bit, 0, keepdims=False)
        sent_half = lax.dynamic_index_in_dim(halves, 1 - own_bit, 0, keepdims=False)
        received = partner(sent_half, "mode", 0)
        first_half = jnp.where(own_bit == 0, kept_half, received)
        second_half = jnp.where(own_bit == 0, received, kept_half)
        finished = jnp.concatenate([first_half, second_half], axis=2)
        results.append(finished)
    return jnp.stack(results)


def local(branch_in, column_order, gate_a, gate_b):
    branches, _, rows_each, width = branch_in.shape
    if branches == 4 and tiles_fit(lax.axis_size("mode"), rows_each, width):
        return fast(branch_in, column_order, gate_a, gate_b)
    return general(branch_in, column_order, gate_a, gate_b)


def solution(mesh):
    in_specs = (
        P(None, None, ("cuts", "mode"), None),
        P(),
        P(None, "mode", None),
        P(None, "mode", None),
    )
    out_specs = P(None, ("cuts", "mode"), None, None)
    return jax.shard_map(local, mesh=mesh, in_specs=in_specs, out_specs=out_specs, check_vma=False)
```

```python
import functools

import jax
import jax.numpy as jnp
from jax import lax
from jax.experimental import pallas as pl
from jax.experimental.pallas import tpu as pltpu
from jax.sharding import PartitionSpec as P

SHARED = 4096
KEPT = 4
CYCLES = 2
LANES = 128
MEBI = 1024 * 1024


def whole(count):
    return [pl.BlockSpec(memory_space=pltpu.VMEM)] * count


def one_hot(shape, axis, wanted):
    return (lax.broadcasted_iota(jnp.int32, shape, axis) == wanted).astype(jnp.bfloat16)


def exact_dot(left, right):
    return jnp.dot(left, right, preferred_element_type=jnp.float32)


def pack_kernel(qs, x_ref, order_ref, o_ref, ordered):
    _, parts, rows_each, width = x_ref.shape
    rows = parts * rows_each
    step = min(256, width)
    new = lax.broadcasted_iota(jnp.int32, (2 * rows, 2 * rows), 0)
    e, side = new // (2 * parts * qs), new // (parts * qs) % 2
    k, q = new // qs % parts, new % qs
    pack = one_hot((2 * rows, 2 * rows), 1, side * rows + k * rows_each + e * qs + q)
    for pair in range(x_ref.shape[0] // 2):
        for side in range(2):
            branch = 2 * pair + side
            values = x_ref[branch].reshape(rows, width)
            for start in range(0, width, step):
                picks = one_hot((width, step), 0, order_ref[branch : branch + 1, start : start + step])
                found = exact_dot(values, picks).astype(jnp.bfloat16)
                ordered[side * rows : (side + 1) * rows, start : start + step] = found
        packed = exact_dot(pack, ordered[...]).astype(jnp.bfloat16)
        o_ref[2 * pair * rows : 2 * (pair + 1) * rows, :] = packed


def swap_sign(tiles, qs):
    turned = pltpu.roll(tiles, qs, 1)
    row = lax.broadcasted_iota(jnp.int32, (1,) + tiles.shape[1:], 1)
    return turned * jnp.where(row < qs, -1.0, 1.0)


def regroup_store(acc, first_lane, group, devices, tile_rows, x_ref):
    width = x_ref.shape[1] // 2
    per = LANES // group
    lane = lax.broadcasted_iota(jnp.int32, (tile_rows, LANES), 1) // group
    for offset in range(0, acc.shape[1], LANES):
        tile = acc[:, offset : offset + LANES].reshape(devices, tile_rows, LANES)
        row_start = (first_lane + offset) // group * tile_rows
        for block in range(devices // per):
            parts = [tile[block * per + m] for m in range(per)]
            bit = 1
            while bit < per:
                moved = list(parts)
                keep = (lane // bit) % 2 == 0
                for m in range(per):
                    if m & bit:
                        continue
                    low, high = parts[m], parts[m | bit]
                    if 2 * bit * group == LANES:
                        up = down = pltpu.roll(jnp.where(keep, high, low), LANES // 2, 1)
                    else:
                        up, down = pltpu.roll(high, bit * group, 1), pltpu.roll(low, LANES - bit * group, 1)
                    moved[m] = jnp.where(keep, low, up)
                    moved[m | bit] = jnp.where(keep, down, high)
                parts = moved
                bit *= 2
            tiles = jnp.stack(parts)
            rows = pl.ds(row_start, per * tile_rows)
            lanes = pl.ds(block * LANES, LANES)
            x_ref[rows, lanes] = tiles.reshape(per * tile_rows, LANES).astype(jnp.bfloat16)
            turned = swap_sign(tiles, tile_rows // 2)
            x_ref[rows, pl.ds(width + block * LANES, LANES)] = turned.reshape(per * tile_rows, LANES).astype(jnp.bfloat16)


def gate_copies(plan, blocks, whole_ref, sems):
    me = lax.axis_index("mode")
    copies = ([], [])
    for (sources, gates), block in zip(plan, blocks):
        for place, source in enumerate(sources):
            device = me
            for bit in source:
                device = device + (1 - 2 * (me // 2**bit % 2)) * 2**bit
            size = block.shape[3]
            rows = pl.ds(pl.multiple_of(device * size, size), size)
            for position, gate in enumerate(gates):
                sem = sems.at[gate, len(copies[gate])]
                copies[gate].append(
                    pltpu.make_async_copy(block.at[position, place], whole_ref.at[gate, :, rows, :], sem)
                )
    return copies


def layers_kernel(sizes, is_left, plan, x_ref, *refs):
    devices, qs, group, rows_each = sizes
    blocks, (o_ref, xs, last, whole_ref, sems) = refs[: len(plan)], refs[len(plan) :]
    copies = gate_copies(plan, blocks, whole_ref, sems)
    for gate in range(2):
        for copy in copies[gate]:
            copy.start()
    tile_rows = 2 * qs
    rows, width = x_ref.shape[0] // 2, x_ref.shape[1]
    first = x_ref[...].astype(jnp.float32).reshape(devices, 2 * tile_rows, width)
    first = first[:, :tile_rows] if is_left else first[:, tile_rows:]
    xs[0, :, :width] = first.reshape(rows, width).astype(jnp.bfloat16)
    xs[0, :, width:] = swap_sign(first, qs).reshape(rows, width).astype(jnp.bfloat16)
    step = min(512, width)
    for layer in range(2 * CYCLES):
        if layer < 2:
            for copy in copies[layer]:
                copy.wait()
        gate = whole_ref.at[layer % 2]
        here, later = xs.at[layer % 2], xs.at[(layer + 1) % 2]
        for start in range(0, width, step):
            cols = slice(start, start + step)
            acc = exact_dot(here[...], gate[:, :, cols].reshape(2 * width, step))
            if layer < 2 * CYCLES - 1:
                regroup_store(acc, start, group, devices, tile_rows, later)
            else:
                last[:, cols] = acc.astype(jnp.bfloat16)
    half = rows // 2
    new = lax.broadcasted_iota(jnp.int32, (rows, rows), 0)
    part, inner = new // half, new % half
    if is_left:
        v, r = inner // devices, inner % devices
        picks = one_hot((rows, rows), 1, r * tile_rows + part * qs + v)
        moved = exact_dot(picks, last[...]).astype(jnp.bfloat16)
        span = 2 * rows_each
        each = width * qs // rows_each
        words = width // span
        step = min(256, width)
        for start in range(0, width, step):
            place = start + lax.broadcasted_iota(jnp.int32, (width, step), 1)
            e, rest = place // each, place % each
            h, w, qr = rest // (words * qs), rest % (words * qs) // qs, rest % qs
            lanes = one_hot((width, step), 0, w * span + (e * qs + qr) * 2 + h)
            sent = exact_dot(moved, lanes)
            low_lane = lax.broadcasted_iota(jnp.int32, (half, LANES), 1) < LANES // 2
            for offset in range(0, step, LANES):
                real = sent[:half, offset : offset + LANES]
                imag = sent[half:, offset : offset + LANES]
                e0 = (start + offset) // each
                even = jnp.where(low_lane, real, pltpu.roll(imag, LANES // 2, 1))
                odd = jnp.where(low_lane, pltpu.roll(real, LANES // 2, 1), imag)
                o_ref[e0 * half : (e0 + 1) * half, :] = even.astype(jnp.bfloat16)
                o_ref[(e0 + 1) * half : (e0 + 2) * half, :] = odd.astype(jnp.bfloat16)
    else:
        r, q = inner // qs, inner % qs
        picks = one_hot((rows, rows), 1, r * tile_rows + part * qs + q)
        o_ref[...] = exact_dot(picks, last[...]).astype(jnp.bfloat16)


def join_kernel(sizes, left_ref, right_ref, o_ref):
    devices, us, vs = sizes
    rows = us * devices
    free = right_ref.shape[1] // (2 * KEPT)
    left = left_ref[...].reshape(us, vs, devices, LANES)
    left = jnp.concatenate([left[:, v].reshape(rows, LANES) for v in range(vs)], axis=1)
    new = lax.broadcasted_iota(jnp.int32, (rows, rows), 0)
    picks = one_hot((rows, rows), 1, new % us * devices + new // us)
    left = exact_dot(picks, left).astype(jnp.bfloat16)
    half = right_ref.shape[0] // 2
    depth = half // vs
    real, imag = right_ref[:half, :], right_ref[half:, :]
    block = rows // KEPT
    for g in range(KEPT):
        stack = []
        for v in range(vs):
            r = [real[v * depth : (v + 1) * depth, (h * KEPT + g) * free :][:, :free] for h in range(2)]
            i = [imag[v * depth : (v + 1) * depth, (h * KEPT + g) * free :][:, :free] for h in range(2)]
            to_real = jnp.concatenate([r[0], r[1], -i[0], -i[1]], axis=0)
            to_imag = jnp.concatenate([i[0], i[1], r[0], r[1]], axis=0)
            stack.append(jnp.concatenate([to_real, to_imag], axis=1))
        stack = jnp.concatenate(stack, axis=0)
        part = exact_dot(left[g * block : (g + 1) * block, :], stack)
        o_ref[g * block : (g + 1) * block, :] = part.astype(jnp.bfloat16)


def call(kernel, out_shape, inputs, scratch=(), flops=0, blocks=(), grant=24):
    moved = sum(x.size * x.dtype.itemsize for x in (*inputs, *blocks))
    return pl.pallas_call(
        kernel,
        out_shape=jax.ShapeDtypeStruct(out_shape, jnp.bfloat16),
        in_specs=whole(len(inputs)) + [pl.BlockSpec(memory_space=pl.ANY)] * len(blocks),
        out_specs=whole(1)[0],
        scratch_shapes=list(scratch),
        compiler_params=pltpu.CompilerParams(vmem_limit_bytes=grant * MEBI),
        cost_estimate=pl.CostEstimate(flops=flops, bytes_accessed=moved, transcendentals=0),
    )(*inputs, *blocks)


def tiles_fit(devices, rows_each, width):
    pair_devices = devices // 2
    if devices < 4 or devices & (devices - 1) or rows_each % pair_devices or width % 256:
        return False
    qs, group = rows_each // pair_devices, width // devices
    return (
        2 * qs == 8
        and LANES % group == 0
        and devices % (LANES // group) == 0
        and qs == SHARED // width
        and devices % 32 == 0
        and 2 * width * qs // rows_each == LANES
        and devices * rows_each * width // SHARED % (KEPT * LANES) == 0
        and 2 * (devices * rows_each * width // SHARED) == width
    )


def fast(branch_in, column_order, gate_a, gate_b):
    devices = lax.axis_size("mode")
    rows_each, width = branch_in.shape[2:]
    halves = devices // 2
    qs, group = rows_each // halves, width // devices
    tile_rows = 2 * qs
    rows = devices * tile_rows
    packed = call(
        functools.partial(pack_kernel, qs),
        (2 * rows, width),
        (branch_in, column_order),
        [pltpu.VMEM((4 * rows_each, width), jnp.bfloat16)],
        8 * rows * width * width,
    )
    blocks, plan, states = spread(gate_a, gate_b, packed.reshape(devices, 2 * tile_rows, width))
    states = states.reshape(2 * rows, width)
    sizes = (devices, qs, group, rows_each)
    scratch = [
        pltpu.VMEM((2, rows, 2 * width), jnp.bfloat16),
        pltpu.VMEM((rows, width), jnp.bfloat16),
        pltpu.VMEM((2, 2, width, width), jnp.bfloat16),
        pltpu.SemaphoreType.DMA((2, devices)),
    ]
    work = 2 * CYCLES * 4 * rows * width * width
    left = call(
        functools.partial(layers_kernel, sizes, True, plan),
        (halves * rows // 2, LANES),
        (states,),
        scratch,
        work,
        blocks,
        56,
    )
    groups = [[h * halves + e for e in range(halves)] for h in range(2)]
    left = trade(left.reshape(halves, rows // 2, LANES), groups)
    right = call(
        functools.partial(layers_kernel, sizes, False, plan), (rows, width), (states,), scratch, work, blocks, 56
    )
    free = width // (2 * KEPT)
    us = halves
    partial_sums = call(
        functools.partial(join_kernel, (devices, us, qs)),
        (devices * us, 2 * free),
        (left.reshape(halves * rows // 2, LANES), right),
        flops=2 * devices * us * LANES * qs * 2 * free,
    )
    parts = trade(partial_sums.reshape(devices, us, 2 * free))
    parts = parts.reshape(2, halves, us, 2 * free).astype(jnp.float32)
    join_scale = (2.0 * SHARED) ** (-0.5)
    return (jnp.sum(parts, axis=1) * join_scale).astype(jnp.bfloat16).reshape(2, us, 2, free)


def flip(value, *bits):
    mask = sum(2**bit for bit in bits)
    pairs = [(source, source ^ mask) for source in range(lax.axis_size("mode"))]
    return lax.ppermute(value, "mode", pairs)


def plane(value, sources):
    over_x, over_y = flip(value, 1), flip(value, 2)
    diagonal = flip(over_x[:1], 2), flip(over_y[1:], 1)
    turned = [tuple(source + more for source in sources) for more in ((1,), (2,), (1, 2))]
    return [
        (value, sources, (0, 1)),
        (over_x, turned[0], (0, 1)),
        (over_y, turned[1], (0, 1)),
        (diagonal[0], turned[2], (0,)),
        (diagonal[1], turned[2], (1,)),
    ]


def spread(gate_a, gate_b, packed):
    bits = lax.axis_size("mode").bit_length() - 1
    own = jnp.stack([gate_a, gate_b])[:, None]
    far = [()]
    for bit in range(3, bits):
        far += [source + (bit,) for source in far]
    came = [flip(own, *source) for source in far[1:]]
    sets = [(own, ((),)), (came[0], tuple(far[1:2]))]
    if came[1:]:
        sets.append((jnp.concatenate(came[1:], axis=1), tuple(far[2:])))
    blocks = []
    for number, (value, sources) in enumerate(sets):
        if number:
            tied = (blocks[3][0], blocks[4][0]) if number == 1 else (packed, blocks[6][0], blocks[7][0])
            value, *_ = lax.optimization_barrier((value, *tied))
        blocks += plane(value, sources)
    packed, *_ = lax.optimization_barrier((packed, *came[1:], blocks[8][0], blocks[9][0]))
    last = len(blocks) - 2
    near = []
    for number, (value, sources, gates) in enumerate(blocks):
        if number >= last:
            value, *_ = lax.optimization_barrier((value, *[earlier for earlier, _, _ in near[:last]]))
        near.append((flip(value, 0), tuple(source + (0,) for source in sources), gates))
    blocks += near
    plan = tuple((sources, gates) for _, sources, gates in blocks)
    return [value for value, _, _ in blocks], plan, trade(packed)


def trade(value, groups=None):
    return lax.all_to_all(value, "mode", split_axis=0, concat_axis=0, axis_index_groups=groups, tiled=True)


def partner(value, axis, bit):
    mask = 2**bit
    pairs = [(source, source ^ mask) for source in range(lax.axis_size(axis))]
    return lax.ppermute(value, axis, pairs)


def product_four(states, layer_block):
    branches, parts, row_count, width = states.shape
    real_in = states[:, 0].reshape(branches * row_count, width)
    imag_in = states[:, 1].reshape(branches * row_count, width)
    real_part = jnp.dot(real_in, layer_block[0], preferred_element_type=jnp.float32) - jnp.dot(
        imag_in, layer_block[1], preferred_element_type=jnp.float32
    )
    imag_part = jnp.dot(real_in, layer_block[1], preferred_element_type=jnp.float32) + jnp.dot(
        imag_in, layer_block[0], preferred_element_type=jnp.float32
    )
    joined_parts = jnp.stack(
        [
            real_part.reshape(branches, row_count, width),
            imag_part.reshape(branches, row_count, width),
        ],
        axis=1,
    )
    return joined_parts.astype(jnp.bfloat16)


def complex_rows(left_real, left_imag, right_real, right_imag):
    real_part = jnp.dot(left_real, right_real, preferred_element_type=jnp.float32) - jnp.dot(
        left_imag, right_imag, preferred_element_type=jnp.float32
    )
    imag_part = jnp.dot(left_real, right_imag, preferred_element_type=jnp.float32) + jnp.dot(
        left_imag, right_real, preferred_element_type=jnp.float32
    )
    return jnp.stack([real_part, imag_part], axis=1)


def read_bit(device_index, bit_number):
    return device_index // 2**bit_number % 2


def trade_axes(buffer, axis_bits, trader, device_index):
    for position, bit_number in enumerate(axis_bits):
        own_bit = read_bit(device_index, bit_number)
        kept_half = lax.dynamic_index_in_dim(buffer, own_bit, position, keepdims=False)
        sent_half = lax.dynamic_index_in_dim(buffer, 1 - own_bit, position, keepdims=False)
        received = trader(sent_half, bit_number)
        first_half = jnp.where(own_bit == 0, kept_half, received)
        second_half = jnp.where(own_bit == 0, received, kept_half)
        buffer = jnp.stack([first_half, second_half], axis=position)
    return buffer


def general(branch_in, column_order, gate_a, gate_b):
    join_scale = (2.0 * SHARED) ** (-0.5)
    devices_mode = lax.axis_size("mode")
    whole_a, whole_b = (
        lax.all_gather(gate_a, "mode", axis=1, tiled=True),
        lax.all_gather(gate_b, "mode", axis=1, tiled=True),
    )
    states = jnp.take_along_axis(branch_in, column_order[:, None, None, :], axis=3)
    for layer_number in range(2 * CYCLES):
        if layer_number > 0:
            states = lax.all_to_all(states, "mode", split_axis=3, concat_axis=3, tiled=True)
        states = product_four(states, whole_a if layer_number % 2 == 0 else whole_b)
    local_cells = states.shape[2] * states.shape[3]
    local_rows = local_cells // SHARED
    shared_rows = SHARED // devices_mode
    join_width = local_cells // (shared_rows * KEPT)
    results = []
    for pair_number in range(2):
        left_part = states[2 * pair_number].reshape(2, local_rows, SHARED)
        right_part = states[2 * pair_number + 1].reshape(2, shared_rows, KEPT, join_width)
        device_index = lax.axis_index("mode")
        total_bits = devices_mode.bit_length() - 1
        group_bits = total_bits - 4
        batch_bits = KEPT.bit_length() - 1
        groups = devices_mode // (4 * KEPT)
        span = 2 * shared_rows
        outer = SHARED // (span * groups)
        half_join = join_width // 2

        def left_trader(piece, bit_number):
            return partner(piece, "mode", bit_number)

        def right_trader(piece, bit_number):
            return partner(piece, "mode", bit_number)

        left_buffer = left_part.reshape(2, local_rows, outer, groups, span).transpose(3, 0, 1, 2, 4)
        left_buffer = left_buffer.reshape((2,) * group_bits + (1, 2, local_rows, outer, span))
        left_buffer = jnp.broadcast_to(
            left_buffer, (2,) * group_bits + (2, 2, local_rows, outer, span)
        )
        left_bits = [group_bits - position for position in range(group_bits)] + [0]
        left_buffer = trade_axes(left_buffer, left_bits, left_trader, device_index)
        left_block = left_buffer.reshape(devices_mode // (2 * KEPT), 2, local_rows, outer * span)
        left_block = left_block.transpose(1, 0, 2, 3).reshape(2, half_join, SHARED // groups)
        right_buffer = right_part.reshape(2, shared_rows, KEPT, 2, half_join).transpose(
            2, 3, 0, 1, 4
        )
        right_buffer = right_buffer.reshape((2,) * batch_bits + (1, 2, 2, shared_rows, half_join))
        right_buffer = jnp.broadcast_to(
            right_buffer, (2,) * batch_bits + (2, 2, 2, shared_rows, half_join)
        )
        right_bits = [total_bits - 1 - position for position in range(batch_bits)] + [
            total_bits - batch_bits - 1,
            0,
        ]
        right_buffer = trade_axes(right_buffer, right_bits, right_trader, device_index)
        right_block = right_buffer.reshape(2 * KEPT, 2, 2, shared_rows, half_join)
        right_block = right_block.transpose(2, 0, 1, 3, 4).reshape(2, SHARED // groups, half_join)
        running = complex_rows(left_block[0], left_block[1], right_block[0], right_block[1])
        for position in range(group_bits):
            bit_number = group_bits - position
            own_bit = read_bit(device_index, bit_number)
            row_count = running.shape[0]
            halves = running.reshape(2, row_count // 2, 2, half_join)
            kept_half = lax.dynamic_index_in_dim(halves, own_bit, 0, keepdims=False)
            sent_half = lax.dynamic_index_in_dim(halves, 1 - own_bit, 0, keepdims=False)
            running = kept_half + partner(
                sent_half.astype(jnp.bfloat16), "mode", bit_number
            ).astype(sent_half.dtype)
        rounded = (running * join_scale).astype(jnp.bfloat16)
        own_bit = read_bit(device_index, 0)
        halves = rounded.reshape(2, local_rows, 2, half_join)
        kept_half = lax.dynamic_index_in_dim(halves, own_bit, 0, keepdims=False)
        sent_half = lax.dynamic_index_in_dim(halves, 1 - own_bit, 0, keepdims=False)
        received = partner(sent_half, "mode", 0)
        first_half = jnp.where(own_bit == 0, kept_half, received)
        second_half = jnp.where(own_bit == 0, received, kept_half)
        finished = jnp.concatenate([first_half, second_half], axis=2)
        results.append(finished)
    return jnp.stack(results)


def local(branch_in, column_order, gate_a, gate_b):
    branches, _, rows_each, width = branch_in.shape
    if branches == 4 and tiles_fit(lax.axis_size("mode"), rows_each, width):
        return fast(branch_in, column_order, gate_a, gate_b)
    return general(branch_in, column_order, gate_a, gate_b)


def solution(mesh):
    in_specs = (
        P(None, None, ("cuts", "mode"), None),
        P(),
        P(None, "mode", None),
        P(None, "mode", None),
    )
    out_specs = P(None, ("cuts", "mode"), None, None)
    return jax.shard_map(local, mesh=mesh, in_specs=in_specs, out_specs=out_specs, check_vma=False)
```

```python
import functools

import jax
import jax.numpy as jnp
from jax import lax
from jax.experimental import pallas as pl
from jax.experimental.pallas import tpu as pltpu
from jax.sharding import PartitionSpec as P

SHARED = 4096
KEPT = 4
CYCLES = 2
LANES = 128
MEBI = 1024 * 1024


def whole(count):
    return [pl.BlockSpec(memory_space=pltpu.VMEM)] * count


def one_hot(shape, axis, wanted):
    return (lax.broadcasted_iota(jnp.int32, shape, axis) == wanted).astype(jnp.bfloat16)


def exact_dot(left, right):
    return jnp.dot(left, right, preferred_element_type=jnp.float32)


def pack_kernel(qs, x_ref, order_ref, o_ref, ordered):
    _, parts, rows_each, width = x_ref.shape
    rows = parts * rows_each
    step = min(256, width)
    new = lax.broadcasted_iota(jnp.int32, (2 * rows, 2 * rows), 0)
    e, side = new // (2 * parts * qs), new // (parts * qs) % 2
    k, q = new // qs % parts, new % qs
    pack = one_hot((2 * rows, 2 * rows), 1, side * rows + k * rows_each + e * qs + q)
    for pair in range(x_ref.shape[0] // 2):
        for side in range(2):
            branch = 2 * pair + side
            values = x_ref[branch].reshape(rows, width)
            for start in range(0, width, step):
                picks = one_hot((width, step), 0, order_ref[branch : branch + 1, start : start + step])
                found = exact_dot(values, picks).astype(jnp.bfloat16)
                ordered[side * rows : (side + 1) * rows, start : start + step] = found
        packed = exact_dot(pack, ordered[...]).astype(jnp.bfloat16)
        o_ref[2 * pair * rows : 2 * (pair + 1) * rows, :] = packed


def swap_sign(tiles, qs):
    turned = pltpu.roll(tiles, qs, 1)
    row = lax.broadcasted_iota(jnp.int32, (1,) + tiles.shape[1:], 1)
    return turned * jnp.where(row < qs, -1.0, 1.0)


def regroup_store(acc, first_lane, group, devices, tile_rows, x_ref):
    width = x_ref.shape[1] // 2
    per = LANES // group
    lane = lax.broadcasted_iota(jnp.int32, (tile_rows, LANES), 1) // group
    for offset in range(0, acc.shape[1], LANES):
        tile = acc[:, offset : offset + LANES].reshape(devices, tile_rows, LANES)
        row_start = (first_lane + offset) // group * tile_rows
        for block in range(devices // per):
            parts = [tile[block * per + m] for m in range(per)]
            bit = 1
            while bit < per:
                moved = list(parts)
                keep = (lane // bit) % 2 == 0
                for m in range(per):
                    if m & bit:
                        continue
                    low, high = parts[m], parts[m | bit]
                    if 2 * bit * group == LANES:
                        up = down = pltpu.roll(jnp.where(keep, high, low), LANES // 2, 1)
                    else:
                        up, down = pltpu.roll(high, bit * group, 1), pltpu.roll(low, LANES - bit * group, 1)
                    moved[m] = jnp.where(keep, low, up)
                    moved[m | bit] = jnp.where(keep, down, high)
                parts = moved
                bit *= 2
            tiles = jnp.stack(parts)
            rows = pl.ds(row_start, per * tile_rows)
            lanes = pl.ds(block * LANES, LANES)
            x_ref[rows, lanes] = tiles.reshape(per * tile_rows, LANES).astype(jnp.bfloat16)
            turned = swap_sign(tiles, tile_rows // 2)
            x_ref[rows, pl.ds(width + block * LANES, LANES)] = turned.reshape(per * tile_rows, LANES).astype(jnp.bfloat16)


def gate_copies(plan, blocks, whole_ref, sems):
    me = lax.axis_index("mode")
    copies = ([], [])
    for (sources, gates), block in zip(plan, blocks):
        for place, source in enumerate(sources):
            device = me
            for bit in source:
                device = device + (1 - 2 * (me // 2**bit % 2)) * 2**bit
            size = block.shape[3]
            rows = pl.ds(pl.multiple_of(device * size, size), size)
            for position, gate in enumerate(gates):
                sem = sems.at[gate, len(copies[gate])]
                copies[gate].append(
                    pltpu.make_async_copy(block.at[position, place], whole_ref.at[gate, :, rows, :], sem)
                )
    return copies


def layers_kernel(sizes, is_left, plan, x_ref, *refs):
    devices, qs, group, rows_each = sizes
    blocks, (o_ref, xs, last, whole_ref, sems) = refs[: len(plan)], refs[len(plan) :]
    copies = gate_copies(plan, blocks, whole_ref, sems)
    for gate in range(2):
        for copy in copies[gate]:
            copy.start()
    tile_rows = 2 * qs
    rows, width = x_ref.shape[0] // 2, x_ref.shape[1]
    first = x_ref[...].astype(jnp.float32).reshape(devices, 2 * tile_rows, width)
    first = first[:, :tile_rows] if is_left else first[:, tile_rows:]
    xs[0, :, :width] = first.reshape(rows, width).astype(jnp.bfloat16)
    xs[0, :, width:] = swap_sign(first, qs).reshape(rows, width).astype(jnp.bfloat16)
    step = min(512, width)
    for layer in range(2 * CYCLES):
        if layer < 2:
            for copy in copies[layer]:
                copy.wait()
        gate = whole_ref.at[layer % 2]
        here, later = xs.at[layer % 2], xs.at[(layer + 1) % 2]
        for start in range(0, width, step):
            cols = slice(start, start + step)
            acc = exact_dot(here[...], gate[:, :, cols].reshape(2 * width, step))
            if layer < 2 * CYCLES - 1:
                regroup_store(acc, start, group, devices, tile_rows, later)
            else:
                last[:, cols] = acc.astype(jnp.bfloat16)
    half = rows // 2
    new = lax.broadcasted_iota(jnp.int32, (rows, rows), 0)
    part, inner = new // half, new % half
    if is_left:
        v, r = inner // devices, inner % devices
        picks = one_hot((rows, rows), 1, r * tile_rows + part * qs + v)
        moved = exact_dot(picks, last[...]).astype(jnp.bfloat16)
        span = 2 * rows_each
        each = width * qs // rows_each
        words = width // span
        step = min(256, width)
        for start in range(0, width, step):
            place = start + lax.broadcasted_iota(jnp.int32, (width, step), 1)
            e, rest = place // each, place % each
            h, w, qr = rest // (words * qs), rest % (words * qs) // qs, rest % qs
            lanes = one_hot((width, step), 0, w * span + (e * qs + qr) * 2 + h)
            sent = exact_dot(moved, lanes)
            low_lane = lax.broadcasted_iota(jnp.int32, (half, LANES), 1) < LANES // 2
            for offset in range(0, step, LANES):
                real = sent[:half, offset : offset + LANES]
                imag = sent[half:, offset : offset + LANES]
                e0 = (start + offset) // each
                even = jnp.where(low_lane, real, pltpu.roll(imag, LANES // 2, 1))
                odd = jnp.where(low_lane, pltpu.roll(real, LANES // 2, 1), imag)
                o_ref[e0 * half : (e0 + 1) * half, :] = even.astype(jnp.bfloat16)
                o_ref[(e0 + 1) * half : (e0 + 2) * half, :] = odd.astype(jnp.bfloat16)
    else:
        r, q = inner // qs, inner % qs
        picks = one_hot((rows, rows), 1, r * tile_rows + part * qs + q)
        o_ref[...] = exact_dot(picks, last[...]).astype(jnp.bfloat16)


def join_kernel(sizes, left_ref, right_ref, o_ref):
    devices, us, vs = sizes
    rows = us * devices
    free = right_ref.shape[1] // (2 * KEPT)
    left = left_ref[...].reshape(us, vs, devices, LANES)
    left = jnp.concatenate([left[:, v].reshape(rows, LANES) for v in range(vs)], axis=1)
    new = lax.broadcasted_iota(jnp.int32, (rows, rows), 0)
    picks = one_hot((rows, rows), 1, new % us * devices + new // us)
    left = exact_dot(picks, left).astype(jnp.bfloat16)
    half = right_ref.shape[0] // 2
    depth = half // vs
    real, imag = right_ref[:half, :], right_ref[half:, :]
    block = rows // KEPT
    for g in range(KEPT):
        stack = []
        for v in range(vs):
            r = [real[v * depth : (v + 1) * depth, (h * KEPT + g) * free :][:, :free] for h in range(2)]
            i = [imag[v * depth : (v + 1) * depth, (h * KEPT + g) * free :][:, :free] for h in range(2)]
            to_real = jnp.concatenate([r[0], r[1], -i[0], -i[1]], axis=0)
            to_imag = jnp.concatenate([i[0], i[1], r[0], r[1]], axis=0)
            stack.append(jnp.concatenate([to_real, to_imag], axis=1))
        stack = jnp.concatenate(stack, axis=0)
        part = exact_dot(left[g * block : (g + 1) * block, :], stack)
        o_ref[g * block : (g + 1) * block, :] = part.astype(jnp.bfloat16)


def call(kernel, out_shape, inputs, scratch=(), flops=0, blocks=(), grant=24):
    moved = sum(x.size * x.dtype.itemsize for x in (*inputs, *blocks))
    return pl.pallas_call(
        kernel,
        out_shape=jax.ShapeDtypeStruct(out_shape, jnp.bfloat16),
        in_specs=whole(len(inputs)) + [pl.BlockSpec(memory_space=pl.ANY)] * len(blocks),
        out_specs=whole(1)[0],
        scratch_shapes=list(scratch),
        compiler_params=pltpu.CompilerParams(vmem_limit_bytes=grant * MEBI),
        cost_estimate=pl.CostEstimate(flops=flops, bytes_accessed=moved, transcendentals=0),
    )(*inputs, *blocks)


def tiles_fit(devices, rows_each, width):
    pair_devices = devices // 2
    if devices < 4 or devices & (devices - 1) or rows_each % pair_devices or width % 256:
        return False
    qs, group = rows_each // pair_devices, width // devices
    return (
        2 * qs == 8
        and LANES % group == 0
        and devices % (LANES // group) == 0
        and qs == SHARED // width
        and devices % 32 == 0
        and 2 * width * qs // rows_each == LANES
        and devices * rows_each * width // SHARED % (KEPT * LANES) == 0
        and 2 * (devices * rows_each * width // SHARED) == width
    )


def fast(branch_in, column_order, gate_a, gate_b):
    devices = lax.axis_size("mode")
    rows_each, width = branch_in.shape[2:]
    halves = devices // 2
    qs, group = rows_each // halves, width // devices
    tile_rows = 2 * qs
    rows = devices * tile_rows
    packed = call(
        functools.partial(pack_kernel, qs),
        (2 * rows, width),
        (branch_in, column_order),
        [pltpu.VMEM((4 * rows_each, width), jnp.bfloat16)],
        8 * rows * width * width,
    )
    blocks, plan, states = spread(gate_a, gate_b, packed.reshape(devices, 2 * tile_rows, width))
    states = states.reshape(2 * rows, width)
    sizes = (devices, qs, group, rows_each)
    scratch = [
        pltpu.VMEM((2, rows, 2 * width), jnp.bfloat16),
        pltpu.VMEM((rows, width), jnp.bfloat16),
        pltpu.VMEM((2, 2, width, width), jnp.bfloat16),
        pltpu.SemaphoreType.DMA((2, devices)),
    ]
    work = 2 * CYCLES * 4 * rows * width * width
    left = call(
        functools.partial(layers_kernel, sizes, True, plan),
        (halves * rows // 2, LANES),
        (states,),
        scratch,
        work,
        blocks,
        56,
    )
    groups = [[h * halves + e for e in range(halves)] for h in range(2)]
    left = trade(left.reshape(halves, rows // 2, LANES), groups)
    right = call(
        functools.partial(layers_kernel, sizes, False, plan), (rows, width), (states,), scratch, work, blocks, 56
    )
    free = width // (2 * KEPT)
    us = halves
    partial_sums = call(
        functools.partial(join_kernel, (devices, us, qs)),
        (devices * us, 2 * free),
        (left.reshape(halves * rows // 2, LANES), right),
        flops=2 * devices * us * LANES * qs * 2 * free,
    )
    parts = trade(partial_sums.reshape(devices, us, 2 * free))
    parts = parts.reshape(2, halves, us, 2 * free).astype(jnp.float32)
    join_scale = (2.0 * SHARED) ** (-0.5)
    return (jnp.sum(parts, axis=1) * join_scale).astype(jnp.bfloat16).reshape(2, us, 2, free)


def flip(value, *bits):
    mask = sum(2**bit for bit in bits)
    pairs = [(source, source ^ mask) for source in range(lax.axis_size("mode"))]
    return lax.ppermute(value, "mode", pairs)


def plane(value, sources):
    over_x, over_y = flip(value, 1), flip(value, 2)
    diagonal = flip(over_x[:1], 2), flip(over_y[1:], 1)
    turned = [tuple(source + more for source in sources) for more in ((1,), (2,), (1, 2))]
    return [
        (value, sources, (0, 1)),
        (over_x, turned[0], (0, 1)),
        (over_y, turned[1], (0, 1)),
        (diagonal[0], turned[2], (0,)),
        (diagonal[1], turned[2], (1,)),
    ]


def spread(gate_a, gate_b, packed):
    bits = lax.axis_size("mode").bit_length() - 1
    own = jnp.stack([gate_a, gate_b])[:, None]
    far = [()]
    for bit in range(3, bits):
        far += [source + (bit,) for source in far]
    came = [flip(own, *source) for source in far[1:]]
    sets = [(own, ((),)), (came[0], tuple(far[1:2]))]
    if came[1:]:
        sets.append((jnp.concatenate(came[1:], axis=1), tuple(far[2:])))
    blocks = []
    for number, (value, sources) in enumerate(sets):
        if number:
            tied = (blocks[3][0], blocks[4][0]) if number == 1 else (packed, blocks[6][0], blocks[7][0])
            value, *_ = lax.optimization_barrier((value, *tied))
        blocks += plane(value, sources)
    packed, *_ = lax.optimization_barrier((packed, *came[1:]))
    last = len(blocks) - 2
    near = []
    for number, (value, sources, gates) in enumerate(blocks):
        if number >= last:
            value, *_ = lax.optimization_barrier((value, *[earlier for earlier, _, _ in near[:last]]))
        near.append((flip(value, 0), tuple(source + (0,) for source in sources), gates))
    blocks += near
    plan = tuple((sources, gates) for _, sources, gates in blocks)
    return [value for value, _, _ in blocks], plan, trade(packed)


def trade(value, groups=None):
    return lax.all_to_all(value, "mode", split_axis=0, concat_axis=0, axis_index_groups=groups, tiled=True)


def partner(value, axis, bit):
    mask = 2**bit
    pairs = [(source, source ^ mask) for source in range(lax.axis_size(axis))]
    return lax.ppermute(value, axis, pairs)


def product_four(states, layer_block):
    branches, parts, row_count, width = states.shape
    real_in = states[:, 0].reshape(branches * row_count, width)
    imag_in = states[:, 1].reshape(branches * row_count, width)
    real_part = jnp.dot(real_in, layer_block[0], preferred_element_type=jnp.float32) - jnp.dot(
        imag_in, layer_block[1], preferred_element_type=jnp.float32
    )
    imag_part = jnp.dot(real_in, layer_block[1], preferred_element_type=jnp.float32) + jnp.dot(
        imag_in, layer_block[0], preferred_element_type=jnp.float32
    )
    joined_parts = jnp.stack(
        [
            real_part.reshape(branches, row_count, width),
            imag_part.reshape(branches, row_count, width),
        ],
        axis=1,
    )
    return joined_parts.astype(jnp.bfloat16)


def complex_rows(left_real, left_imag, right_real, right_imag):
    real_part = jnp.dot(left_real, right_real, preferred_element_type=jnp.float32) - jnp.dot(
        left_imag, right_imag, preferred_element_type=jnp.float32
    )
    imag_part = jnp.dot(left_real, right_imag, preferred_element_type=jnp.float32) + jnp.dot(
        left_imag, right_real, preferred_element_type=jnp.float32
    )
    return jnp.stack([real_part, imag_part], axis=1)


def read_bit(device_index, bit_number):
    return device_index // 2**bit_number % 2


def trade_axes(buffer, axis_bits, trader, device_index):
    for position, bit_number in enumerate(axis_bits):
        own_bit = read_bit(device_index, bit_number)
        kept_half = lax.dynamic_index_in_dim(buffer, own_bit, position, keepdims=False)
        sent_half = lax.dynamic_index_in_dim(buffer, 1 - own_bit, position, keepdims=False)
        received = trader(sent_half, bit_number)
        first_half = jnp.where(own_bit == 0, kept_half, received)
        second_half = jnp.where(own_bit == 0, received, kept_half)
        buffer = jnp.stack([first_half, second_half], axis=position)
    return buffer


def general(branch_in, column_order, gate_a, gate_b):
    join_scale = (2.0 * SHARED) ** (-0.5)
    devices_mode = lax.axis_size("mode")
    whole_a, whole_b = (
        lax.all_gather(gate_a, "mode", axis=1, tiled=True),
        lax.all_gather(gate_b, "mode", axis=1, tiled=True),
    )
    states = jnp.take_along_axis(branch_in, column_order[:, None, None, :], axis=3)
    for layer_number in range(2 * CYCLES):
        if layer_number > 0:
            states = lax.all_to_all(states, "mode", split_axis=3, concat_axis=3, tiled=True)
        states = product_four(states, whole_a if layer_number % 2 == 0 else whole_b)
    local_cells = states.shape[2] * states.shape[3]
    local_rows = local_cells // SHARED
    shared_rows = SHARED // devices_mode
    join_width = local_cells // (shared_rows * KEPT)
    results = []
    for pair_number in range(2):
        left_part = states[2 * pair_number].reshape(2, local_rows, SHARED)
        right_part = states[2 * pair_number + 1].reshape(2, shared_rows, KEPT, join_width)
        device_index = lax.axis_index("mode")
        total_bits = devices_mode.bit_length() - 1
        group_bits = total_bits - 4
        batch_bits = KEPT.bit_length() - 1
        groups = devices_mode // (4 * KEPT)
        span = 2 * shared_rows
        outer = SHARED // (span * groups)
        half_join = join_width // 2

        def left_trader(piece, bit_number):
            return partner(piece, "mode", bit_number)

        def right_trader(piece, bit_number):
            return partner(piece, "mode", bit_number)

        left_buffer = left_part.reshape(2, local_rows, outer, groups, span).transpose(3, 0, 1, 2, 4)
        left_buffer = left_buffer.reshape((2,) * group_bits + (1, 2, local_rows, outer, span))
        left_buffer = jnp.broadcast_to(
            left_buffer, (2,) * group_bits + (2, 2, local_rows, outer, span)
        )
        left_bits = [group_bits - position for position in range(group_bits)] + [0]
        left_buffer = trade_axes(left_buffer, left_bits, left_trader, device_index)
        left_block = left_buffer.reshape(devices_mode // (2 * KEPT), 2, local_rows, outer * span)
        left_block = left_block.transpose(1, 0, 2, 3).reshape(2, half_join, SHARED // groups)
        right_buffer = right_part.reshape(2, shared_rows, KEPT, 2, half_join).transpose(
            2, 3, 0, 1, 4
        )
        right_buffer = right_buffer.reshape((2,) * batch_bits + (1, 2, 2, shared_rows, half_join))
        right_buffer = jnp.broadcast_to(
            right_buffer, (2,) * batch_bits + (2, 2, 2, shared_rows, half_join)
        )
        right_bits = [total_bits - 1 - position for position in range(batch_bits)] + [
            total_bits - batch_bits - 1,
            0,
        ]
        right_buffer = trade_axes(right_buffer, right_bits, right_trader, device_index)
        right_block = right_buffer.reshape(2 * KEPT, 2, 2, shared_rows, half_join)
        right_block = right_block.transpose(2, 0, 1, 3, 4).reshape(2, SHARED // groups, half_join)
        running = complex_rows(left_block[0], left_block[1], right_block[0], right_block[1])
        for position in range(group_bits):
            bit_number = group_bits - position
            own_bit = read_bit(device_index, bit_number)
            row_count = running.shape[0]
            halves = running.reshape(2, row_count // 2, 2, half_join)
            kept_half = lax.dynamic_index_in_dim(halves, own_bit, 0, keepdims=False)
            sent_half = lax.dynamic_index_in_dim(halves, 1 - own_bit, 0, keepdims=False)
            running = kept_half + partner(
                sent_half.astype(jnp.bfloat16), "mode", bit_number
            ).astype(sent_half.dtype)
        rounded = (running * join_scale).astype(jnp.bfloat16)
        own_bit = read_bit(device_index, 0)
        halves = rounded.reshape(2, local_rows, 2, half_join)
        kept_half = lax.dynamic_index_in_dim(halves, own_bit, 0, keepdims=False)
        sent_half = lax.dynamic_index_in_dim(halves, 1 - own_bit, 0, keepdims=False)
        received = partner(sent_half, "mode", 0)
        first_half = jnp.where(own_bit == 0, kept_half, received)
        second_half = jnp.where(own_bit == 0, received, kept_half)
        finished = jnp.concatenate([first_half, second_half], axis=2)
        results.append(finished)
    return jnp.stack(results)


def local(branch_in, column_order, gate_a, gate_b):
    branches, _, rows_each, width = branch_in.shape
    if branches == 4 and tiles_fit(lax.axis_size("mode"), rows_each, width):
        return fast(branch_in, column_order, gate_a, gate_b)
    return general(branch_in, column_order, gate_a, gate_b)


def solution(mesh):
    in_specs = (
        P(None, None, ("cuts", "mode"), None),
        P(),
        P(None, "mode", None),
        P(None, "mode", None),
    )
    out_specs = P(None, ("cuts", "mode"), None, None)
    return jax.shard_map(local, mesh=mesh, in_specs=in_specs, out_specs=out_specs, check_vma=False)
```

```python
import functools

import jax
import jax.numpy as jnp
from jax import lax
from jax.experimental import pallas as pl
from jax.experimental.pallas import tpu as pltpu
from jax.sharding import PartitionSpec as P

SHARED = 4096
KEPT = 4
CYCLES = 2
LANES = 128
MEBI = 1024 * 1024


def whole(count):
    return [pl.BlockSpec(memory_space=pltpu.VMEM)] * count


def one_hot(shape, axis, wanted):
    return (lax.broadcasted_iota(jnp.int32, shape, axis) == wanted).astype(jnp.bfloat16)


def exact_dot(left, right):
    return jnp.dot(left, right, preferred_element_type=jnp.float32)


def pack_kernel(qs, x_ref, order_ref, left_ref, right_ref):
    _, parts, rows_each, width = x_ref.shape
    rows = parts * rows_each
    step = min(256, width)
    new = lax.broadcasted_iota(jnp.int32, (rows, rows), 0)
    e, k, q = new // (parts * qs), new // qs % parts, new % qs
    pack = one_hot((rows, rows), 1, k * rows_each + e * qs + q)
    for branch in range(x_ref.shape[0]):
        o_ref = (left_ref, right_ref)[branch % 2]
        place = branch // 2 * rows
        packed = exact_dot(pack, x_ref[branch].reshape(rows, width)).astype(jnp.bfloat16)
        for start in range(0, width, step):
            picks = one_hot((width, step), 0, order_ref[branch : branch + 1, start : start + step])
            o_ref[place : place + rows, start : start + step] = exact_dot(packed, picks).astype(jnp.bfloat16)


def swap_sign(tiles, qs):
    turned = pltpu.roll(tiles, qs, 1)
    row = lax.broadcasted_iota(jnp.int32, (1,) + tiles.shape[1:], 1)
    return turned * jnp.where(row < qs, -1.0, 1.0)


def regroup_store(acc, first_lane, group, devices, tile_rows, x_ref):
    width = x_ref.shape[1] // 2
    per = LANES // group
    lane = lax.broadcasted_iota(jnp.int32, (tile_rows, LANES), 1) // group
    for offset in range(0, acc.shape[1], LANES):
        tile = acc[:, offset : offset + LANES].reshape(devices, tile_rows, LANES)
        row_start = (first_lane + offset) // group * tile_rows
        for block in range(devices // per):
            parts = [tile[block * per + m] for m in range(per)]
            bit = 1
            while bit < per:
                moved = list(parts)
                keep = (lane // bit) % 2 == 0
                for m in range(per):
                    if m & bit:
                        continue
                    low, high = parts[m], parts[m | bit]
                    if 2 * bit * group == LANES:
                        up = down = pltpu.roll(jnp.where(keep, high, low), LANES // 2, 1)
                    else:
                        up, down = pltpu.roll(high, bit * group, 1), pltpu.roll(low, LANES - bit * group, 1)
                    moved[m] = jnp.where(keep, low, up)
                    moved[m | bit] = jnp.where(keep, down, high)
                parts = moved
                bit *= 2
            tiles = jnp.stack(parts)
            rows = pl.ds(row_start, per * tile_rows)
            lanes = pl.ds(block * LANES, LANES)
            x_ref[rows, lanes] = tiles.reshape(per * tile_rows, LANES).astype(jnp.bfloat16)
            turned = swap_sign(tiles, tile_rows // 2)
            x_ref[rows, pl.ds(width + block * LANES, LANES)] = turned.reshape(per * tile_rows, LANES).astype(jnp.bfloat16)


def gate_copies(plan, blocks, whole_ref, sems):
    me = lax.axis_index("mode")
    copies = ([], [])
    for (sources, gates), block in zip(plan, blocks):
        for place, source in enumerate(sources):
            device = me
            for bit in source:
                device = device + (1 - 2 * (me // 2**bit % 2)) * 2**bit
            size = block.shape[3]
            rows = pl.ds(pl.multiple_of(device * size, size), size)
            for position, gate in enumerate(gates):
                sem = sems.at[gate, len(copies[gate])]
                copies[gate].append(
                    pltpu.make_async_copy(block.at[position, place], whole_ref.at[gate, :, rows, :], sem)
                )
    return copies


def layers_kernel(sizes, is_left, plan, x_ref, *refs):
    devices, qs, group, rows_each = sizes
    blocks, (o_ref, xs, last, whole_ref, sems) = refs[: len(plan)], refs[len(plan) :]
    copies = gate_copies(plan, blocks, whole_ref, sems)
    for gate in range(2):
        for copy in copies[gate]:
            copy.start()
    tile_rows = 2 * qs
    rows, width = x_ref.shape
    first = x_ref[...].astype(jnp.float32).reshape(devices, tile_rows, width)
    xs[0, :, :width] = x_ref[...]
    xs[0, :, width:] = swap_sign(first, qs).reshape(rows, width).astype(jnp.bfloat16)
    step = min(512, width)
    for layer in range(2 * CYCLES):
        if layer < 2:
            for copy in copies[layer]:
                copy.wait()
        gate = whole_ref.at[layer % 2]
        here, later = xs.at[layer % 2], xs.at[(layer + 1) % 2]
        for start in range(0, width, step):
            cols = slice(start, start + step)
            acc = exact_dot(here[...], gate[:, :, cols].reshape(2 * width, step))
            if layer < 2 * CYCLES - 1:
                regroup_store(acc, start, group, devices, tile_rows, later)
            else:
                last[:, cols] = acc.astype(jnp.bfloat16)
    half = rows // 2
    new = lax.broadcasted_iota(jnp.int32, (rows, rows), 0)
    part, inner = new // half, new % half
    if is_left:
        v, r = inner // devices, inner % devices
        picks = one_hot((rows, rows), 1, r * tile_rows + part * qs + v)
        moved = exact_dot(picks, last[...]).astype(jnp.bfloat16)
        span = 2 * rows_each
        each = width * qs // rows_each
        words = width // span
        step = min(256, width)
        for start in range(0, width, step):
            place = start + lax.broadcasted_iota(jnp.int32, (width, step), 1)
            e, rest = place // each, place % each
            h, w, qr = rest // (words * qs), rest % (words * qs) // qs, rest % qs
            lanes = one_hot((width, step), 0, w * span + (e * qs + qr) * 2 + h)
            sent = exact_dot(moved, lanes)
            low_lane = lax.broadcasted_iota(jnp.int32, (half, LANES), 1) < LANES // 2
            for offset in range(0, step, LANES):
                real = sent[:half, offset : offset + LANES]
                imag = sent[half:, offset : offset + LANES]
                e0 = (start + offset) // each
                even = jnp.where(low_lane, real, pltpu.roll(imag, LANES // 2, 1))
                odd = jnp.where(low_lane, pltpu.roll(real, LANES // 2, 1), imag)
                o_ref[e0 * half : (e0 + 1) * half, :] = even.astype(jnp.bfloat16)
                o_ref[(e0 + 1) * half : (e0 + 2) * half, :] = odd.astype(jnp.bfloat16)
    else:
        r, q = inner // qs, inner % qs
        picks = one_hot((rows, rows), 1, r * tile_rows + part * qs + q)
        o_ref[...] = exact_dot(picks, last[...]).astype(jnp.bfloat16)


def join_kernel(sizes, left_ref, right_ref, o_ref):
    devices, us, vs = sizes
    rows = us * devices
    free = right_ref.shape[1] // (2 * KEPT)
    left = left_ref[...].reshape(us, vs, devices, LANES)
    left = jnp.concatenate([left[:, v].reshape(rows, LANES) for v in range(vs)], axis=1)
    new = lax.broadcasted_iota(jnp.int32, (rows, rows), 0)
    picks = one_hot((rows, rows), 1, new % us * devices + new // us)
    left = exact_dot(picks, left).astype(jnp.bfloat16)
    half = right_ref.shape[0] // 2
    depth = half // vs
    real, imag = right_ref[:half, :], right_ref[half:, :]
    block = rows // KEPT
    for g in range(KEPT):
        stack = []
        for v in range(vs):
            r = [real[v * depth : (v + 1) * depth, (h * KEPT + g) * free :][:, :free] for h in range(2)]
            i = [imag[v * depth : (v + 1) * depth, (h * KEPT + g) * free :][:, :free] for h in range(2)]
            to_real = jnp.concatenate([r[0], r[1], -i[0], -i[1]], axis=0)
            to_imag = jnp.concatenate([i[0], i[1], r[0], r[1]], axis=0)
            stack.append(jnp.concatenate([to_real, to_imag], axis=1))
        stack = jnp.concatenate(stack, axis=0)
        part = exact_dot(left[g * block : (g + 1) * block, :], stack)
        o_ref[g * block : (g + 1) * block, :] = part.astype(jnp.bfloat16)


def call(kernel, out_shape, inputs, scratch=(), flops=0, blocks=(), grant=24, outputs=0):
    moved = sum(x.size * x.dtype.itemsize for x in (*inputs, *blocks))
    out = jax.ShapeDtypeStruct(out_shape, jnp.bfloat16)
    return pl.pallas_call(
        kernel,
        out_shape=[out] * outputs if outputs else out,
        in_specs=whole(len(inputs)) + [pl.BlockSpec(memory_space=pl.ANY)] * len(blocks),
        out_specs=whole(outputs) if outputs else whole(1)[0],
        scratch_shapes=list(scratch),
        compiler_params=pltpu.CompilerParams(vmem_limit_bytes=grant * MEBI),
        cost_estimate=pl.CostEstimate(flops=flops, bytes_accessed=moved, transcendentals=0),
    )(*inputs, *blocks)


def tiles_fit(devices, rows_each, width):
    pair_devices = devices // 2
    if devices < 4 or devices & (devices - 1) or rows_each % pair_devices or width % 256:
        return False
    qs, group = rows_each // pair_devices, width // devices
    return (
        2 * qs == 8
        and LANES % group == 0
        and devices % (LANES // group) == 0
        and qs == SHARED // width
        and devices % 32 == 0
        and 2 * width * qs // rows_each == LANES
        and devices * rows_each * width // SHARED % (KEPT * LANES) == 0
        and 2 * (devices * rows_each * width // SHARED) == width
    )


def fast(branch_in, column_order, gate_a, gate_b):
    devices = lax.axis_size("mode")
    rows_each, width = branch_in.shape[2:]
    halves = devices // 2
    qs, group = rows_each // halves, width // devices
    tile_rows = 2 * qs
    rows = devices * tile_rows
    packed = call(
        functools.partial(pack_kernel, qs),
        (rows, width),
        (branch_in, column_order),
        flops=8 * rows * width * width,
        outputs=2,
    )
    packed = [side.reshape(devices, tile_rows, width) for side in packed]
    blocks, plan, *states = spread(gate_a, gate_b, packed)
    states = [state.reshape(rows, width) for state in states]
    sizes = (devices, qs, group, rows_each)
    scratch = [
        pltpu.VMEM((2, rows, 2 * width), jnp.bfloat16),
        pltpu.VMEM((rows, width), jnp.bfloat16),
        pltpu.VMEM((2, 2, width, width), jnp.bfloat16),
        pltpu.SemaphoreType.DMA((2, devices)),
    ]
    work = 2 * CYCLES * 4 * rows * width * width
    left = call(
        functools.partial(layers_kernel, sizes, True, plan),
        (halves * rows // 2, LANES),
        (states[0],),
        scratch,
        work,
        blocks,
        56,
    )
    groups = [[h * halves + e for e in range(halves)] for h in range(2)]
    left = trade(left.reshape(halves, rows // 2, LANES), groups)
    right = call(
        functools.partial(layers_kernel, sizes, False, plan), (rows, width), (states[1],), scratch, work, blocks, 56
    )
    free = width // (2 * KEPT)
    us = halves
    partial_sums = call(
        functools.partial(join_kernel, (devices, us, qs)),
        (devices * us, 2 * free),
        (left.reshape(halves * rows // 2, LANES), right),
        flops=2 * devices * us * LANES * qs * 2 * free,
    )
    parts = trade(partial_sums.reshape(devices, us, 2 * free))
    parts = parts.reshape(2, halves, us, 2 * free).astype(jnp.float32)
    join_scale = (2.0 * SHARED) ** (-0.5)
    return (jnp.sum(parts, axis=1) * join_scale).astype(jnp.bfloat16).reshape(2, us, 2, free)


def flip(value, *bits):
    mask = sum(2**bit for bit in bits)
    pairs = [(source, source ^ mask) for source in range(lax.axis_size("mode"))]
    return lax.ppermute(value, "mode", pairs)


def plane(value, sources):
    over_x, over_y = flip(value, 1), flip(value, 2)
    diagonal = flip(over_x[:1], 2), flip(over_y[1:], 1)
    turned = [tuple(source + more for source in sources) for more in ((1,), (2,), (1, 2))]
    return [
        (value, sources, (0, 1)),
        (over_x, turned[0], (0, 1)),
        (over_y, turned[1], (0, 1)),
        (diagonal[0], turned[2], (0,)),
        (diagonal[1], turned[2], (1,)),
    ]


def spread(gate_a, gate_b, packed):
    bits = lax.axis_size("mode").bit_length() - 1
    own = jnp.stack([gate_a, gate_b])[:, None]
    far = [()]
    for bit in range(3, bits):
        far += [source + (bit,) for source in far]
    came = [flip(own, *source) for source in far[1:]]
    left, *rest = lax.optimization_barrier((packed[0], *came[1:]))
    sets = [(own, ((),)), (came[0], tuple(far[1:2]))]
    if rest:
        sets.append((jnp.concatenate(rest, axis=1), tuple(far[2:])))
    blocks = []
    for number, (value, sources) in enumerate(sets):
        if number:
            value, *_ = lax.optimization_barrier((value, *packed, blocks[-2][0], blocks[-1][0]))
        blocks += plane(value, sources)
    right, *_ = lax.optimization_barrier((packed[1], blocks[-2][0], blocks[-1][0]))
    last = len(blocks) - 2
    near = []
    for number, (value, sources, gates) in enumerate(blocks):
        if number >= last:
            value, *_ = lax.optimization_barrier((value, *[earlier for earlier, _, _ in near[:last]]))
        near.append((flip(value, 0), tuple(source + (0,) for source in sources), gates))
    blocks += near
    plan = tuple((sources, gates) for _, sources, gates in blocks)
    return [value for value, _, _ in blocks], plan, trade(left), trade(right)


def trade(value, groups=None):
    return lax.all_to_all(value, "mode", split_axis=0, concat_axis=0, axis_index_groups=groups, tiled=True)


def partner(value, axis, bit):
    mask = 2**bit
    pairs = [(source, source ^ mask) for source in range(lax.axis_size(axis))]
    return lax.ppermute(value, axis, pairs)


def product_four(states, layer_block):
    branches, parts, row_count, width = states.shape
    real_in = states[:, 0].reshape(branches * row_count, width)
    imag_in = states[:, 1].reshape(branches * row_count, width)
    real_part = jnp.dot(real_in, layer_block[0], preferred_element_type=jnp.float32) - jnp.dot(
        imag_in, layer_block[1], preferred_element_type=jnp.float32
    )
    imag_part = jnp.dot(real_in, layer_block[1], preferred_element_type=jnp.float32) + jnp.dot(
        imag_in, layer_block[0], preferred_element_type=jnp.float32
    )
    joined_parts = jnp.stack(
        [
            real_part.reshape(branches, row_count, width),
            imag_part.reshape(branches, row_count, width),
        ],
        axis=1,
    )
    return joined_parts.astype(jnp.bfloat16)


def complex_rows(left_real, left_imag, right_real, right_imag):
    real_part = jnp.dot(left_real, right_real, preferred_element_type=jnp.float32) - jnp.dot(
        left_imag, right_imag, preferred_element_type=jnp.float32
    )
    imag_part = jnp.dot(left_real, right_imag, preferred_element_type=jnp.float32) + jnp.dot(
        left_imag, right_real, preferred_element_type=jnp.float32
    )
    return jnp.stack([real_part, imag_part], axis=1)


def read_bit(device_index, bit_number):
    return device_index // 2**bit_number % 2


def trade_axes(buffer, axis_bits, trader, device_index):
    for position, bit_number in enumerate(axis_bits):
        own_bit = read_bit(device_index, bit_number)
        kept_half = lax.dynamic_index_in_dim(buffer, own_bit, position, keepdims=False)
        sent_half = lax.dynamic_index_in_dim(buffer, 1 - own_bit, position, keepdims=False)
        received = trader(sent_half, bit_number)
        first_half = jnp.where(own_bit == 0, kept_half, received)
        second_half = jnp.where(own_bit == 0, received, kept_half)
        buffer = jnp.stack([first_half, second_half], axis=position)
    return buffer


def general(branch_in, column_order, gate_a, gate_b):
    join_scale = (2.0 * SHARED) ** (-0.5)
    devices_mode = lax.axis_size("mode")
    whole_a, whole_b = (
        lax.all_gather(gate_a, "mode", axis=1, tiled=True),
        lax.all_gather(gate_b, "mode", axis=1, tiled=True),
    )
    states = jnp.take_along_axis(branch_in, column_order[:, None, None, :], axis=3)
    for layer_number in range(2 * CYCLES):
        if layer_number > 0:
            states = lax.all_to_all(states, "mode", split_axis=3, concat_axis=3, tiled=True)
        states = product_four(states, whole_a if layer_number % 2 == 0 else whole_b)
    local_cells = states.shape[2] * states.shape[3]
    local_rows = local_cells // SHARED
    shared_rows = SHARED // devices_mode
    join_width = local_cells // (shared_rows * KEPT)
    results = []
    for pair_number in range(2):
        left_part = states[2 * pair_number].reshape(2, local_rows, SHARED)
        right_part = states[2 * pair_number + 1].reshape(2, shared_rows, KEPT, join_width)
        device_index = lax.axis_index("mode")
        total_bits = devices_mode.bit_length() - 1
        group_bits = total_bits - 4
        batch_bits = KEPT.bit_length() - 1
        groups = devices_mode // (4 * KEPT)
        span = 2 * shared_rows
        outer = SHARED // (span * groups)
        half_join = join_width // 2

        def left_trader(piece, bit_number):
            return partner(piece, "mode", bit_number)

        def right_trader(piece, bit_number):
            return partner(piece, "mode", bit_number)

        left_buffer = left_part.reshape(2, local_rows, outer, groups, span).transpose(3, 0, 1, 2, 4)
        left_buffer = left_buffer.reshape((2,) * group_bits + (1, 2, local_rows, outer, span))
        left_buffer = jnp.broadcast_to(
            left_buffer, (2,) * group_bits + (2, 2, local_rows, outer, span)
        )
        left_bits = [group_bits - position for position in range(group_bits)] + [0]
        left_buffer = trade_axes(left_buffer, left_bits, left_trader, device_index)
        left_block = left_buffer.reshape(devices_mode // (2 * KEPT), 2, local_rows, outer * span)
        left_block = left_block.transpose(1, 0, 2, 3).reshape(2, half_join, SHARED // groups)
        right_buffer = right_part.reshape(2, shared_rows, KEPT, 2, half_join).transpose(
            2, 3, 0, 1, 4
        )
        right_buffer = right_buffer.reshape((2,) * batch_bits + (1, 2, 2, shared_rows, half_join))
        right_buffer = jnp.broadcast_to(
            right_buffer, (2,) * batch_bits + (2, 2, 2, shared_rows, half_join)
        )
        right_bits = [total_bits - 1 - position for position in range(batch_bits)] + [
            total_bits - batch_bits - 1,
            0,
        ]
        right_buffer = trade_axes(right_buffer, right_bits, right_trader, device_index)
        right_block = right_buffer.reshape(2 * KEPT, 2, 2, shared_rows, half_join)
        right_block = right_block.transpose(2, 0, 1, 3, 4).reshape(2, SHARED // groups, half_join)
        running = complex_rows(left_block[0], left_block[1], right_block[0], right_block[1])
        for position in range(group_bits):
            bit_number = group_bits - position
            own_bit = read_bit(device_index, bit_number)
            row_count = running.shape[0]
            halves = running.reshape(2, row_count // 2, 2, half_join)
            kept_half = lax.dynamic_index_in_dim(halves, own_bit, 0, keepdims=False)
            sent_half = lax.dynamic_index_in_dim(halves, 1 - own_bit, 0, keepdims=False)
            running = kept_half + partner(
                sent_half.astype(jnp.bfloat16), "mode", bit_number
            ).astype(sent_half.dtype)
        rounded = (running * join_scale).astype(jnp.bfloat16)
        own_bit = read_bit(device_index, 0)
        halves = rounded.reshape(2, local_rows, 2, half_join)
        kept_half = lax.dynamic_index_in_dim(halves, own_bit, 0, keepdims=False)
        sent_half = lax.dynamic_index_in_dim(halves, 1 - own_bit, 0, keepdims=False)
        received = partner(sent_half, "mode", 0)
        first_half = jnp.where(own_bit == 0, kept_half, received)
        second_half = jnp.where(own_bit == 0, received, kept_half)
        finished = jnp.concatenate([first_half, second_half], axis=2)
        results.append(finished)
    return jnp.stack(results)


def local(branch_in, column_order, gate_a, gate_b):
    branches, _, rows_each, width = branch_in.shape
    if branches == 4 and tiles_fit(lax.axis_size("mode"), rows_each, width):
        return fast(branch_in, column_order, gate_a, gate_b)
    return general(branch_in, column_order, gate_a, gate_b)


def solution(mesh):
    in_specs = (
        P(None, None, ("cuts", "mode"), None),
        P(),
        P(None, "mode", None),
        P(None, "mode", None),
    )
    out_specs = P(None, ("cuts", "mode"), None, None)
    return jax.shard_map(local, mesh=mesh, in_specs=in_specs, out_specs=out_specs, check_vma=False)
```

```python
import functools

import jax
import jax.numpy as jnp
from jax import lax
from jax.experimental import pallas as pl
from jax.experimental.pallas import tpu as pltpu
from jax.sharding import PartitionSpec as P

SHARED = 4096
KEPT = 4
CYCLES = 2
LANES = 128
MEBI = 1024 * 1024


def whole(count):
    return [pl.BlockSpec(memory_space=pltpu.VMEM)] * count


def one_hot(shape, axis, wanted):
    return (lax.broadcasted_iota(jnp.int32, shape, axis) == wanted).astype(jnp.bfloat16)


def exact_dot(left, right):
    return jnp.dot(left, right, preferred_element_type=jnp.float32)


def pack_kernel(qs, x_ref, order_ref, left_ref, right_ref):
    _, parts, rows_each, width = x_ref.shape
    rows = parts * rows_each
    step = min(256, width)
    new = lax.broadcasted_iota(jnp.int32, (rows, rows), 0)
    e, k, q = new // (parts * qs), new // qs % parts, new % qs
    pack = one_hot((rows, rows), 1, k * rows_each + e * qs + q)
    for branch in range(x_ref.shape[0]):
        o_ref = (left_ref, right_ref)[branch % 2]
        place = branch // 2 * rows
        packed = exact_dot(pack, x_ref[branch].reshape(rows, width)).astype(jnp.bfloat16)
        for start in range(0, width, step):
            picks = one_hot((width, step), 0, order_ref[branch : branch + 1, start : start + step])
            o_ref[place : place + rows, start : start + step] = exact_dot(packed, picks).astype(jnp.bfloat16)


def swap_sign(tiles, qs):
    turned = pltpu.roll(tiles, qs, 1)
    row = lax.broadcasted_iota(jnp.int32, (1,) + tiles.shape[1:], 1)
    return turned * jnp.where(row < qs, -1.0, 1.0)


def regroup_store(acc, first_lane, group, devices, tile_rows, x_ref):
    width = x_ref.shape[1] // 2
    per = LANES // group
    lane = lax.broadcasted_iota(jnp.int32, (tile_rows, LANES), 1) // group
    for offset in range(0, acc.shape[1], LANES):
        tile = acc[:, offset : offset + LANES].reshape(devices, tile_rows, LANES)
        row_start = (first_lane + offset) // group * tile_rows
        for block in range(devices // per):
            parts = [tile[block * per + m] for m in range(per)]
            bit = 1
            while bit < per:
                moved = list(parts)
                keep = (lane // bit) % 2 == 0
                for m in range(per):
                    if m & bit:
                        continue
                    low, high = parts[m], parts[m | bit]
                    if 2 * bit * group == LANES:
                        up = down = pltpu.roll(jnp.where(keep, high, low), LANES // 2, 1)
                    else:
                        up, down = pltpu.roll(high, bit * group, 1), pltpu.roll(low, LANES - bit * group, 1)
                    moved[m] = jnp.where(keep, low, up)
                    moved[m | bit] = jnp.where(keep, down, high)
                parts = moved
                bit *= 2
            tiles = jnp.stack(parts)
            rows = pl.ds(row_start, per * tile_rows)
            lanes = pl.ds(block * LANES, LANES)
            x_ref[rows, lanes] = tiles.reshape(per * tile_rows, LANES).astype(jnp.bfloat16)
            turned = swap_sign(tiles, tile_rows // 2)
            x_ref[rows, pl.ds(width + block * LANES, LANES)] = turned.reshape(per * tile_rows, LANES).astype(jnp.bfloat16)


def gate_copies(plan, blocks, whole_ref, sems):
    me = lax.axis_index("mode")
    copies = ([], [])
    for (sources, gates), block in zip(plan, blocks):
        for place, source in enumerate(sources):
            device = me
            for bit in source:
                device = device + (1 - 2 * (me // 2**bit % 2)) * 2**bit
            size = block.shape[3]
            rows = pl.ds(pl.multiple_of(device * size, size), size)
            for position, gate in enumerate(gates):
                sem = sems.at[gate, len(copies[gate])]
                copies[gate].append(
                    pltpu.make_async_copy(block.at[position, place], whole_ref.at[gate, :, rows, :], sem)
                )
    return copies


def layers_kernel(sizes, is_left, plan, x_ref, *refs):
    devices, qs, group, rows_each = sizes
    blocks, (o_ref, xs, last, whole_ref, sems) = refs[: len(plan)], refs[len(plan) :]
    copies = gate_copies(plan, blocks, whole_ref, sems)
    for gate in range(2):
        for copy in copies[gate]:
            copy.start()
    tile_rows = 2 * qs
    rows, width = x_ref.shape
    first = x_ref[...].astype(jnp.float32).reshape(devices, tile_rows, width)
    xs[0, :, :width] = x_ref[...]
    xs[0, :, width:] = swap_sign(first, qs).reshape(rows, width).astype(jnp.bfloat16)
    step = min(512, width)
    for layer in range(2 * CYCLES):
        if layer < 2:
            for copy in copies[layer]:
                copy.wait()
        gate = whole_ref.at[layer % 2]
        here, later = xs.at[layer % 2], xs.at[(layer + 1) % 2]
        for start in range(0, width, step):
            cols = slice(start, start + step)
            acc = exact_dot(here[...], gate[:, :, cols].reshape(2 * width, step))
            if layer < 2 * CYCLES - 1:
                regroup_store(acc, start, group, devices, tile_rows, later)
            else:
                last[:, cols] = acc.astype(jnp.bfloat16)
    half = rows // 2
    new = lax.broadcasted_iota(jnp.int32, (rows, rows), 0)
    part, inner = new // half, new % half
    if is_left:
        v, r = inner // devices, inner % devices
        picks = one_hot((rows, rows), 1, r * tile_rows + part * qs + v)
        moved = exact_dot(picks, last[...]).astype(jnp.bfloat16)
        span = 2 * rows_each
        each = width * qs // rows_each
        words = width // span
        step = min(256, width)
        for start in range(0, width, step):
            place = start + lax.broadcasted_iota(jnp.int32, (width, step), 1)
            e, rest = place // each, place % each
            h, w, qr = rest // (words * qs), rest % (words * qs) // qs, rest % qs
            lanes = one_hot((width, step), 0, w * span + (e * qs + qr) * 2 + h)
            sent = exact_dot(moved, lanes)
            low_lane = lax.broadcasted_iota(jnp.int32, (half, LANES), 1) < LANES // 2
            for offset in range(0, step, LANES):
                real = sent[:half, offset : offset + LANES]
                imag = sent[half:, offset : offset + LANES]
                e0 = (start + offset) // each
                even = jnp.where(low_lane, real, pltpu.roll(imag, LANES // 2, 1))
                odd = jnp.where(low_lane, pltpu.roll(real, LANES // 2, 1), imag)
                o_ref[e0 * half : (e0 + 1) * half, :] = even.astype(jnp.bfloat16)
                o_ref[(e0 + 1) * half : (e0 + 2) * half, :] = odd.astype(jnp.bfloat16)
    else:
        r, q = inner // qs, inner % qs
        picks = one_hot((rows, rows), 1, r * tile_rows + part * qs + q)
        o_ref[...] = exact_dot(picks, last[...]).astype(jnp.bfloat16)


def join_kernel(sizes, left_ref, right_ref, o_ref):
    devices, us, vs = sizes
    rows = us * devices
    free = right_ref.shape[1] // (2 * KEPT)
    left = left_ref[...].reshape(us, vs, devices, LANES)
    left = jnp.concatenate([left[:, v].reshape(rows, LANES) for v in range(vs)], axis=1)
    new = lax.broadcasted_iota(jnp.int32, (rows, rows), 0)
    picks = one_hot((rows, rows), 1, new % us * devices + new // us)
    left = exact_dot(picks, left).astype(jnp.bfloat16)
    half = right_ref.shape[0] // 2
    depth = half // vs
    real, imag = right_ref[:half, :], right_ref[half:, :]
    block = rows // KEPT
    for g in range(KEPT):
        stack = []
        for v in range(vs):
            r = [real[v * depth : (v + 1) * depth, (h * KEPT + g) * free :][:, :free] for h in range(2)]
            i = [imag[v * depth : (v + 1) * depth, (h * KEPT + g) * free :][:, :free] for h in range(2)]
            to_real = jnp.concatenate([r[0], r[1], -i[0], -i[1]], axis=0)
            to_imag = jnp.concatenate([i[0], i[1], r[0], r[1]], axis=0)
            stack.append(jnp.concatenate([to_real, to_imag], axis=1))
        stack = jnp.concatenate(stack, axis=0)
        part = exact_dot(left[g * block : (g + 1) * block, :], stack)
        o_ref[g * block : (g + 1) * block, :] = part.astype(jnp.bfloat16)


def call(kernel, out_shape, inputs, scratch=(), flops=0, blocks=(), grant=24, outputs=0):
    moved = sum(x.size * x.dtype.itemsize for x in (*inputs, *blocks))
    out = jax.ShapeDtypeStruct(out_shape, jnp.bfloat16)
    return pl.pallas_call(
        kernel,
        out_shape=[out] * outputs if outputs else out,
        in_specs=whole(len(inputs)) + [pl.BlockSpec(memory_space=pl.ANY)] * len(blocks),
        out_specs=whole(outputs) if outputs else whole(1)[0],
        scratch_shapes=list(scratch),
        compiler_params=pltpu.CompilerParams(vmem_limit_bytes=grant * MEBI),
        cost_estimate=pl.CostEstimate(flops=flops, bytes_accessed=moved, transcendentals=0),
    )(*inputs, *blocks)


def tiles_fit(devices, rows_each, width):
    pair_devices = devices // 2
    if devices < 4 or devices & (devices - 1) or rows_each % pair_devices or width % 256:
        return False
    qs, group = rows_each // pair_devices, width // devices
    return (
        2 * qs == 8
        and LANES % group == 0
        and devices % (LANES // group) == 0
        and qs == SHARED // width
        and devices % 32 == 0
        and 2 * width * qs // rows_each == LANES
        and devices * rows_each * width // SHARED % (KEPT * LANES) == 0
        and 2 * (devices * rows_each * width // SHARED) == width
    )


def fast(branch_in, column_order, gate_a, gate_b):
    devices = lax.axis_size("mode")
    rows_each, width = branch_in.shape[2:]
    halves = devices // 2
    qs, group = rows_each // halves, width // devices
    tile_rows = 2 * qs
    rows = devices * tile_rows
    packed = call(
        functools.partial(pack_kernel, qs),
        (rows, width),
        (branch_in, column_order),
        flops=8 * rows * width * width,
        outputs=2,
    )
    packed = [side.reshape(devices, tile_rows, width) for side in packed]
    blocks, plan, *states = spread(gate_a, gate_b, packed)
    states = [state.reshape(rows, width) for state in states]
    sizes = (devices, qs, group, rows_each)
    scratch = [
        pltpu.VMEM((2, rows, 2 * width), jnp.bfloat16),
        pltpu.VMEM((rows, width), jnp.bfloat16),
        pltpu.VMEM((2, 2, width, width), jnp.bfloat16),
        pltpu.SemaphoreType.DMA((2, devices)),
    ]
    work = 2 * CYCLES * 4 * rows * width * width
    left = call(
        functools.partial(layers_kernel, sizes, True, plan),
        (halves * rows // 2, LANES),
        (states[0],),
        scratch,
        work,
        blocks,
        56,
    )
    groups = [[h * halves + e for e in range(halves)] for h in range(2)]
    left = trade(left.reshape(halves, rows // 2, LANES), groups)
    right = call(
        functools.partial(layers_kernel, sizes, False, plan), (rows, width), (states[1],), scratch, work, blocks, 56
    )
    free = width // (2 * KEPT)
    us = halves
    partial_sums = call(
        functools.partial(join_kernel, (devices, us, qs)),
        (devices * us, 2 * free),
        (left.reshape(halves * rows // 2, LANES), right),
        flops=2 * devices * us * LANES * qs * 2 * free,
    )
    parts = trade(partial_sums.reshape(devices, us, 2 * free))
    parts = parts.reshape(2, halves, us, 2 * free).astype(jnp.float32)
    join_scale = (2.0 * SHARED) ** (-0.5)
    return (jnp.sum(parts, axis=1) * join_scale).astype(jnp.bfloat16).reshape(2, us, 2, free)


def flip(value, *bits):
    mask = sum(2**bit for bit in bits)
    pairs = [(source, source ^ mask) for source in range(lax.axis_size("mode"))]
    return lax.ppermute(value, "mode", pairs)


def plane(value, sources):
    over_x, over_y = flip(value, 1), flip(value, 2)
    diagonal = flip(over_x[:1], 2), flip(over_y[1:], 1)
    turned = [tuple(source + more for source in sources) for more in ((1,), (2,), (1, 2))]
    return [
        (value, sources, (0, 1)),
        (over_x, turned[0], (0, 1)),
        (over_y, turned[1], (0, 1)),
        (diagonal[0], turned[2], (0,)),
        (diagonal[1], turned[2], (1,)),
    ]


def spread(gate_a, gate_b, packed):
    bits = lax.axis_size("mode").bit_length() - 1
    own = jnp.stack([gate_a, gate_b])[:, None]
    far = [()]
    for bit in range(3, bits):
        far += [source + (bit,) for source in far]
    came = [flip(own, *source) for source in far[1:]]
    sets = [(own, ((),)), (jnp.concatenate(came[:2], axis=1), tuple(far[1:3]))]
    if came[2:]:
        sets.append((jnp.concatenate(came[2:], axis=1), tuple(far[3:])))
    blocks = []
    for number, (value, sources) in enumerate(sets):
        if number:
            tied = (*packed, blocks[3][0], blocks[4][0]) if number == 1 else (blocks[6][0], blocks[7][0])
            value, *_ = lax.optimization_barrier((value, *tied))
        blocks += plane(value, sources)
    left, *_ = lax.optimization_barrier((packed[0], *came[2:], blocks[8][0], blocks[9][0]))
    right, *_ = lax.optimization_barrier((packed[1], blocks[-2][0], blocks[-1][0]))
    last = len(blocks) - 2
    near = []
    for number, (value, sources, gates) in enumerate(blocks):
        if number >= last:
            value, *_ = lax.optimization_barrier((value, *[earlier for earlier, _, _ in near[:last]]))
        near.append((flip(value, 0), tuple(source + (0,) for source in sources), gates))
    blocks += near
    plan = tuple((sources, gates) for _, sources, gates in blocks)
    return [value for value, _, _ in blocks], plan, trade(left), trade(right)


def trade(value, groups=None):
    return lax.all_to_all(value, "mode", split_axis=0, concat_axis=0, axis_index_groups=groups, tiled=True)


def partner(value, axis, bit):
    mask = 2**bit
    pairs = [(source, source ^ mask) for source in range(lax.axis_size(axis))]
    return lax.ppermute(value, axis, pairs)


def product_four(states, layer_block):
    branches, parts, row_count, width = states.shape
    real_in = states[:, 0].reshape(branches * row_count, width)
    imag_in = states[:, 1].reshape(branches * row_count, width)
    real_part = jnp.dot(real_in, layer_block[0], preferred_element_type=jnp.float32) - jnp.dot(
        imag_in, layer_block[1], preferred_element_type=jnp.float32
    )
    imag_part = jnp.dot(real_in, layer_block[1], preferred_element_type=jnp.float32) + jnp.dot(
        imag_in, layer_block[0], preferred_element_type=jnp.float32
    )
    joined_parts = jnp.stack(
        [
            real_part.reshape(branches, row_count, width),
            imag_part.reshape(branches, row_count, width),
        ],
        axis=1,
    )
    return joined_parts.astype(jnp.bfloat16)


def complex_rows(left_real, left_imag, right_real, right_imag):
    real_part = jnp.dot(left_real, right_real, preferred_element_type=jnp.float32) - jnp.dot(
        left_imag, right_imag, preferred_element_type=jnp.float32
    )
    imag_part = jnp.dot(left_real, right_imag, preferred_element_type=jnp.float32) + jnp.dot(
        left_imag, right_real, preferred_element_type=jnp.float32
    )
    return jnp.stack([real_part, imag_part], axis=1)


def read_bit(device_index, bit_number):
    return device_index // 2**bit_number % 2


def trade_axes(buffer, axis_bits, trader, device_index):
    for position, bit_number in enumerate(axis_bits):
        own_bit = read_bit(device_index, bit_number)
        kept_half = lax.dynamic_index_in_dim(buffer, own_bit, position, keepdims=False)
        sent_half = lax.dynamic_index_in_dim(buffer, 1 - own_bit, position, keepdims=False)
        received = trader(sent_half, bit_number)
        first_half = jnp.where(own_bit == 0, kept_half, received)
        second_half = jnp.where(own_bit == 0, received, kept_half)
        buffer = jnp.stack([first_half, second_half], axis=position)
    return buffer


def general(branch_in, column_order, gate_a, gate_b):
    join_scale = (2.0 * SHARED) ** (-0.5)
    devices_mode = lax.axis_size("mode")
    whole_a, whole_b = (
        lax.all_gather(gate_a, "mode", axis=1, tiled=True),
        lax.all_gather(gate_b, "mode", axis=1, tiled=True),
    )
    states = jnp.take_along_axis(branch_in, column_order[:, None, None, :], axis=3)
    for layer_number in range(2 * CYCLES):
        if layer_number > 0:
            states = lax.all_to_all(states, "mode", split_axis=3, concat_axis=3, tiled=True)
        states = product_four(states, whole_a if layer_number % 2 == 0 else whole_b)
    local_cells = states.shape[2] * states.shape[3]
    local_rows = local_cells // SHARED
    shared_rows = SHARED // devices_mode
    join_width = local_cells // (shared_rows * KEPT)
    results = []
    for pair_number in range(2):
        left_part = states[2 * pair_number].reshape(2, local_rows, SHARED)
        right_part = states[2 * pair_number + 1].reshape(2, shared_rows, KEPT, join_width)
        device_index = lax.axis_index("mode")
        total_bits = devices_mode.bit_length() - 1
        group_bits = total_bits - 4
        batch_bits = KEPT.bit_length() - 1
        groups = devices_mode // (4 * KEPT)
        span = 2 * shared_rows
        outer = SHARED // (span * groups)
        half_join = join_width // 2

        def left_trader(piece, bit_number):
            return partner(piece, "mode", bit_number)

        def right_trader(piece, bit_number):
            return partner(piece, "mode", bit_number)

        left_buffer = left_part.reshape(2, local_rows, outer, groups, span).transpose(3, 0, 1, 2, 4)
        left_buffer = left_buffer.reshape((2,) * group_bits + (1, 2, local_rows, outer, span))
        left_buffer = jnp.broadcast_to(
            left_buffer, (2,) * group_bits + (2, 2, local_rows, outer, span)
        )
        left_bits = [group_bits - position for position in range(group_bits)] + [0]
        left_buffer = trade_axes(left_buffer, left_bits, left_trader, device_index)
        left_block = left_buffer.reshape(devices_mode // (2 * KEPT), 2, local_rows, outer * span)
        left_block = left_block.transpose(1, 0, 2, 3).reshape(2, half_join, SHARED // groups)
        right_buffer = right_part.reshape(2, shared_rows, KEPT, 2, half_join).transpose(
            2, 3, 0, 1, 4
        )
        right_buffer = right_buffer.reshape((2,) * batch_bits + (1, 2, 2, shared_rows, half_join))
        right_buffer = jnp.broadcast_to(
            right_buffer, (2,) * batch_bits + (2, 2, 2, shared_rows, half_join)
        )
        right_bits = [total_bits - 1 - position for position in range(batch_bits)] + [
            total_bits - batch_bits - 1,
            0,
        ]
        right_buffer = trade_axes(right_buffer, right_bits, right_trader, device_index)
        right_block = right_buffer.reshape(2 * KEPT, 2, 2, shared_rows, half_join)
        right_block = right_block.transpose(2, 0, 1, 3, 4).reshape(2, SHARED // groups, half_join)
        running = complex_rows(left_block[0], left_block[1], right_block[0], right_block[1])
        for position in range(group_bits):
            bit_number = group_bits - position
            own_bit = read_bit(device_index, bit_number)
            row_count = running.shape[0]
            halves = running.reshape(2, row_count // 2, 2, half_join)
            kept_half = lax.dynamic_index_in_dim(halves, own_bit, 0, keepdims=False)
            sent_half = lax.dynamic_index_in_dim(halves, 1 - own_bit, 0, keepdims=False)
            running = kept_half + partner(
                sent_half.astype(jnp.bfloat16), "mode", bit_number
            ).astype(sent_half.dtype)
        rounded = (running * join_scale).astype(jnp.bfloat16)
        own_bit = read_bit(device_index, 0)
        halves = rounded.reshape(2, local_rows, 2, half_join)
        kept_half = lax.dynamic_index_in_dim(halves, own_bit, 0, keepdims=False)
        sent_half = lax.dynamic_index_in_dim(halves, 1 - own_bit, 0, keepdims=False)
        received = partner(sent_half, "mode", 0)
        first_half = jnp.where(own_bit == 0, kept_half, received)
        second_half = jnp.where(own_bit == 0, received, kept_half)
        finished = jnp.concatenate([first_half, second_half], axis=2)
        results.append(finished)
    return jnp.stack(results)


def local(branch_in, column_order, gate_a, gate_b):
    branches, _, rows_each, width = branch_in.shape
    if branches == 4 and tiles_fit(lax.axis_size("mode"), rows_each, width):
        return fast(branch_in, column_order, gate_a, gate_b)
    return general(branch_in, column_order, gate_a, gate_b)


def solution(mesh):
    in_specs = (
        P(None, None, ("cuts", "mode"), None),
        P(),
        P(None, "mode", None),
        P(None, "mode", None),
    )
    out_specs = P(None, ("cuts", "mode"), None, None)
    return jax.shard_map(local, mesh=mesh, in_specs=in_specs, out_specs=out_specs, check_vma=False)
```

```python
import functools

import jax
import jax.numpy as jnp
from jax import lax
from jax.experimental import pallas as pl
from jax.experimental.pallas import tpu as pltpu
from jax.sharding import PartitionSpec as P

SHARED = 4096
KEPT = 4
CYCLES = 2
LANES = 128
MEBI = 1024 * 1024


def whole(count):
    return [pl.BlockSpec(memory_space=pltpu.VMEM)] * count


def one_hot(shape, axis, wanted):
    return (lax.broadcasted_iota(jnp.int32, shape, axis) == wanted).astype(jnp.bfloat16)


def exact_dot(left, right):
    return jnp.dot(left, right, preferred_element_type=jnp.float32)


def pack_kernel(qs, x_ref, order_ref, left_ref, right_ref):
    _, parts, rows_each, width = x_ref.shape
    rows = parts * rows_each
    step = min(256, width)
    new = lax.broadcasted_iota(jnp.int32, (rows, rows), 0)
    e, k, q = new // (parts * qs), new // qs % parts, new % qs
    pack = one_hot((rows, rows), 1, k * rows_each + e * qs + q)
    for branch in range(x_ref.shape[0]):
        o_ref = (left_ref, right_ref)[branch % 2]
        place = branch // 2 * rows
        packed = exact_dot(pack, x_ref[branch].reshape(rows, width)).astype(jnp.bfloat16)
        for start in range(0, width, step):
            picks = one_hot((width, step), 0, order_ref[branch : branch + 1, start : start + step])
            o_ref[place : place + rows, start : start + step] = exact_dot(packed, picks).astype(jnp.bfloat16)


def swap_sign(tiles, qs):
    turned = pltpu.roll(tiles, qs, 1)
    row = lax.broadcasted_iota(jnp.int32, (1,) + tiles.shape[1:], 1)
    return turned * jnp.where(row < qs, -1.0, 1.0)


def regroup_store(acc, first_lane, group, devices, tile_rows, x_ref):
    width = x_ref.shape[1] // 2
    per = LANES // group
    lane = lax.broadcasted_iota(jnp.int32, (tile_rows, LANES), 1) // group
    for offset in range(0, acc.shape[1], LANES):
        tile = acc[:, offset : offset + LANES].reshape(devices, tile_rows, LANES)
        row_start = (first_lane + offset) // group * tile_rows
        for block in range(devices // per):
            parts = [tile[block * per + m] for m in range(per)]
            bit = 1
            while bit < per:
                moved = list(parts)
                keep = (lane // bit) % 2 == 0
                for m in range(per):
                    if m & bit:
                        continue
                    low, high = parts[m], parts[m | bit]
                    if 2 * bit * group == LANES:
                        up = down = pltpu.roll(jnp.where(keep, high, low), LANES // 2, 1)
                    else:
                        up, down = pltpu.roll(high, bit * group, 1), pltpu.roll(low, LANES - bit * group, 1)
                    moved[m] = jnp.where(keep, low, up)
                    moved[m | bit] = jnp.where(keep, down, high)
                parts = moved
                bit *= 2
            tiles = jnp.stack(parts)
            rows = pl.ds(row_start, per * tile_rows)
            lanes = pl.ds(block * LANES, LANES)
            x_ref[rows, lanes] = tiles.reshape(per * tile_rows, LANES).astype(jnp.bfloat16)
            turned = swap_sign(tiles, tile_rows // 2)
            x_ref[rows, pl.ds(width + block * LANES, LANES)] = turned.reshape(per * tile_rows, LANES).astype(jnp.bfloat16)


def gate_copies(plan, blocks, whole_ref, sems):
    me = lax.axis_index("mode")
    copies = ([], [])
    for (sources, gates), block in zip(plan, blocks):
        for place, source in enumerate(sources):
            device = me
            for bit in source:
                device = device + (1 - 2 * (me // 2**bit % 2)) * 2**bit
            size = block.shape[3]
            rows = pl.ds(pl.multiple_of(device * size, size), size)
            for position, gate in enumerate(gates):
                sem = sems.at[gate, len(copies[gate])]
                copies[gate].append(
                    pltpu.make_async_copy(block.at[position, place], whole_ref.at[gate, :, rows, :], sem)
                )
    return copies


def layers_kernel(sizes, is_left, plan, x_ref, *refs):
    devices, qs, group, rows_each = sizes
    blocks, (o_ref, xs, last, whole_ref, sems) = refs[: len(plan)], refs[len(plan) :]
    copies = gate_copies(plan, blocks, whole_ref, sems)
    for gate in range(2):
        for copy in copies[gate]:
            copy.start()
    tile_rows = 2 * qs
    rows, width = x_ref.shape
    first = x_ref[...].astype(jnp.float32).reshape(devices, tile_rows, width)
    xs[0, :, :width] = x_ref[...]
    xs[0, :, width:] = swap_sign(first, qs).reshape(rows, width).astype(jnp.bfloat16)
    step = min(512, width)
    for layer in range(2 * CYCLES):
        if layer < 2:
            for copy in copies[layer]:
                copy.wait()
        gate = whole_ref.at[layer % 2]
        here, later = xs.at[layer % 2], xs.at[(layer + 1) % 2]
        for start in range(0, width, step):
            cols = slice(start, start + step)
            acc = exact_dot(here[...], gate[:, :, cols].reshape(2 * width, step))
            if layer < 2 * CYCLES - 1:
                regroup_store(acc, start, group, devices, tile_rows, later)
            else:
                last[:, cols] = acc.astype(jnp.bfloat16)
    half = rows // 2
    new = lax.broadcasted_iota(jnp.int32, (rows, rows), 0)
    part, inner = new // half, new % half
    if is_left:
        v, r = inner // devices, inner % devices
        picks = one_hot((rows, rows), 1, r * tile_rows + part * qs + v)
        moved = exact_dot(picks, last[...]).astype(jnp.bfloat16)
        span = 2 * rows_each
        each = width * qs // rows_each
        words = width // span
        step = min(256, width)
        for start in range(0, width, step):
            place = start + lax.broadcasted_iota(jnp.int32, (width, step), 1)
            e, rest = place // each, place % each
            h, w, qr = rest // (words * qs), rest % (words * qs) // qs, rest % qs
            lanes = one_hot((width, step), 0, w * span + (e * qs + qr) * 2 + h)
            sent = exact_dot(moved, lanes)
            low_lane = lax.broadcasted_iota(jnp.int32, (half, LANES), 1) < LANES // 2
            for offset in range(0, step, LANES):
                real = sent[:half, offset : offset + LANES]
                imag = sent[half:, offset : offset + LANES]
                e0 = (start + offset) // each
                even = jnp.where(low_lane, real, pltpu.roll(imag, LANES // 2, 1))
                odd = jnp.where(low_lane, pltpu.roll(real, LANES // 2, 1), imag)
                o_ref[e0 * half : (e0 + 1) * half, :] = even.astype(jnp.bfloat16)
                o_ref[(e0 + 1) * half : (e0 + 2) * half, :] = odd.astype(jnp.bfloat16)
    else:
        r, q = inner // qs, inner % qs
        picks = one_hot((rows, rows), 1, r * tile_rows + part * qs + q)
        o_ref[...] = exact_dot(picks, last[...]).astype(jnp.bfloat16)


def join_kernel(sizes, left_ref, right_ref, o_ref):
    devices, us, vs = sizes
    rows = us * devices
    free = right_ref.shape[1] // (2 * KEPT)
    left = left_ref[...].reshape(us, vs, devices, LANES)
    left = jnp.concatenate([left[:, v].reshape(rows, LANES) for v in range(vs)], axis=1)
    new = lax.broadcasted_iota(jnp.int32, (rows, rows), 0)
    picks = one_hot((rows, rows), 1, new % us * devices + new // us)
    left = exact_dot(picks, left).astype(jnp.bfloat16)
    half = right_ref.shape[0] // 2
    depth = half // vs
    real, imag = right_ref[:half, :], right_ref[half:, :]
    block = rows // KEPT
    for g in range(KEPT):
        stack = []
        for v in range(vs):
            r = [real[v * depth : (v + 1) * depth, (h * KEPT + g) * free :][:, :free] for h in range(2)]
            i = [imag[v * depth : (v + 1) * depth, (h * KEPT + g) * free :][:, :free] for h in range(2)]
            to_real = jnp.concatenate([r[0], r[1], -i[0], -i[1]], axis=0)
            to_imag = jnp.concatenate([i[0], i[1], r[0], r[1]], axis=0)
            stack.append(jnp.concatenate([to_real, to_imag], axis=1))
        stack = jnp.concatenate(stack, axis=0)
        part = exact_dot(left[g * block : (g + 1) * block, :], stack)
        o_ref[g * block : (g + 1) * block, :] = part.astype(jnp.bfloat16)


def call(kernel, out_shape, inputs, scratch=(), flops=0, blocks=(), grant=24, outputs=0):
    moved = sum(x.size * x.dtype.itemsize for x in (*inputs, *blocks))
    out = jax.ShapeDtypeStruct(out_shape, jnp.bfloat16)
    return pl.pallas_call(
        kernel,
        out_shape=[out] * outputs if outputs else out,
        in_specs=whole(len(inputs)) + [pl.BlockSpec(memory_space=pl.ANY)] * len(blocks),
        out_specs=whole(outputs) if outputs else whole(1)[0],
        scratch_shapes=list(scratch),
        compiler_params=pltpu.CompilerParams(vmem_limit_bytes=grant * MEBI),
        cost_estimate=pl.CostEstimate(flops=flops, bytes_accessed=moved, transcendentals=0),
    )(*inputs, *blocks)


def tiles_fit(devices, rows_each, width):
    pair_devices = devices // 2
    if devices < 4 or devices & (devices - 1) or rows_each % pair_devices or width % 256:
        return False
    qs, group = rows_each // pair_devices, width // devices
    return (
        2 * qs == 8
        and LANES % group == 0
        and devices % (LANES // group) == 0
        and qs == SHARED // width
        and devices % 32 == 0
        and 2 * width * qs // rows_each == LANES
        and devices * rows_each * width // SHARED % (KEPT * LANES) == 0
        and 2 * (devices * rows_each * width // SHARED) == width
    )


def fast(branch_in, column_order, gate_a, gate_b):
    devices = lax.axis_size("mode")
    rows_each, width = branch_in.shape[2:]
    halves = devices // 2
    qs, group = rows_each // halves, width // devices
    tile_rows = 2 * qs
    rows = devices * tile_rows
    packed = call(
        functools.partial(pack_kernel, qs),
        (rows, width),
        (branch_in, column_order),
        flops=8 * rows * width * width,
        outputs=2,
    )
    packed = [side.reshape(devices, tile_rows, width) for side in packed]
    blocks, plan, *states = spread(gate_a, gate_b, packed)
    states = [state.reshape(rows, width) for state in states]
    sizes = (devices, qs, group, rows_each)
    scratch = [
        pltpu.VMEM((2, rows, 2 * width), jnp.bfloat16),
        pltpu.VMEM((rows, width), jnp.bfloat16),
        pltpu.VMEM((2, 2, width, width), jnp.bfloat16),
        pltpu.SemaphoreType.DMA((2, devices)),
    ]
    work = 2 * CYCLES * 4 * rows * width * width
    left = call(
        functools.partial(layers_kernel, sizes, True, plan),
        (halves * rows // 2, LANES),
        (states[0],),
        scratch,
        work,
        blocks,
        56,
    )
    groups = [[h * halves + e for e in range(halves)] for h in range(2)]
    left = trade(left.reshape(halves, rows // 2, LANES), groups)
    right = call(
        functools.partial(layers_kernel, sizes, False, plan), (rows, width), (states[1],), scratch, work, blocks, 56
    )
    free = width // (2 * KEPT)
    us = halves
    partial_sums = call(
        functools.partial(join_kernel, (devices, us, qs)),
        (devices * us, 2 * free),
        (left.reshape(halves * rows // 2, LANES), right),
        flops=2 * devices * us * LANES * qs * 2 * free,
    )
    parts = trade(partial_sums.reshape(devices, us, 2 * free))
    parts = parts.reshape(2, halves, us, 2 * free).astype(jnp.float32)
    join_scale = (2.0 * SHARED) ** (-0.5)
    return (jnp.sum(parts, axis=1) * join_scale).astype(jnp.bfloat16).reshape(2, us, 2, free)


def flip(value, *bits):
    mask = sum(2**bit for bit in bits)
    pairs = [(source, source ^ mask) for source in range(lax.axis_size("mode"))]
    return lax.ppermute(value, "mode", pairs)


def plane(value, sources):
    over_x, over_y = flip(value, 1), flip(value, 2)
    diagonal = flip(over_x[:1], 2), flip(over_y[1:], 1)
    turned = [tuple(source + more for source in sources) for more in ((1,), (2,), (1, 2))]
    return [
        (value, sources, (0, 1)),
        (over_x, turned[0], (0, 1)),
        (over_y, turned[1], (0, 1)),
        (diagonal[0], turned[2], (0,)),
        (diagonal[1], turned[2], (1,)),
    ]


def spread(gate_a, gate_b, packed):
    bits = lax.axis_size("mode").bit_length() - 1
    own = jnp.stack([gate_a, gate_b])[:, None]
    far = [()]
    for bit in range(3, bits):
        far += [source + (bit,) for source in far]
    came = [flip(own, *source) for source in far[1:]]
    sets = [(own, ((),)), (jnp.concatenate(came[:2], axis=1), tuple(far[1:3]))]
    if came[2:]:
        sets.append((jnp.concatenate(came[2:], axis=1), tuple(far[3:])))
    blocks = []
    for number, (value, sources) in enumerate(sets):
        if number:
            tied = (*packed, blocks[3][0], blocks[4][0]) if number == 1 else (blocks[6][0], blocks[7][0])
            value, *_ = lax.optimization_barrier((value, *tied))
        blocks += plane(value, sources)
    left, *_ = lax.optimization_barrier((packed[0], blocks[8][0], blocks[9][0], blocks[-4][0], blocks[-3][0]))
    right, *_ = lax.optimization_barrier((packed[1], blocks[-2][0], blocks[-1][0]))
    last = len(blocks) - 2
    near = []
    for number, (value, sources, gates) in enumerate(blocks):
        if number >= last:
            value, *_ = lax.optimization_barrier((value, *[earlier for earlier, _, _ in near[:last]]))
        near.append((flip(value, 0), tuple(source + (0,) for source in sources), gates))
    blocks += near
    plan = tuple((sources, gates) for _, sources, gates in blocks)
    return [value for value, _, _ in blocks], plan, trade(left), trade(right)


def trade(value, groups=None):
    return lax.all_to_all(value, "mode", split_axis=0, concat_axis=0, axis_index_groups=groups, tiled=True)


def partner(value, axis, bit):
    mask = 2**bit
    pairs = [(source, source ^ mask) for source in range(lax.axis_size(axis))]
    return lax.ppermute(value, axis, pairs)


def product_four(states, layer_block):
    branches, parts, row_count, width = states.shape
    real_in = states[:, 0].reshape(branches * row_count, width)
    imag_in = states[:, 1].reshape(branches * row_count, width)
    real_part = jnp.dot(real_in, layer_block[0], preferred_element_type=jnp.float32) - jnp.dot(
        imag_in, layer_block[1], preferred_element_type=jnp.float32
    )
    imag_part = jnp.dot(real_in, layer_block[1], preferred_element_type=jnp.float32) + jnp.dot(
        imag_in, layer_block[0], preferred_element_type=jnp.float32
    )
    joined_parts = jnp.stack(
        [
            real_part.reshape(branches, row_count, width),
            imag_part.reshape(branches, row_count, width),
        ],
        axis=1,
    )
    return joined_parts.astype(jnp.bfloat16)


def complex_rows(left_real, left_imag, right_real, right_imag):
    real_part = jnp.dot(left_real, right_real, preferred_element_type=jnp.float32) - jnp.dot(
        left_imag, right_imag, preferred_element_type=jnp.float32
    )
    imag_part = jnp.dot(left_real, right_imag, preferred_element_type=jnp.float32) + jnp.dot(
        left_imag, right_real, preferred_element_type=jnp.float32
    )
    return jnp.stack([real_part, imag_part], axis=1)


def read_bit(device_index, bit_number):
    return device_index // 2**bit_number % 2


def trade_axes(buffer, axis_bits, trader, device_index):
    for position, bit_number in enumerate(axis_bits):
        own_bit = read_bit(device_index, bit_number)
        kept_half = lax.dynamic_index_in_dim(buffer, own_bit, position, keepdims=False)
        sent_half = lax.dynamic_index_in_dim(buffer, 1 - own_bit, position, keepdims=False)
        received = trader(sent_half, bit_number)
        first_half = jnp.where(own_bit == 0, kept_half, received)
        second_half = jnp.where(own_bit == 0, received, kept_half)
        buffer = jnp.stack([first_half, second_half], axis=position)
    return buffer


def general(branch_in, column_order, gate_a, gate_b):
    join_scale = (2.0 * SHARED) ** (-0.5)
    devices_mode = lax.axis_size("mode")
    whole_a, whole_b = (
        lax.all_gather(gate_a, "mode", axis=1, tiled=True),
        lax.all_gather(gate_b, "mode", axis=1, tiled=True),
    )
    states = jnp.take_along_axis(branch_in, column_order[:, None, None, :], axis=3)
    for layer_number in range(2 * CYCLES):
        if layer_number > 0:
            states = lax.all_to_all(states, "mode", split_axis=3, concat_axis=3, tiled=True)
        states = product_four(states, whole_a if layer_number % 2 == 0 else whole_b)
    local_cells = states.shape[2] * states.shape[3]
    local_rows = local_cells // SHARED
    shared_rows = SHARED // devices_mode
    join_width = local_cells // (shared_rows * KEPT)
    results = []
    for pair_number in range(2):
        left_part = states[2 * pair_number].reshape(2, local_rows, SHARED)
        right_part = states[2 * pair_number + 1].reshape(2, shared_rows, KEPT, join_width)
        device_index = lax.axis_index("mode")
        total_bits = devices_mode.bit_length() - 1
        group_bits = total_bits - 4
        batch_bits = KEPT.bit_length() - 1
        groups = devices_mode // (4 * KEPT)
        span = 2 * shared_rows
        outer = SHARED // (span * groups)
        half_join = join_width // 2

        def left_trader(piece, bit_number):
            return partner(piece, "mode", bit_number)

        def right_trader(piece, bit_number):
            return partner(piece, "mode", bit_number)

        left_buffer = left_part.reshape(2, local_rows, outer, groups, span).transpose(3, 0, 1, 2, 4)
        left_buffer = left_buffer.reshape((2,) * group_bits + (1, 2, local_rows, outer, span))
        left_buffer = jnp.broadcast_to(
            left_buffer, (2,) * group_bits + (2, 2, local_rows, outer, span)
        )
        left_bits = [group_bits - position for position in range(group_bits)] + [0]
        left_buffer = trade_axes(left_buffer, left_bits, left_trader, device_index)
        left_block = left_buffer.reshape(devices_mode // (2 * KEPT), 2, local_rows, outer * span)
        left_block = left_block.transpose(1, 0, 2, 3).reshape(2, half_join, SHARED // groups)
        right_buffer = right_part.reshape(2, shared_rows, KEPT, 2, half_join).transpose(
            2, 3, 0, 1, 4
        )
        right_buffer = right_buffer.reshape((2,) * batch_bits + (1, 2, 2, shared_rows, half_join))
        right_buffer = jnp.broadcast_to(
            right_buffer, (2,) * batch_bits + (2, 2, 2, shared_rows, half_join)
        )
        right_bits = [total_bits - 1 - position for position in range(batch_bits)] + [
            total_bits - batch_bits - 1,
            0,
        ]
        right_buffer = trade_axes(right_buffer, right_bits, right_trader, device_index)
        right_block = right_buffer.reshape(2 * KEPT, 2, 2, shared_rows, half_join)
        right_block = right_block.transpose(2, 0, 1, 3, 4).reshape(2, SHARED // groups, half_join)
        running = complex_rows(left_block[0], left_block[1], right_block[0], right_block[1])
        for position in range(group_bits):
            bit_number = group_bits - position
            own_bit = read_bit(device_index, bit_number)
            row_count = running.shape[0]
            halves = running.reshape(2, row_count // 2, 2, half_join)
            kept_half = lax.dynamic_index_in_dim(halves, own_bit, 0, keepdims=False)
            sent_half = lax.dynamic_index_in_dim(halves, 1 - own_bit, 0, keepdims=False)
            running = kept_half + partner(
                sent_half.astype(jnp.bfloat16), "mode", bit_number
            ).astype(sent_half.dtype)
        rounded = (running * join_scale).astype(jnp.bfloat16)
        own_bit = read_bit(device_index, 0)
        halves = rounded.reshape(2, local_rows, 2, half_join)
        kept_half = lax.dynamic_index_in_dim(halves, own_bit, 0, keepdims=False)
        sent_half = lax.dynamic_index_in_dim(halves, 1 - own_bit, 0, keepdims=False)
        received = partner(sent_half, "mode", 0)
        first_half = jnp.where(own_bit == 0, kept_half, received)
        second_half = jnp.where(own_bit == 0, received, kept_half)
        finished = jnp.concatenate([first_half, second_half], axis=2)
        results.append(finished)
    return jnp.stack(results)


def local(branch_in, column_order, gate_a, gate_b):
    branches, _, rows_each, width = branch_in.shape
    if branches == 4 and tiles_fit(lax.axis_size("mode"), rows_each, width):
        return fast(branch_in, column_order, gate_a, gate_b)
    return general(branch_in, column_order, gate_a, gate_b)


def solution(mesh):
    in_specs = (
        P(None, None, ("cuts", "mode"), None),
        P(),
        P(None, "mode", None),
        P(None, "mode", None),
    )
    out_specs = P(None, ("cuts", "mode"), None, None)
    return jax.shard_map(local, mesh=mesh, in_specs=in_specs, out_specs=out_specs, check_vma=False)
```

```python
import functools

import jax
import jax.numpy as jnp
from jax import lax
from jax.experimental import pallas as pl
from jax.experimental.pallas import tpu as pltpu
from jax.sharding import PartitionSpec as P

SHARED = 4096
KEPT = 4
CYCLES = 2
LANES = 128
MEBI = 1024 * 1024


def whole(count):
    return [pl.BlockSpec(memory_space=pltpu.VMEM)] * count


def one_hot(shape, axis, wanted):
    return (lax.broadcasted_iota(jnp.int32, shape, axis) == wanted).astype(jnp.bfloat16)


def exact_dot(left, right):
    return jnp.dot(left, right, preferred_element_type=jnp.float32)


def pack_kernel(qs, x_ref, order_ref, left_ref, right_ref):
    _, parts, rows_each, width = x_ref.shape
    rows = parts * rows_each
    step = min(256, width)
    new = lax.broadcasted_iota(jnp.int32, (rows, rows), 0)
    e, k, q = new // (parts * qs), new // qs % parts, new % qs
    pack = one_hot((rows, rows), 1, k * rows_each + e * qs + q)
    for branch in range(x_ref.shape[0]):
        o_ref = (left_ref, right_ref)[branch % 2]
        place = branch // 2 * rows
        packed = exact_dot(pack, x_ref[branch].reshape(rows, width)).astype(jnp.bfloat16)
        for start in range(0, width, step):
            picks = one_hot((width, step), 0, order_ref[branch : branch + 1, start : start + step])
            o_ref[place : place + rows, start : start + step] = exact_dot(packed, picks).astype(jnp.bfloat16)


def swap_sign(tiles, qs):
    turned = pltpu.roll(tiles, qs, 1)
    row = lax.broadcasted_iota(jnp.int32, (1,) + tiles.shape[1:], 1)
    return turned * jnp.where(row < qs, -1.0, 1.0)


def regroup_store(acc, first_lane, group, devices, tile_rows, x_ref):
    width = x_ref.shape[1] // 2
    per = LANES // group
    lane = lax.broadcasted_iota(jnp.int32, (tile_rows, LANES), 1) // group
    for offset in range(0, acc.shape[1], LANES):
        tile = acc[:, offset : offset + LANES].reshape(devices, tile_rows, LANES)
        row_start = (first_lane + offset) // group * tile_rows
        for block in range(devices // per):
            parts = [tile[block * per + m] for m in range(per)]
            bit = 1
            while bit < per:
                moved = list(parts)
                keep = (lane // bit) % 2 == 0
                for m in range(per):
                    if m & bit:
                        continue
                    low, high = parts[m], parts[m | bit]
                    if 2 * bit * group == LANES:
                        up = down = pltpu.roll(jnp.where(keep, high, low), LANES // 2, 1)
                    else:
                        up, down = pltpu.roll(high, bit * group, 1), pltpu.roll(low, LANES - bit * group, 1)
                    moved[m] = jnp.where(keep, low, up)
                    moved[m | bit] = jnp.where(keep, down, high)
                parts = moved
                bit *= 2
            tiles = jnp.stack(parts)
            rows = pl.ds(row_start, per * tile_rows)
            lanes = pl.ds(block * LANES, LANES)
            x_ref[rows, lanes] = tiles.reshape(per * tile_rows, LANES).astype(jnp.bfloat16)
            turned = swap_sign(tiles, tile_rows // 2)
            x_ref[rows, pl.ds(width + block * LANES, LANES)] = turned.reshape(per * tile_rows, LANES).astype(jnp.bfloat16)


def gate_copies(plan, blocks, whole_ref, sems):
    me = lax.axis_index("mode")
    copies = ([], [])
    for (sources, gates), block in zip(plan, blocks):
        for place, source in enumerate(sources):
            device = me
            for bit in source:
                device = device + (1 - 2 * (me // 2**bit % 2)) * 2**bit
            size = block.shape[3]
            rows = pl.ds(pl.multiple_of(device * size, size), size)
            for position, gate in enumerate(gates):
                sem = sems.at[gate, len(copies[gate])]
                copies[gate].append(
                    pltpu.make_async_copy(block.at[position, place], whole_ref.at[gate, :, rows, :], sem)
                )
    return copies


def layers_kernel(sizes, is_left, plan, x_ref, *refs):
    devices, qs, group, rows_each = sizes
    blocks, (o_ref, xs, last, whole_ref, sems) = refs[: len(plan)], refs[len(plan) :]
    copies = gate_copies(plan, blocks, whole_ref, sems)
    for gate in range(2):
        for copy in copies[gate]:
            copy.start()
    tile_rows = 2 * qs
    rows, width = x_ref.shape
    first = x_ref[...].astype(jnp.float32).reshape(devices, tile_rows, width)
    xs[0, :, :width] = x_ref[...]
    xs[0, :, width:] = swap_sign(first, qs).reshape(rows, width).astype(jnp.bfloat16)
    step = min(512, width)
    for layer in range(2 * CYCLES):
        if layer < 2:
            for copy in copies[layer]:
                copy.wait()
        gate = whole_ref.at[layer % 2]
        here, later = xs.at[layer % 2], xs.at[(layer + 1) % 2]
        for start in range(0, width, step):
            cols = slice(start, start + step)
            acc = exact_dot(here[...], gate[:, :, cols].reshape(2 * width, step))
            if layer < 2 * CYCLES - 1:
                regroup_store(acc, start, group, devices, tile_rows, later)
            else:
                last[:, cols] = acc.astype(jnp.bfloat16)
    half = rows // 2
    new = lax.broadcasted_iota(jnp.int32, (rows, rows), 0)
    part, inner = new // half, new % half
    if is_left:
        v, r = inner // devices, inner % devices
        picks = one_hot((rows, rows), 1, r * tile_rows + part * qs + v)
        moved = exact_dot(picks, last[...]).astype(jnp.bfloat16)
        span = 2 * rows_each
        each = width * qs // rows_each
        words = width // span
        step = min(256, width)
        for start in range(0, width, step):
            place = start + lax.broadcasted_iota(jnp.int32, (width, step), 1)
            e, rest = place // each, place % each
            h, w, qr = rest // (words * qs), rest % (words * qs) // qs, rest % qs
            lanes = one_hot((width, step), 0, w * span + (e * qs + qr) * 2 + h)
            sent = exact_dot(moved, lanes)
            low_lane = lax.broadcasted_iota(jnp.int32, (half, LANES), 1) < LANES // 2
            for offset in range(0, step, LANES):
                real = sent[:half, offset : offset + LANES]
                imag = sent[half:, offset : offset + LANES]
                e0 = (start + offset) // each
                even = jnp.where(low_lane, real, pltpu.roll(imag, LANES // 2, 1))
                odd = jnp.where(low_lane, pltpu.roll(real, LANES // 2, 1), imag)
                o_ref[e0 * half : (e0 + 1) * half, :] = even.astype(jnp.bfloat16)
                o_ref[(e0 + 1) * half : (e0 + 2) * half, :] = odd.astype(jnp.bfloat16)
    else:
        r, q = inner // qs, inner % qs
        picks = one_hot((rows, rows), 1, r * tile_rows + part * qs + q)
        o_ref[...] = exact_dot(picks, last[...]).astype(jnp.bfloat16)


def join_kernel(sizes, left_ref, right_ref, o_ref):
    devices, us, vs = sizes
    rows = us * devices
    free = right_ref.shape[1] // (2 * KEPT)
    left = left_ref[...].reshape(us, vs, devices, LANES)
    left = jnp.concatenate([left[:, v].reshape(rows, LANES) for v in range(vs)], axis=1)
    new = lax.broadcasted_iota(jnp.int32, (rows, rows), 0)
    picks = one_hot((rows, rows), 1, new % us * devices + new // us)
    left = exact_dot(picks, left).astype(jnp.bfloat16)
    half = right_ref.shape[0] // 2
    depth = half // vs
    real, imag = right_ref[:half, :], right_ref[half:, :]
    block = rows // KEPT
    for g in range(KEPT):
        stack = []
        for v in range(vs):
            r = [real[v * depth : (v + 1) * depth, (h * KEPT + g) * free :][:, :free] for h in range(2)]
            i = [imag[v * depth : (v + 1) * depth, (h * KEPT + g) * free :][:, :free] for h in range(2)]
            to_real = jnp.concatenate([r[0], r[1], -i[0], -i[1]], axis=0)
            to_imag = jnp.concatenate([i[0], i[1], r[0], r[1]], axis=0)
            stack.append(jnp.concatenate([to_real, to_imag], axis=1))
        stack = jnp.concatenate(stack, axis=0)
        part = exact_dot(left[g * block : (g + 1) * block, :], stack)
        o_ref[g * block : (g + 1) * block, :] = part.astype(jnp.bfloat16)


def call(kernel, out_shape, inputs, scratch=(), flops=0, blocks=(), grant=24, outputs=0):
    moved = sum(x.size * x.dtype.itemsize for x in (*inputs, *blocks))
    out = jax.ShapeDtypeStruct(out_shape, jnp.bfloat16)
    return pl.pallas_call(
        kernel,
        out_shape=[out] * outputs if outputs else out,
        in_specs=whole(len(inputs)) + [pl.BlockSpec(memory_space=pl.ANY)] * len(blocks),
        out_specs=whole(outputs) if outputs else whole(1)[0],
        scratch_shapes=list(scratch),
        compiler_params=pltpu.CompilerParams(vmem_limit_bytes=grant * MEBI),
        cost_estimate=pl.CostEstimate(flops=flops, bytes_accessed=moved, transcendentals=0),
    )(*inputs, *blocks)


def tiles_fit(devices, rows_each, width):
    pair_devices = devices // 2
    if devices < 4 or devices & (devices - 1) or rows_each % pair_devices or width % 256:
        return False
    qs, group = rows_each // pair_devices, width // devices
    return (
        2 * qs == 8
        and LANES % group == 0
        and devices % (LANES // group) == 0
        and qs == SHARED // width
        and devices % 32 == 0
        and 2 * width * qs // rows_each == LANES
        and devices * rows_each * width // SHARED % (KEPT * LANES) == 0
        and 2 * (devices * rows_each * width // SHARED) == width
    )


def fast(branch_in, column_order, gate_a, gate_b):
    devices = lax.axis_size("mode")
    rows_each, width = branch_in.shape[2:]
    halves = devices // 2
    qs, group = rows_each // halves, width // devices
    tile_rows = 2 * qs
    rows = devices * tile_rows
    packed = call(
        functools.partial(pack_kernel, qs),
        (rows, width),
        (branch_in, column_order),
        flops=8 * rows * width * width,
        outputs=2,
    )
    packed = [side.reshape(devices, tile_rows, width) for side in packed]
    blocks, plan, *states = spread(gate_a, gate_b, packed)
    states = [state.reshape(rows, width) for state in states]
    sizes = (devices, qs, group, rows_each)
    scratch = [
        pltpu.VMEM((2, rows, 2 * width), jnp.bfloat16),
        pltpu.VMEM((rows, width), jnp.bfloat16),
        pltpu.VMEM((2, 2, width, width), jnp.bfloat16),
        pltpu.SemaphoreType.DMA((2, devices)),
    ]
    work = 2 * CYCLES * 4 * rows * width * width
    left = call(
        functools.partial(layers_kernel, sizes, True, plan),
        (halves * rows // 2, LANES),
        (states[0],),
        scratch,
        work,
        blocks,
        56,
    )
    groups = [[h * halves + e for e in range(halves)] for h in range(2)]
    left = trade(left.reshape(halves, rows // 2, LANES), groups)
    right = call(
        functools.partial(layers_kernel, sizes, False, plan), (rows, width), (states[1],), scratch, work, blocks, 56
    )
    free = width // (2 * KEPT)
    us = halves
    partial_sums = call(
        functools.partial(join_kernel, (devices, us, qs)),
        (devices * us, 2 * free),
        (left.reshape(halves * rows // 2, LANES), right),
        flops=2 * devices * us * LANES * qs * 2 * free,
    )
    parts = trade(partial_sums.reshape(devices, us, 2 * free))
    parts = parts.reshape(2, halves, us, 2 * free).astype(jnp.float32)
    join_scale = (2.0 * SHARED) ** (-0.5)
    return (jnp.sum(parts, axis=1) * join_scale).astype(jnp.bfloat16).reshape(2, us, 2, free)


def flip(value, *bits):
    mask = sum(2**bit for bit in bits)
    pairs = [(source, source ^ mask) for source in range(lax.axis_size("mode"))]
    return lax.ppermute(value, "mode", pairs)


def plane(value, sources):
    over_x, over_y = flip(value, 1), flip(value, 2)
    diagonal = flip(over_x[:1], 2), flip(over_y[1:], 1)
    turned = [tuple(source + more for source in sources) for more in ((1,), (2,), (1, 2))]
    return [
        (value, sources, (0, 1)),
        (over_x, turned[0], (0, 1)),
        (over_y, turned[1], (0, 1)),
        (diagonal[0], turned[2], (0,)),
        (diagonal[1], turned[2], (1,)),
    ]


def spread(gate_a, gate_b, packed):
    bits = lax.axis_size("mode").bit_length() - 1
    own = jnp.stack([gate_a, gate_b])[:, None]
    far = [()]
    for bit in range(3, bits):
        far += [source + (bit,) for source in far]
    came = [flip(own, *source) for source in far[1:]]
    sets = [(own, ((),)), (jnp.concatenate(came[:2], axis=1), tuple(far[1:3]))]
    if came[2:]:
        sets.append((jnp.concatenate(came[2:], axis=1), tuple(far[3:])))
    blocks = []
    for number, (value, sources) in enumerate(sets):
        if number:
            tied = (blocks[3][0], blocks[4][0]) if number == 1 else (*packed, blocks[6][0], blocks[7][0])
            value, *_ = lax.optimization_barrier((value, *tied))
        blocks += plane(value, sources)
    left, *_ = lax.optimization_barrier((packed[0], blocks[8][0], blocks[9][0], blocks[-4][0], blocks[-3][0]))
    right, *_ = lax.optimization_barrier((packed[1], blocks[-2][0], blocks[-1][0]))
    last = len(blocks) - 2
    near = []
    for number, (value, sources, gates) in enumerate(blocks):
        if number >= last:
            value, *_ = lax.optimization_barrier((value, *[earlier for earlier, _, _ in near[:last]]))
        near.append((flip(value, 0), tuple(source + (0,) for source in sources), gates))
    blocks += near
    plan = tuple((sources, gates) for _, sources, gates in blocks)
    return [value for value, _, _ in blocks], plan, trade(left), trade(right)


def trade(value, groups=None):
    return lax.all_to_all(value, "mode", split_axis=0, concat_axis=0, axis_index_groups=groups, tiled=True)


def partner(value, axis, bit):
    mask = 2**bit
    pairs = [(source, source ^ mask) for source in range(lax.axis_size(axis))]
    return lax.ppermute(value, axis, pairs)


def product_four(states, layer_block):
    branches, parts, row_count, width = states.shape
    real_in = states[:, 0].reshape(branches * row_count, width)
    imag_in = states[:, 1].reshape(branches * row_count, width)
    real_part = jnp.dot(real_in, layer_block[0], preferred_element_type=jnp.float32) - jnp.dot(
        imag_in, layer_block[1], preferred_element_type=jnp.float32
    )
    imag_part = jnp.dot(real_in, layer_block[1], preferred_element_type=jnp.float32) + jnp.dot(
        imag_in, layer_block[0], preferred_element_type=jnp.float32
    )
    joined_parts = jnp.stack(
        [
            real_part.reshape(branches, row_count, width),
            imag_part.reshape(branches, row_count, width),
        ],
        axis=1,
    )
    return joined_parts.astype(jnp.bfloat16)


def complex_rows(left_real, left_imag, right_real, right_imag):
    real_part = jnp.dot(left_real, right_real, preferred_element_type=jnp.float32) - jnp.dot(
        left_imag, right_imag, preferred_element_type=jnp.float32
    )
    imag_part = jnp.dot(left_real, right_imag, preferred_element_type=jnp.float32) + jnp.dot(
        left_imag, right_real, preferred_element_type=jnp.float32
    )
    return jnp.stack([real_part, imag_part], axis=1)


def read_bit(device_index, bit_number):
    return device_index // 2**bit_number % 2


def trade_axes(buffer, axis_bits, trader, device_index):
    for position, bit_number in enumerate(axis_bits):
        own_bit = read_bit(device_index, bit_number)
        kept_half = lax.dynamic_index_in_dim(buffer, own_bit, position, keepdims=False)
        sent_half = lax.dynamic_index_in_dim(buffer, 1 - own_bit, position, keepdims=False)
        received = trader(sent_half, bit_number)
        first_half = jnp.where(own_bit == 0, kept_half, received)
        second_half = jnp.where(own_bit == 0, received, kept_half)
        buffer = jnp.stack([first_half, second_half], axis=position)
    return buffer


def general(branch_in, column_order, gate_a, gate_b):
    join_scale = (2.0 * SHARED) ** (-0.5)
    devices_mode = lax.axis_size("mode")
    whole_a, whole_b = (
        lax.all_gather(gate_a, "mode", axis=1, tiled=True),
        lax.all_gather(gate_b, "mode", axis=1, tiled=True),
    )
    states = jnp.take_along_axis(branch_in, column_order[:, None, None, :], axis=3)
    for layer_number in range(2 * CYCLES):
        if layer_number > 0:
            states = lax.all_to_all(states, "mode", split_axis=3, concat_axis=3, tiled=True)
        states = product_four(states, whole_a if layer_number % 2 == 0 else whole_b)
    local_cells = states.shape[2] * states.shape[3]
    local_rows = local_cells // SHARED
    shared_rows = SHARED // devices_mode
    join_width = local_cells // (shared_rows * KEPT)
    results = []
    for pair_number in range(2):
        left_part = states[2 * pair_number].reshape(2, local_rows, SHARED)
        right_part = states[2 * pair_number + 1].reshape(2, shared_rows, KEPT, join_width)
        device_index = lax.axis_index("mode")
        total_bits = devices_mode.bit_length() - 1
        group_bits = total_bits - 4
        batch_bits = KEPT.bit_length() - 1
        groups = devices_mode // (4 * KEPT)
        span = 2 * shared_rows
        outer = SHARED // (span * groups)
        half_join = join_width // 2

        def left_trader(piece, bit_number):
            return partner(piece, "mode", bit_number)

        def right_trader(piece, bit_number):
            return partner(piece, "mode", bit_number)

        left_buffer = left_part.reshape(2, local_rows, outer, groups, span).transpose(3, 0, 1, 2, 4)
        left_buffer = left_buffer.reshape((2,) * group_bits + (1, 2, local_rows, outer, span))
        left_buffer = jnp.broadcast_to(
            left_buffer, (2,) * group_bits + (2, 2, local_rows, outer, span)
        )
        left_bits = [group_bits - position for position in range(group_bits)] + [0]
        left_buffer = trade_axes(left_buffer, left_bits, left_trader, device_index)
        left_block = left_buffer.reshape(devices_mode // (2 * KEPT), 2, local_rows, outer * span)
        left_block = left_block.transpose(1, 0, 2, 3).reshape(2, half_join, SHARED // groups)
        right_buffer = right_part.reshape(2, shared_rows, KEPT, 2, half_join).transpose(
            2, 3, 0, 1, 4
        )
        right_buffer = right_buffer.reshape((2,) * batch_bits + (1, 2, 2, shared_rows, half_join))
        right_buffer = jnp.broadcast_to(
            right_buffer, (2,) * batch_bits + (2, 2, 2, shared_rows, half_join)
        )
        right_bits = [total_bits - 1 - position for position in range(batch_bits)] + [
            total_bits - batch_bits - 1,
            0,
        ]
        right_buffer = trade_axes(right_buffer, right_bits, right_trader, device_index)
        right_block = right_buffer.reshape(2 * KEPT, 2, 2, shared_rows, half_join)
        right_block = right_block.transpose(2, 0, 1, 3, 4).reshape(2, SHARED // groups, half_join)
        running = complex_rows(left_block[0], left_block[1], right_block[0], right_block[1])
        for position in range(group_bits):
            bit_number = group_bits - position
            own_bit = read_bit(device_index, bit_number)
            row_count = running.shape[0]
            halves = running.reshape(2, row_count // 2, 2, half_join)
            kept_half = lax.dynamic_index_in_dim(halves, own_bit, 0, keepdims=False)
            sent_half = lax.dynamic_index_in_dim(halves, 1 - own_bit, 0, keepdims=False)
            running = kept_half + partner(
                sent_half.astype(jnp.bfloat16), "mode", bit_number
            ).astype(sent_half.dtype)
        rounded = (running * join_scale).astype(jnp.bfloat16)
        own_bit = read_bit(device_index, 0)
        halves = rounded.reshape(2, local_rows, 2, half_join)
        kept_half = lax.dynamic_index_in_dim(halves, own_bit, 0, keepdims=False)
        sent_half = lax.dynamic_index_in_dim(halves, 1 - own_bit, 0, keepdims=False)
        received = partner(sent_half, "mode", 0)
        first_half = jnp.where(own_bit == 0, kept_half, received)
        second_half = jnp.where(own_bit == 0, received, kept_half)
        finished = jnp.concatenate([first_half, second_half], axis=2)
        results.append(finished)
    return jnp.stack(results)


def local(branch_in, column_order, gate_a, gate_b):
    branches, _, rows_each, width = branch_in.shape
    if branches == 4 and tiles_fit(lax.axis_size("mode"), rows_each, width):
        return fast(branch_in, column_order, gate_a, gate_b)
    return general(branch_in, column_order, gate_a, gate_b)


def solution(mesh):
    in_specs = (
        P(None, None, ("cuts", "mode"), None),
        P(),
        P(None, "mode", None),
        P(None, "mode", None),
    )
    out_specs = P(None, ("cuts", "mode"), None, None)
    return jax.shard_map(local, mesh=mesh, in_specs=in_specs, out_specs=out_specs, check_vma=False)
```

```python
import functools

import jax
import jax.numpy as jnp
from jax import lax
from jax.experimental import pallas as pl
from jax.experimental.pallas import tpu as pltpu
from jax.sharding import PartitionSpec as P

SHARED = 4096
KEPT = 4
CYCLES = 2
LANES = 128
MEBI = 1024 * 1024


def whole(count):
    return [pl.BlockSpec(memory_space=pltpu.VMEM)] * count


def one_hot(shape, axis, wanted):
    return (lax.broadcasted_iota(jnp.int32, shape, axis) == wanted).astype(jnp.bfloat16)


def exact_dot(left, right):
    return jnp.dot(left, right, preferred_element_type=jnp.float32)


def pack_kernel(qs, x_ref, order_ref, left_ref, right_ref):
    _, parts, rows_each, width = x_ref.shape
    rows = parts * rows_each
    step = min(256, width)
    new = lax.broadcasted_iota(jnp.int32, (rows, rows), 0)
    e, k, q = new // (parts * qs), new // qs % parts, new % qs
    pack = one_hot((rows, rows), 1, k * rows_each + e * qs + q)
    for branch in range(x_ref.shape[0]):
        o_ref = (left_ref, right_ref)[branch % 2]
        place = branch // 2 * rows
        packed = exact_dot(pack, x_ref[branch].reshape(rows, width)).astype(jnp.bfloat16)
        for start in range(0, width, step):
            picks = one_hot((width, step), 0, order_ref[branch : branch + 1, start : start + step])
            o_ref[place : place + rows, start : start + step] = exact_dot(packed, picks).astype(jnp.bfloat16)


def swap_sign(tiles, qs):
    turned = pltpu.roll(tiles, qs, 1)
    row = lax.broadcasted_iota(jnp.int32, (1,) + tiles.shape[1:], 1)
    return turned * jnp.where(row < qs, -1.0, 1.0)


def regroup_store(acc, first_lane, group, devices, tile_rows, x_ref):
    width = x_ref.shape[1] // 2
    per = LANES // group
    lane = lax.broadcasted_iota(jnp.int32, (tile_rows, LANES), 1) // group
    for offset in range(0, acc.shape[1], LANES):
        tile = acc[:, offset : offset + LANES].reshape(devices, tile_rows, LANES)
        row_start = (first_lane + offset) // group * tile_rows
        for block in range(devices // per):
            parts = [tile[block * per + m] for m in range(per)]
            bit = 1
            while bit < per:
                moved = list(parts)
                keep = (lane // bit) % 2 == 0
                for m in range(per):
                    if m & bit:
                        continue
                    low, high = parts[m], parts[m | bit]
                    if 2 * bit * group == LANES:
                        up = down = pltpu.roll(jnp.where(keep, high, low), LANES // 2, 1)
                    else:
                        up, down = pltpu.roll(high, bit * group, 1), pltpu.roll(low, LANES - bit * group, 1)
                    moved[m] = jnp.where(keep, low, up)
                    moved[m | bit] = jnp.where(keep, down, high)
                parts = moved
                bit *= 2
            tiles = jnp.stack(parts)
            rows = pl.ds(row_start, per * tile_rows)
            lanes = pl.ds(block * LANES, LANES)
            x_ref[rows, lanes] = tiles.reshape(per * tile_rows, LANES).astype(jnp.bfloat16)
            turned = swap_sign(tiles, tile_rows // 2)
            x_ref[rows, pl.ds(width + block * LANES, LANES)] = turned.reshape(per * tile_rows, LANES).astype(jnp.bfloat16)


def gate_copies(plan, blocks, whole_ref, sems):
    me = lax.axis_index("mode")
    copies = ([], [])
    for (sources, gates), block in zip(plan, blocks):
        for place, source in enumerate(sources):
            device = me
            for bit in source:
                device = device + (1 - 2 * (me // 2**bit % 2)) * 2**bit
            size = block.shape[3]
            rows = pl.ds(pl.multiple_of(device * size, size), size)
            for position, gate in enumerate(gates):
                sem = sems.at[gate, len(copies[gate])]
                copies[gate].append(
                    pltpu.make_async_copy(block.at[position, place], whole_ref.at[gate, :, rows, :], sem)
                )
    return copies


def layers_kernel(sizes, is_left, plan, x_ref, *refs):
    devices, qs, group, rows_each = sizes
    blocks, (o_ref, xs, last, whole_ref, sems) = refs[: len(plan)], refs[len(plan) :]
    copies = gate_copies(plan, blocks, whole_ref, sems)
    for gate in range(2):
        for copy in copies[gate]:
            copy.start()
    tile_rows = 2 * qs
    rows, width = x_ref.shape
    first = x_ref[...].astype(jnp.float32).reshape(devices, tile_rows, width)
    xs[0, :, :width] = x_ref[...]
    xs[0, :, width:] = swap_sign(first, qs).reshape(rows, width).astype(jnp.bfloat16)
    step = min(512, width)
    for layer in range(2 * CYCLES):
        if layer < 2:
            for copy in copies[layer]:
                copy.wait()
        gate = whole_ref.at[layer % 2]
        here, later = xs.at[layer % 2], xs.at[(layer + 1) % 2]
        for start in range(0, width, step):
            cols = slice(start, start + step)
            acc = exact_dot(here[...], gate[:, :, cols].reshape(2 * width, step))
            if layer < 2 * CYCLES - 1:
                regroup_store(acc, start, group, devices, tile_rows, later)
            else:
                last[:, cols] = acc.astype(jnp.bfloat16)
    half = rows // 2
    new = lax.broadcasted_iota(jnp.int32, (rows, rows), 0)
    part, inner = new // half, new % half
    if is_left:
        v, r = inner // devices, inner % devices
        picks = one_hot((rows, rows), 1, r * tile_rows + part * qs + v)
        moved = exact_dot(picks, last[...]).astype(jnp.bfloat16)
        span = 2 * rows_each
        each = width * qs // rows_each
        words = width // span
        step = min(256, width)
        for start in range(0, width, step):
            place = start + lax.broadcasted_iota(jnp.int32, (width, step), 1)
            e, rest = place // each, place % each
            h, w, qr = rest // (words * qs), rest % (words * qs) // qs, rest % qs
            lanes = one_hot((width, step), 0, w * span + (e * qs + qr) * 2 + h)
            sent = exact_dot(moved, lanes)
            low_lane = lax.broadcasted_iota(jnp.int32, (half, LANES), 1) < LANES // 2
            for offset in range(0, step, LANES):
                real = sent[:half, offset : offset + LANES]
                imag = sent[half:, offset : offset + LANES]
                e0 = (start + offset) // each
                even = jnp.where(low_lane, real, pltpu.roll(imag, LANES // 2, 1))
                odd = jnp.where(low_lane, pltpu.roll(real, LANES // 2, 1), imag)
                o_ref[e0 * half : (e0 + 1) * half, :] = even.astype(jnp.bfloat16)
                o_ref[(e0 + 1) * half : (e0 + 2) * half, :] = odd.astype(jnp.bfloat16)
    else:
        r, q = inner // qs, inner % qs
        picks = one_hot((rows, rows), 1, r * tile_rows + part * qs + q)
        o_ref[...] = exact_dot(picks, last[...]).astype(jnp.bfloat16)


def join_kernel(sizes, left_ref, right_ref, o_ref):
    devices, us, vs = sizes
    rows = us * devices
    free = right_ref.shape[1] // (2 * KEPT)
    left = left_ref[...].reshape(us, vs, devices, LANES)
    left = jnp.concatenate([left[:, v].reshape(rows, LANES) for v in range(vs)], axis=1)
    new = lax.broadcasted_iota(jnp.int32, (rows, rows), 0)
    picks = one_hot((rows, rows), 1, new % us * devices + new // us)
    left = exact_dot(picks, left).astype(jnp.bfloat16)
    half = right_ref.shape[0] // 2
    depth = half // vs
    real, imag = right_ref[:half, :], right_ref[half:, :]
    block = rows // KEPT
    for g in range(KEPT):
        stack = []
        for v in range(vs):
            r = [real[v * depth : (v + 1) * depth, (h * KEPT + g) * free :][:, :free] for h in range(2)]
            i = [imag[v * depth : (v + 1) * depth, (h * KEPT + g) * free :][:, :free] for h in range(2)]
            to_real = jnp.concatenate([r[0], r[1], -i[0], -i[1]], axis=0)
            to_imag = jnp.concatenate([i[0], i[1], r[0], r[1]], axis=0)
            stack.append(jnp.concatenate([to_real, to_imag], axis=1))
        stack = jnp.concatenate(stack, axis=0)
        part = exact_dot(left[g * block : (g + 1) * block, :], stack)
        o_ref[g * block : (g + 1) * block, :] = part.astype(jnp.bfloat16)


def call(kernel, out_shape, inputs, scratch=(), flops=0, blocks=(), grant=24, outputs=0):
    moved = sum(x.size * x.dtype.itemsize for x in (*inputs, *blocks))
    out = jax.ShapeDtypeStruct(out_shape, jnp.bfloat16)
    return pl.pallas_call(
        kernel,
        out_shape=[out] * outputs if outputs else out,
        in_specs=whole(len(inputs)) + [pl.BlockSpec(memory_space=pl.ANY)] * len(blocks),
        out_specs=whole(outputs) if outputs else whole(1)[0],
        scratch_shapes=list(scratch),
        compiler_params=pltpu.CompilerParams(vmem_limit_bytes=grant * MEBI),
        cost_estimate=pl.CostEstimate(flops=flops, bytes_accessed=moved, transcendentals=0),
    )(*inputs, *blocks)


def tiles_fit(devices, rows_each, width):
    pair_devices = devices // 2
    if devices < 4 or devices & (devices - 1) or rows_each % pair_devices or width % 256:
        return False
    qs, group = rows_each // pair_devices, width // devices
    return (
        2 * qs == 8
        and LANES % group == 0
        and devices % (LANES // group) == 0
        and qs == SHARED // width
        and devices % 32 == 0
        and 2 * width * qs // rows_each == LANES
        and devices * rows_each * width // SHARED % (KEPT * LANES) == 0
        and 2 * (devices * rows_each * width // SHARED) == width
    )


def fast(branch_in, column_order, gate_a, gate_b):
    devices = lax.axis_size("mode")
    rows_each, width = branch_in.shape[2:]
    halves = devices // 2
    qs, group = rows_each // halves, width // devices
    tile_rows = 2 * qs
    rows = devices * tile_rows
    packed = call(
        functools.partial(pack_kernel, qs),
        (rows, width),
        (branch_in, column_order),
        flops=8 * rows * width * width,
        outputs=2,
    )
    packed = [side.reshape(devices, tile_rows, width) for side in packed]
    blocks, plan, *states = spread(gate_a, gate_b, packed)
    states = [state.reshape(rows, width) for state in states]
    sizes = (devices, qs, group, rows_each)
    scratch = [
        pltpu.VMEM((2, rows, 2 * width), jnp.bfloat16),
        pltpu.VMEM((rows, width), jnp.bfloat16),
        pltpu.VMEM((2, 2, width, width), jnp.bfloat16),
        pltpu.SemaphoreType.DMA((2, devices)),
    ]
    work = 2 * CYCLES * 4 * rows * width * width
    left = call(
        functools.partial(layers_kernel, sizes, True, plan),
        (halves * rows // 2, LANES),
        (states[0],),
        scratch,
        work,
        blocks,
        56,
    )
    groups = [[h * halves + e for e in range(halves)] for h in range(2)]
    left = trade(left.reshape(halves, rows // 2, LANES), groups)
    right = call(
        functools.partial(layers_kernel, sizes, False, plan), (rows, width), (states[1],), scratch, work, blocks, 56
    )
    free = width // (2 * KEPT)
    us = halves
    partial_sums = call(
        functools.partial(join_kernel, (devices, us, qs)),
        (devices * us, 2 * free),
        (left.reshape(halves * rows // 2, LANES), right),
        flops=2 * devices * us * LANES * qs * 2 * free,
    )
    parts = trade(partial_sums.reshape(devices, us, 2 * free))
    parts = parts.reshape(2, halves, us, 2 * free).astype(jnp.float32)
    join_scale = (2.0 * SHARED) ** (-0.5)
    return (jnp.sum(parts, axis=1) * join_scale).astype(jnp.bfloat16).reshape(2, us, 2, free)


def flip(value, *bits):
    mask = sum(2**bit for bit in bits)
    pairs = [(source, source ^ mask) for source in range(lax.axis_size("mode"))]
    return lax.ppermute(value, "mode", pairs)


def plane(value, sources):
    over_x, over_y = flip(value, 1), flip(value, 2)
    diagonal = flip(over_x[:1], 2), flip(over_y[1:], 1)
    turned = [tuple(source + more for source in sources) for more in ((1,), (2,), (1, 2))]
    return [
        (value, sources, (0, 1)),
        (over_x, turned[0], (0, 1)),
        (over_y, turned[1], (0, 1)),
        (diagonal[0], turned[2], (0,)),
        (diagonal[1], turned[2], (1,)),
    ]


def spread(gate_a, gate_b, packed):
    bits = lax.axis_size("mode").bit_length() - 1
    own = jnp.stack([gate_a, gate_b])[:, None]
    far = [()]
    for bit in range(3, bits):
        far += [source + (bit,) for source in far]
    came = [flip(own, *source) for source in far[1:]]
    sets = [(own, ((),)), (jnp.concatenate(came[:2], axis=1), tuple(far[1:3]))]
    if came[2:]:
        sets.append((jnp.concatenate(came[2:], axis=1), tuple(far[3:])))
    blocks = []
    for number, (value, sources) in enumerate(sets):
        if number:
            tied = (blocks[3][0], blocks[4][0]) if number == 1 else (*packed, blocks[6][0], blocks[7][0])
            value, *_ = lax.optimization_barrier((value, *tied))
        blocks += plane(value, sources)
    left, *_ = lax.optimization_barrier((packed[0], blocks[8][0], blocks[9][0], blocks[-2][0], blocks[-1][0]))
    left = trade(left)
    right, left = lax.optimization_barrier((packed[1], left))
    last = len(blocks) - 2
    near = []
    for number, (value, sources, gates) in enumerate(blocks):
        if number >= last:
            value, *_ = lax.optimization_barrier((value, *[earlier for earlier, _, _ in near[:last]]))
        near.append((flip(value, 0), tuple(source + (0,) for source in sources), gates))
    blocks += near
    plan = tuple((sources, gates) for _, sources, gates in blocks)
    return [value for value, _, _ in blocks], plan, left, trade(right)


def trade(value, groups=None):
    return lax.all_to_all(value, "mode", split_axis=0, concat_axis=0, axis_index_groups=groups, tiled=True)


def partner(value, axis, bit):
    mask = 2**bit
    pairs = [(source, source ^ mask) for source in range(lax.axis_size(axis))]
    return lax.ppermute(value, axis, pairs)


def product_four(states, layer_block):
    branches, parts, row_count, width = states.shape
    real_in = states[:, 0].reshape(branches * row_count, width)
    imag_in = states[:, 1].reshape(branches * row_count, width)
    real_part = jnp.dot(real_in, layer_block[0], preferred_element_type=jnp.float32) - jnp.dot(
        imag_in, layer_block[1], preferred_element_type=jnp.float32
    )
    imag_part = jnp.dot(real_in, layer_block[1], preferred_element_type=jnp.float32) + jnp.dot(
        imag_in, layer_block[0], preferred_element_type=jnp.float32
    )
    joined_parts = jnp.stack(
        [
            real_part.reshape(branches, row_count, width),
            imag_part.reshape(branches, row_count, width),
        ],
        axis=1,
    )
    return joined_parts.astype(jnp.bfloat16)


def complex_rows(left_real, left_imag, right_real, right_imag):
    real_part = jnp.dot(left_real, right_real, preferred_element_type=jnp.float32) - jnp.dot(
        left_imag, right_imag, preferred_element_type=jnp.float32
    )
    imag_part = jnp.dot(left_real, right_imag, preferred_element_type=jnp.float32) + jnp.dot(
        left_imag, right_real, preferred_element_type=jnp.float32
    )
    return jnp.stack([real_part, imag_part], axis=1)


def read_bit(device_index, bit_number):
    return device_index // 2**bit_number % 2


def trade_axes(buffer, axis_bits, trader, device_index):
    for position, bit_number in enumerate(axis_bits):
        own_bit = read_bit(device_index, bit_number)
        kept_half = lax.dynamic_index_in_dim(buffer, own_bit, position, keepdims=False)
        sent_half = lax.dynamic_index_in_dim(buffer, 1 - own_bit, position, keepdims=False)
        received = trader(sent_half, bit_number)
        first_half = jnp.where(own_bit == 0, kept_half, received)
        second_half = jnp.where(own_bit == 0, received, kept_half)
        buffer = jnp.stack([first_half, second_half], axis=position)
    return buffer


def general(branch_in, column_order, gate_a, gate_b):
    join_scale = (2.0 * SHARED) ** (-0.5)
    devices_mode = lax.axis_size("mode")
    whole_a, whole_b = (
        lax.all_gather(gate_a, "mode", axis=1, tiled=True),
        lax.all_gather(gate_b, "mode", axis=1, tiled=True),
    )
    states = jnp.take_along_axis(branch_in, column_order[:, None, None, :], axis=3)
    for layer_number in range(2 * CYCLES):
        if layer_number > 0:
            states = lax.all_to_all(states, "mode", split_axis=3, concat_axis=3, tiled=True)
        states = product_four(states, whole_a if layer_number % 2 == 0 else whole_b)
    local_cells = states.shape[2] * states.shape[3]
    local_rows = local_cells // SHARED
    shared_rows = SHARED // devices_mode
    join_width = local_cells // (shared_rows * KEPT)
    results = []
    for pair_number in range(2):
        left_part = states[2 * pair_number].reshape(2, local_rows, SHARED)
        right_part = states[2 * pair_number + 1].reshape(2, shared_rows, KEPT, join_width)
        device_index = lax.axis_index("mode")
        total_bits = devices_mode.bit_length() - 1
        group_bits = total_bits - 4
        batch_bits = KEPT.bit_length() - 1
        groups = devices_mode // (4 * KEPT)
        span = 2 * shared_rows
        outer = SHARED // (span * groups)
        half_join = join_width // 2

        def left_trader(piece, bit_number):
            return partner(piece, "mode", bit_number)

        def right_trader(piece, bit_number):
            return partner(piece, "mode", bit_number)

        left_buffer = left_part.reshape(2, local_rows, outer, groups, span).transpose(3, 0, 1, 2, 4)
        left_buffer = left_buffer.reshape((2,) * group_bits + (1, 2, local_rows, outer, span))
        left_buffer = jnp.broadcast_to(
            left_buffer, (2,) * group_bits + (2, 2, local_rows, outer, span)
        )
        left_bits = [group_bits - position for position in range(group_bits)] + [0]
        left_buffer = trade_axes(left_buffer, left_bits, left_trader, device_index)
        left_block = left_buffer.reshape(devices_mode // (2 * KEPT), 2, local_rows, outer * span)
        left_block = left_block.transpose(1, 0, 2, 3).reshape(2, half_join, SHARED // groups)
        right_buffer = right_part.reshape(2, shared_rows, KEPT, 2, half_join).transpose(
            2, 3, 0, 1, 4
        )
        right_buffer = right_buffer.reshape((2,) * batch_bits + (1, 2, 2, shared_rows, half_join))
        right_buffer = jnp.broadcast_to(
            right_buffer, (2,) * batch_bits + (2, 2, 2, shared_rows, half_join)
        )
        right_bits = [total_bits - 1 - position for position in range(batch_bits)] + [
            total_bits - batch_bits - 1,
            0,
        ]
        right_buffer = trade_axes(right_buffer, right_bits, right_trader, device_index)
        right_block = right_buffer.reshape(2 * KEPT, 2, 2, shared_rows, half_join)
        right_block = right_block.transpose(2, 0, 1, 3, 4).reshape(2, SHARED // groups, half_join)
        running = complex_rows(left_block[0], left_block[1], right_block[0], right_block[1])
        for position in range(group_bits):
            bit_number = group_bits - position
            own_bit = read_bit(device_index, bit_number)
            row_count = running.shape[0]
            halves = running.reshape(2, row_count // 2, 2, half_join)
            kept_half = lax.dynamic_index_in_dim(halves, own_bit, 0, keepdims=False)
            sent_half = lax.dynamic_index_in_dim(halves, 1 - own_bit, 0, keepdims=False)
            running = kept_half + partner(
                sent_half.astype(jnp.bfloat16), "mode", bit_number
            ).astype(sent_half.dtype)
        rounded = (running * join_scale).astype(jnp.bfloat16)
        own_bit = read_bit(device_index, 0)
        halves = rounded.reshape(2, local_rows, 2, half_join)
        kept_half = lax.dynamic_index_in_dim(halves, own_bit, 0, keepdims=False)
        sent_half = lax.dynamic_index_in_dim(halves, 1 - own_bit, 0, keepdims=False)
        received = partner(sent_half, "mode", 0)
        first_half = jnp.where(own_bit == 0, kept_half, received)
        second_half = jnp.where(own_bit == 0, received, kept_half)
        finished = jnp.concatenate([first_half, second_half], axis=2)
        results.append(finished)
    return jnp.stack(results)


def local(branch_in, column_order, gate_a, gate_b):
    branches, _, rows_each, width = branch_in.shape
    if branches == 4 and tiles_fit(lax.axis_size("mode"), rows_each, width):
        return fast(branch_in, column_order, gate_a, gate_b)
    return general(branch_in, column_order, gate_a, gate_b)


def solution(mesh):
    in_specs = (
        P(None, None, ("cuts", "mode"), None),
        P(),
        P(None, "mode", None),
        P(None, "mode", None),
    )
    out_specs = P(None, ("cuts", "mode"), None, None)
    return jax.shard_map(local, mesh=mesh, in_specs=in_specs, out_specs=out_specs, check_vma=False)
```
